128 devices in a mesh: dp: 4 (over y), mp: 32 (over x, z, core).
Axes of the slice: x: 4, y: 4, z: 4, core: 2. Of those that a mesh axis runs over, the one named last changes fastest.
Arguments:
- events: bfloat16 [128, 1024, 512], P(('dp', 'mp')), may hold values from -6 to 6
- lengths: int32 [128], P(('dp', 'mp')), may hold values from 1 to 1024, 81920 in all
- target_ids: int32 [128, 1024], P(('dp', 'mp')), may hold values from 0 to 524287, as said below
- neg_ids: int32 [1024], replicated, may hold values from 0 to 524287, as said below
- neg_counts: int32 [1024], replicated, may hold values from 1 to 64
- item_table: bfloat16 [524288, 512], P(('dp', 'mp')), may hold values from -2 to 2
- w_uvqk: bfloat16 [512, 2048], P('mp'), may hold values from -0.25 to 0.25
- w_out: bfloat16 [512, 512], P('mp'), may hold values from -0.25 to 0.25
Outputs:
- token_loss: float32 [128, 1024], P(('dp', 'mp'))
- table_grad: bfloat16 [524288, 512], P(('dp', 'mp'))
The draws below stay inside these ranges and needn't reach their ends.
Inputs may be any that keep to these rules, and one draw needn't show every extreme that they name: `neg_ids`: the negatives are distinct. No device's rows hold more than 16 of them, one device's rows hold exactly 16, and the other devices' shares differ by one at most. `target_ids`: in each sequence no device's rows hold more than 16 of the targets; one device's rows, the same for every sequence, hold exactly 16 in each, and the other devices' shares in a sequence differ by one at most.
All inputs are finite; a program needn't handle non-finite values. No bound on the sum of `lengths` on one device may be relied on, other than what follows from the above.
Results may differ from the reference program's by a relative error of at most 0.0075.
Values may be sent and summed in bfloat16 or wider, within the bound.
No kernel may reach another device: no remote copies, remote signals or barrier semaphores. Data moves between devices by JAX's collectives and lax.ppermute only.
A program may use at most 128 MiB of HBM per device.

```python
import math
import jax
import jax.numpy as jnp
import numpy as np
from jax import lax

D = 512
H = 4
DH = 128
LEN = 1024
NEG = 1024
ITEMS_DEV = 4096
SEQS = 128
ITEMS = 524288
NCAP = 16
PCAP = 16


def negative_ids(key):
    inner = jax.random.fold_in(key, 60)
    key_owner, key_row, key_order = jax.random.split(inner, 3)
    owners = ITEMS // ITEMS_DEV
    slot_index = jnp.arange(NEG, dtype=jnp.int32)
    base_owner = jnp.where(slot_index < NCAP, 0, 1 + (slot_index - NCAP) % (owners - 1))
    occurrence = jnp.where(slot_index < NCAP, slot_index, (slot_index - NCAP) // (owners - 1))
    owner_order = jax.random.permutation(key_owner, owners)
    stride = ITEMS_DEV // NCAP
    local_row = occurrence * stride + jax.random.randint(key_row, (NEG,), 0, stride)
    chosen_ids = owner_order[base_owner] * ITEMS_DEV + local_row
    return chosen_ids[jax.random.permutation(key_order, NEG)]


def draw_neg_ids(key, part):
    chosen_ids = negative_ids(key)
    return chosen_ids


def draw_target_ids(key, part):
    key = jax.random.fold_in(key, 7)
    key_hot, key_rest = jax.random.split(key)
    owners = ITEMS // ITEMS_DEV
    hot_owner = jax.random.randint(key_hot, (), 0, owners)
    slot_index = jnp.arange(LEN, dtype=jnp.int32)
    base_owner = jnp.where(slot_index < PCAP, 0, 1 + (slot_index - PCAP) % (owners - 1))

    def one_sequence(seq_key):
        key_perm, key_row, key_order = jax.random.split(seq_key, 3)
        others = (hot_owner + 1 + jax.random.permutation(key_perm, owners - 1)) % owners
        owner_of = jnp.where(base_owner == 0, hot_owner, others[jnp.maximum(base_owner - 1, 0)])
        local_row = jax.random.randint(key_row, (LEN,), 0, ITEMS_DEV)
        chosen = owner_of * ITEMS_DEV + local_row
        return chosen[jax.random.permutation(key_order, LEN)]
    return jax.vmap(one_sequence)(jax.random.split(key_rest, SEQS))


def draw_events(key, part):
    key = jax.random.fold_in(key, 3)
    return jnp.clip(0.25 * jax.random.normal(key, (SEQS, LEN, D), jnp.float32), -1.0, 1.0).astype(jnp.bfloat16)


def draw_item_table(key, part):
    key = jax.random.fold_in(key, 5)
    return jnp.clip(0.25 * jax.random.normal(key, (ITEMS, D), jnp.float32), -1.0, 1.0).astype(jnp.bfloat16)


def plant(result, key, smallest, largest):
    index_at = [jax.random.randint(jax.random.fold_in(key, axis), (), 0, length) for axis, length in enumerate(result.shape)]
    main_axis = result.shape.index(max(result.shape))
    next_to = index_at[:main_axis] + [(index_at[main_axis] + 1) % result.shape[main_axis]] + index_at[main_axis + 1:]
    return result.at[tuple(index_at)].set(smallest).at[tuple(next_to)].set(largest)


def level_of(rng, extent, shards, least, largest):
    def one(dim, blocks):
        heights = jax.random.uniform(jax.random.fold_in(jax.random.fold_in(rng, 6), dim), (blocks,), jnp.float32, least / len(shards), largest / len(shards))
        return jnp.repeat(jnp.exp(heights), extent[dim] // blocks).reshape((-1,) + (1,) * (len(extent) - dim - 1))

    loudness = one(*shards[0])
    for cut in shards[1:]:
        loudness = loudness * one(*cut)
    return loudness


def length_profile(number_of, total, limit, skew):
    portions = [(1 << 20) // math.isqrt(standing ** skew) + 1 for standing in range(2, number_of + 1)]
    rest, holding = total - limit - (number_of - 1), [1] * (number_of - 1)
    while rest > 0:
        candidates = [i for i in range(number_of - 1) if holding[i] < limit]
        mass, remaining = sum([portions[i] for i in candidates]), rest
        for i in candidates:
            more = min(limit - holding[i], max(1, remaining * portions[i] // mass), rest)
            holding[i] = holding[i] + more
            rest = rest - more
    return np.array([limit] + holding)


def uneven(rng, count, total, bound, slope):
    if count == 2:
        one = jax.random.randint(rng, (), max(1, total - bound), min(bound, total - 1) + 1)
        return jnp.stack([one, total - one])
    sizes = jnp.asarray(length_profile(count, total, bound, slope), jnp.int32)
    couples = (count - 1) // 2
    source_of, taker = sizes[1:1 + 2 * couples:2], sizes[2:2 + 2 * couples:2]
    slack = jnp.minimum(source_of - 1, bound - taker)
    passed = jax.random.randint(jax.random.fold_in(rng, 1), (couples,), 0, 1 << 20) % (slack + 1)
    sizes = sizes.at[1:1 + 2 * couples:2].set(source_of - passed).at[2:2 + 2 * couples:2].set(taker + passed)
    return sizes[jax.random.permutation(jax.random.fold_in(rng, 2), count)]


def centred(rng, dims, width, bound, pieces=(), kind=jnp.bfloat16):
    level = level_of(rng, dims, pieces, -0.22, 0.18) if pieces else 1.0
    values = jax.random.normal(rng, dims, jnp.float32) * width * level
    return jnp.minimum(jnp.maximum(values, -bound), bound).astype(kind)


def setup_inputs(seed: int = 0) -> dict:
    key_list = jax.random.split(jax.random.key(seed), 9)
    events = draw_events(jax.random.fold_in(key_list[8], 71), 0)
    lengths = uneven(key_list[1], SEQS, SEQS * LEN * 5 // 8, LEN, 1).astype(jnp.int32)
    target_ids = draw_target_ids(jax.random.fold_in(key_list[8], 71), 0)
    neg_ids = draw_neg_ids(jax.random.fold_in(key_list[8], 71), 0)
    neg_counts = plant(jax.random.randint(key_list[4], (NEG,), 1, 65), jax.random.fold_in(key_list[4], 1), 1, 64).astype(jnp.int32)
    item_table = draw_item_table(jax.random.fold_in(key_list[8], 71), 0)
    w_uvqk = centred(key_list[6], (D, 4 * D), D ** -0.5, 0.25, ((0, 32),))
    w_out = centred(key_list[7], (D, D), D ** -0.5, 0.25, ((0, 32),))
    return {"events": events, "lengths": lengths, "target_ids": target_ids, "neg_ids": neg_ids, "neg_counts": neg_counts, "item_table": item_table, "w_uvqk": w_uvqk, "w_out": w_out}


EPSILON = 1e-05

def layer_norm(values):
    center = values - lax.optimization_barrier(jnp.mean(values, axis=-1, keepdims=True))
    spread = lax.optimization_barrier(jnp.mean(center * center, axis=-1, keepdims=True))
    return center * lax.rsqrt(spread + EPSILON)

def hstu_layer(events_seq, length, w_uvqk, w_out):
    inputs = events_seq.astype(jnp.float32)
    normed = layer_norm(inputs).astype(jnp.bfloat16)
    projected = jnp.dot(normed, w_uvqk, preferred_element_type=jnp.float32)
    activated = jax.nn.silu(projected).astype(jnp.bfloat16)
    gate_units = activated[:, :D]
    value_heads = activated[:, D:2 * D].reshape(LEN, H, DH)
    query_heads = activated[:, 2 * D:3 * D].reshape(LEN, H, DH)
    key_heads = activated[:, 3 * D:].reshape(LEN, H, DH)
    scores = jnp.einsum('qhd,khd->hqk', query_heads.astype(jnp.float32), key_heads.astype(jnp.float32)) / math.sqrt(DH)
    row_ids = jnp.arange(LEN, dtype=jnp.int32)[:, None]
    col_ids = jnp.arange(LEN, dtype=jnp.int32)[None, :]
    allowed = (col_ids <= row_ids) & (col_ids < length)
    attention_weights = jnp.where(allowed[None], jax.nn.silu(scores), 0.0).astype(jnp.bfloat16)
    attended = jnp.einsum('hqk,khd->qhd', attention_weights.astype(jnp.float32), value_heads.astype(jnp.float32)).reshape(LEN, D)
    gated_rows = (layer_norm(attended) * gate_units.astype(jnp.float32)).astype(jnp.bfloat16)
    output = jnp.dot(gated_rows, w_out, preferred_element_type=jnp.float32)
    return (inputs + output).astype(jnp.bfloat16)

def loss_terms(hidden, events_seq, targets, length, neg_rows, neg_ids, log_counts):
    position = jnp.arange(LEN, dtype=jnp.int32)
    in_range = position < length - 1
    following = jnp.concatenate([events_seq[1:], jnp.zeros((1, D), jnp.bfloat16)], axis=0)
    positive = lax.optimization_barrier(jnp.sum(hidden.astype(jnp.float32) * following.astype(jnp.float32), axis=1))
    negative = jnp.dot(hidden, neg_rows.T, preferred_element_type=jnp.float32) - log_counts[None, :]
    kept_mask = targets[:, None] != neg_ids[None, :]
    row_top = jnp.maximum(positive, lax.optimization_barrier(jnp.max(jnp.where(kept_mask, negative, positive[:, None]), axis=1)))
    row_total = jnp.exp(positive - row_top) + lax.optimization_barrier(jnp.sum(jnp.where(kept_mask, jnp.exp(negative - row_top[:, None]), 0.0), axis=1))
    log_total = row_top + jnp.log(row_total)
    token_cost = jnp.where(in_range, log_total - positive, 0.0)
    neg_probs = jnp.where(in_range[:, None] & kept_mask, jnp.exp(negative - log_total[:, None]), 0.0).astype(jnp.bfloat16)
    neg_term = jnp.dot(neg_probs.T, hidden, preferred_element_type=jnp.float32)
    pos_grad = jnp.where(in_range[:, None], (jnp.exp(positive - log_total) - 1.0)[:, None] * hidden.astype(jnp.float32), 0.0).astype(jnp.bfloat16)
    return (token_cost, neg_term, pos_grad)

def reference(events, lengths, target_ids, neg_ids, neg_counts, item_table, w_uvqk, w_out):
    neg_rows = item_table[neg_ids]
    log_counts = jnp.log(neg_counts.astype(jnp.float32))

    def per_sequence(neg_sum, sequence_in):
        events_seq, length, targets = sequence_in
        hidden = hstu_layer(events_seq, length, w_uvqk, w_out)
        token_cost, neg_term, pos_grad = loss_terms(hidden, events_seq, targets, length, neg_rows, neg_ids, log_counts)
        return (neg_sum + neg_term, (token_cost, pos_grad))
    neg_total, (token_loss, pos_grads) = lax.scan(per_sequence, jnp.zeros((NEG, D), jnp.float32), (events, lengths, target_ids))
    table_grad = jnp.zeros((ITEMS, D), jnp.float32).at[neg_ids].add(neg_total)
    table_grad = table_grad.at[target_ids.reshape(-1)].add(pos_grads.reshape(-1, D).astype(jnp.float32))
    return (token_loss, table_grad.astype(jnp.bfloat16))
```

```python
import math

import jax
import jax.numpy as jnp
from jax import lax
from jax.sharding import Mesh, PartitionSpec as P

H = 4
EPSILON = 1e-05
ALL = ("y", "x", "z", "c")
MP = ("x", "z", "c")
BF = jnp.bfloat16
F32 = jnp.float32
DEVS = 128
SLOTS = 16
ITEMS_DEV = 4096


def layer_norm(values):
    center = values - jnp.mean(values, axis=-1, keepdims=True)
    spread = jnp.mean(center * center, axis=-1, keepdims=True)
    return center * lax.rsqrt(spread + EPSILON)


def silu(v):
    h = 0.5 * v
    return h + h * jnp.tanh(h)


def ranks(owner):
    n = owner.shape[0]
    hot = (lax.broadcasted_iota(jnp.int32, (DEVS, n), 0) == owner[None, :]).astype(BF)
    tri = (
        lax.broadcasted_iota(jnp.int32, (n, n), 0) < lax.broadcasted_iota(jnp.int32, (n, n), 1)
    ).astype(BF)
    before = jnp.dot(hot, tri, preferred_element_type=F32)
    return jnp.sum(before * hot.astype(F32), axis=0).astype(jnp.int32)


def a2a(v):
    return lax.all_to_all(v, ALL, split_axis=0, concat_axis=0, tiled=True)


def per_device(events, lengths, target_ids, neg_ids, neg_counts, item_table, w_uvqk, w_out):
    seq_len, width = events.shape[1], events.shape[2]
    head_dim = width // H
    me = lax.axis_index(ALL)
    length = lengths[0]
    targets = target_ids[0]

    w_all = jnp.concatenate([w_uvqk, w_out], axis=1)
    w_full = lax.all_to_all(
        jnp.broadcast_to(w_all[None], (32,) + w_all.shape), MP, split_axis=0, concat_axis=0, tiled=True
    ).reshape(width, -1)

    neg_owner = neg_ids // ITEMS_DEV
    neg_slot = neg_owner * SLOTS + ranks(neg_owner)
    slot_ids = jnp.arange(DEVS * SLOTS, dtype=jnp.int32)
    mine = lax.broadcasted_iota(jnp.int32, (SLOTS, 1), 0) + me * SLOTS == neg_slot[None, :]
    neg_local = jnp.sum(jnp.where(mine, (neg_ids % ITEMS_DEV)[None, :], 0), axis=1)
    neg_used = jnp.any(mine, axis=1)
    packed = item_table[neg_local]
    gathered = a2a(jnp.broadcast_to(packed[None], (DEVS,) + packed.shape)).reshape(-1, width)
    neg_hot = (slot_ids[:, None] == neg_slot[None, :]).astype(BF)
    neg_rows = lax.dot_general(
        neg_hot, gathered, (((0,), (0,)), ((), ())), preferred_element_type=F32
    ).astype(BF)

    target_owner = targets // ITEMS_DEV
    target_slot = target_owner * SLOTS + ranks(target_owner)
    target_match = slot_ids[:, None] == target_slot[None, :]
    target_hot = target_match.astype(BF)
    send_local = jnp.sum(
        jnp.where(target_match, (targets % ITEMS_DEV)[None, :] + 1, 0), axis=1
    ) - 1
    recv_local = a2a(send_local.reshape(DEVS, 1, SLOTS)).reshape(-1)

    inputs = events[0].astype(F32)
    normed = layer_norm(inputs).astype(BF)
    activated = silu(jnp.dot(normed, w_full[:, : 4 * width], preferred_element_type=F32)).astype(BF)
    gate_units = activated[:, :width]
    values, queries, keys = (
        activated[:, (i + 1) * width : (i + 2) * width].reshape(seq_len, H, head_dim) for i in range(3)
    )
    outputs = []
    block = 512
    for start in range(0, seq_len, block):
        stop = start + block
        scores = jnp.einsum(
            "qhd,khd->hqk", queries[start:stop], keys[:stop], preferred_element_type=F32
        ) / math.sqrt(head_dim)
        row_ids = jnp.arange(start, stop, dtype=jnp.int32)[:, None]
        col_ids = jnp.arange(stop, dtype=jnp.int32)[None, :]
        allowed = (col_ids <= row_ids) & (col_ids < length)
        weights = jnp.where(allowed[None], silu(scores), 0.0).astype(BF)
        outputs.append(
            jnp.einsum("hqk,khd->qhd", weights, values[:stop], preferred_element_type=F32)
        )
    attended = jnp.concatenate(outputs, axis=0).reshape(seq_len, width)
    gated = (layer_norm(attended) * gate_units.astype(F32)).astype(BF)
    hidden = (inputs + jnp.dot(gated, w_full[:, 4 * width :], preferred_element_type=F32)).astype(BF)

    send_rows = jnp.dot(target_hot, hidden, preferred_element_type=F32).astype(BF)
    recv_rows = a2a(send_rows.reshape(DEVS, SLOTS, width))

    log_counts = jnp.log(neg_counts.astype(F32))
    in_range = jnp.arange(seq_len, dtype=jnp.int32) < length - 1
    following = jnp.concatenate([events[0, 1:], jnp.zeros((1, width), BF)], axis=0)
    positive = jnp.sum(hidden.astype(F32) * following.astype(F32), axis=1)
    negative = (
        lax.dot_general(neg_rows, hidden, (((1,), (1,)), ((), ())), preferred_element_type=F32)
        - log_counts[:, None]
    )
    kept = neg_ids[:, None] != targets[None, :]
    top = jnp.maximum(
        positive, jnp.max(jnp.where(kept, negative, positive[None, :]), axis=0)
    )
    total = jnp.exp(positive - top) + jnp.sum(
        jnp.where(kept, jnp.exp(negative - top[None, :]), 0.0), axis=0
    )
    log_total = top + jnp.log(total)
    token_loss = jnp.where(in_range, log_total - positive, 0.0)
    probs = jnp.where(
        in_range[None, :] & kept, jnp.exp(negative - log_total[None, :]), 0.0
    ).astype(BF)
    neg_term = jnp.dot(probs, hidden, preferred_element_type=F32).astype(BF)
    coef = jnp.where(in_range, jnp.exp(positive - log_total) - 1.0, 0.0)
    send_coef = jnp.sum(jnp.where(target_match, coef[None, :], 0.0), axis=1)
    recv_coef = a2a(send_coef.reshape(DEVS, 1, SLOTS)).reshape(-1)

    send_neg = jnp.dot(neg_hot, neg_term, preferred_element_type=F32).astype(BF)
    summed = jnp.sum(a2a(send_neg.reshape(DEVS, SLOTS, width)).astype(F32), axis=0)

    pos_rows = (recv_rows.reshape(-1, width).astype(F32) * recv_coef[:, None]).astype(BF)
    high = summed.astype(BF)
    low = (summed - high.astype(F32)).astype(BF)
    rows = jnp.concatenate([pos_rows, high, low], axis=0)
    neg_at = jnp.where(neg_used, neg_local, -1)
    row_at = jnp.concatenate([recv_local, neg_at, neg_at])
    place = (
        lax.broadcasted_iota(jnp.int32, (ITEMS_DEV, 1), 0) == row_at[None, :]
    ).astype(BF)
    grad = jnp.dot(place, rows, preferred_element_type=F32).astype(BF)
    return token_loss[None], grad


def solution(mesh):
    fine = Mesh(mesh.devices.reshape(4, 4, 4, 2), ALL)
    in_specs = (P(ALL), P(ALL), P(ALL), P(), P(), P(ALL), P(MP), P(MP))
    return jax.shard_map(
        per_device, mesh=fine, in_specs=in_specs, out_specs=(P(ALL), P(ALL)), check_vma=False
    )
```

```python
import math

import jax
import jax.numpy as jnp
from jax import lax
from jax.experimental import pallas as pl
from jax.experimental.pallas import tpu as pltpu
from jax.sharding import Mesh, PartitionSpec as P

H = 4
EPSILON = 1e-05
ALL = ("y", "x", "z", "c")
CHIPS = ("y", "x", "z")
MP = ("x", "z", "c")
BF = jnp.bfloat16
F32 = jnp.float32
I32 = jnp.int32
DEVS = 128
NCHIPS = 64
CSLOTS = 24
SLOTS = NCHIPS * CSLOTS
ITEMS_DEV = 4096
B = 256
VMEM = pl.BlockSpec(memory_space=pltpu.VMEM)
SMEM = pl.BlockSpec(memory_space=pltpu.SMEM)
NT = (((1,), (1,)), ((), ()))
NEG_INF = float("-inf")
POS_INF = float("inf")
SWAP = ((0, 1), (1, 0))


def dot(a, b):
    return jnp.dot(a, b, preferred_element_type=F32)


def dot_nt(a, b):
    return lax.dot_general(a, b, NT, preferred_element_type=F32)


def iota(shape, dim):
    return lax.broadcasted_iota(I32, shape, dim)


def layer_norm(values):
    center = values - jnp.mean(values, axis=-1, keepdims=True)
    spread = jnp.mean(center * center, axis=-1, keepdims=True)
    return center * lax.rsqrt(spread + EPSILON)


def call(body, out_shape, in_specs, scratch=(), flops=0, nbytes=0):
    return pl.pallas_call(
        body,
        out_shape=out_shape,
        in_specs=in_specs,
        out_specs=jax.tree.map(lambda _: VMEM, out_shape),
        scratch_shapes=list(scratch),
        cost_estimate=pl.CostEstimate(flops=flops, bytes_accessed=nbytes, transcendentals=0),
        compiler_params=pltpu.CompilerParams(vmem_limit_bytes=56 << 20),
    )


def norm_kernel(events_ref, out_ref):
    @pl.loop(0, 4)
    def _(i):
        rows = pl.ds(pl.multiple_of(i * B, B), B)
        out_ref[rows, :] = layer_norm(events_ref[rows, :].astype(F32)).astype(BF)


def silu_of_half(h):
    return h + h * jnp.tanh(h)


def layer_kernel(
    info_ref, normed_ref, own_ref, other_ref, events_ref, follow_ref, hot_ref,
    hidden_ref, positive_ref, send_ref, w_ref, act_ref, att_ref,
):
    core, length = info_ref[0], info_ref[1]
    for b in range(16):
        block = slice(b * 16, (b + 1) * 16)
        w_ref[pl.ds(pl.multiple_of(b * 32 + core * 16, 16), 16), :] = own_ref[block, :]
        w_ref[pl.ds(pl.multiple_of(b * 32 + (1 - core) * 16, 16), 16), :] = other_ref[block, :]

    @pl.loop(0, 4)
    def _(i):
        rows = pl.ds(pl.multiple_of(i * B, B), B)
        a = normed_ref[rows, :]
        live = iota((B, 512), 0) + i * B < length
        for n in range(4):
            cols = slice(n * 512, (n + 1) * 512)
            v = silu_of_half(0.5 * dot(a, w_ref[:, cols]))
            if n == 1:
                v = jnp.where(live, v, 0.0)
            act_ref[rows, cols] = v.astype(BF)

    causal = iota((B, B), 1) <= iota((B, B), 0)
    eye = iota((B, B), 1) == iota((B, B), 0)
    scale = 0.5 / math.sqrt(128)
    for i in range(4):
        rows = slice(i * B, (i + 1) * B)
        for h in range(H):
            q = act_ref[rows, 1024 + h * 128 : 1024 + (h + 1) * 128]
            total = None
            for j in range(i + 1):
                keys = slice(j * B, (j + 1) * B)
                s = dot_nt(q, act_ref[keys, 1536 + h * 128 : 1536 + (h + 1) * 128])
                w = silu_of_half(s * scale)
                if j == i:
                    w = jnp.where(causal, w, 0.0)
                t = dot(w.astype(BF), act_ref[keys, 512 + h * 128 : 512 + (h + 1) * 128])
                total = t if total is None else total + t
            att_ref[:, h * 128 : (h + 1) * 128] = total
        gated = (layer_norm(att_ref[...]) * act_ref[rows, :512].astype(F32)).astype(BF)
        hidden = (events_ref[rows, :].astype(F32) + dot(gated, w_ref[:, 2048:])).astype(BF)
        hidden_ref[rows, :] = hidden
        pos = jnp.sum(hidden.astype(F32) * follow_ref[rows, :].astype(F32), axis=1, keepdims=True)
        positive_ref[:, rows] = jnp.sum(jnp.where(eye, pos, 0.0), axis=0, keepdims=True)

    @pl.loop(0, SLOTS // B)
    def _(m):
        rows = pl.ds(pl.multiple_of(m * B, B), B)
        send_ref[rows, :] = dot(hot_ref[rows, :], hidden_ref[...]).astype(BF)


def loss_kernel(
    info_ref, hidden_ref, own_ref, other_ref, ids_ref, logc_ref, positive_ref, targets_ref, hot_ref,
    index_ref, loss_ref, term_own_ref, term_other_ref, meta_ref, l_ref, probs_ref, coef_ref,
):
    core, length = info_ref[0], info_ref[1]
    own_cols = pl.ds(pl.multiple_of(core * B, B), B)
    other_cols = pl.ds(pl.multiple_of((1 - core) * B, B), B)
    chunks = [slice(m * B, (m + 1) * B) for m in range(SLOTS // B)]

    @pl.loop(0, 4)
    def _(t):
        at = pl.ds(pl.multiple_of(t * B, B), B)
        h_own = hidden_ref[at, own_cols]
        h_other = hidden_ref[at, other_cols]
        pos = positive_ref[:, at]
        target = targets_ref[:, at]
        top = pos
        for m in chunks:
            value = dot_nt(own_ref[m, :], h_own) + dot_nt(other_ref[m, :], h_other) - logc_ref[m, :]
            value = jnp.where(ids_ref[m, :] != target, value, NEG_INF)
            l_ref[m, :] = value
            top = jnp.maximum(top, jnp.max(value, axis=0, keepdims=True))
        total = jnp.exp(pos - top)
        for m in chunks:
            total = total + jnp.sum(jnp.exp(l_ref[m, :] - top), axis=0, keepdims=True)
        log_total = top + jnp.log(total)
        in_range = iota((1, B), 1) + t * B < length - 1
        loss_ref[:, at] = jnp.where(in_range, log_total - pos, 0.0)
        coef_ref[:, at] = jnp.where(in_range, jnp.exp(pos - log_total) - 1.0, 0.0)
        shift = jnp.where(in_range, log_total, POS_INF)
        for m in chunks:
            probs_ref[m, at] = jnp.exp(l_ref[m, :] - shift).astype(BF)

    coef = coef_ref[...]
    high = coef.astype(BF).astype(F32)
    middle = (coef - high).astype(BF).astype(F32)
    low = coef - high - middle
    pieces = jnp.concatenate(
        [high, middle, low, index_ref[...], jnp.zeros((11, 1024), F32)], axis=0
    ).astype(BF)
    for m in chunks:
        meta_ref[:, m] = dot_nt(pieces, hot_ref[m, :]).astype(BF)
        term_other_ref[m, :] = dot(probs_ref[m, :], hidden_ref[:, other_cols]).astype(BF)
        term_own_ref[m, :] = dot(probs_ref[m, :], hidden_ref[:, own_cols])


def place_kernel(index_ref, rows_ref, neg_index_ref, neg_ref, out_ref):
    tile = out_ref.shape[0]
    base = pl.program_id(0) * tile

    def onehot(index):
        return (iota((tile, index.shape[1]), 0) + base == index).astype(F32).astype(BF)

    out_ref[...] = (
        dot(onehot(index_ref[...]), rows_ref[...]) + dot(onehot(neg_index_ref[...]), neg_ref[...])
    ).astype(BF)


def chip_slots(ids):
    n = ids.shape[0]
    owner = ids // ITEMS_DEV
    hot = (iota((DEVS, n), 0) == owner[None, :]).astype(BF)
    tri = (iota((n, n), 0) < iota((n, n), 1)).astype(BF)
    rank = jnp.sum(dot(hot, tri) * hot.astype(F32), axis=0).astype(I32)
    within = jnp.where(rank < 8, (owner % 2) * 8 + rank, 8 + rank)
    return (owner // 2) * CSLOTS + within


def swap(v):
    return lax.ppermute(v, "c", SWAP)


def chips_a2a(v):
    return lax.all_to_all(v, CHIPS, split_axis=0, concat_axis=0, tiled=True)


def per_device(events, lengths, target_ids, neg_ids, neg_counts, item_table, w_uvqk, w_out):
    width = 512
    core = lax.axis_index("c")
    chip = lax.axis_index(CHIPS)
    info = jnp.stack([core, lengths[0]]).astype(I32)
    targets = target_ids[0]
    ev = events[0]

    w_mine = jnp.concatenate([w_uvqk, w_out], axis=1)
    w_own = lax.all_to_all(
        jnp.broadcast_to(w_mine[None], (16,) + w_mine.shape), ("x", "z"), split_axis=0, concat_axis=0, tiled=True
    ).reshape(256, 2560)
    w_other = swap(w_own)

    normed = call(norm_kernel, jax.ShapeDtypeStruct((1024, 512), BF), [VMEM], nbytes=2 << 20, flops=1 << 20)(ev)

    neg_slot = chip_slots(neg_ids)
    slot_ids = jnp.arange(SLOTS, dtype=I32)
    here = iota((CSLOTS, 1), 0) + chip * CSLOTS == neg_slot[None, :]
    mine = here & ((neg_ids // ITEMS_DEV) % 2 == core)[None, :]
    neg_local = jnp.sum(jnp.where(mine, (neg_ids % ITEMS_DEV)[None, :] + 1, 0), axis=1) - 1
    packed = jnp.where((neg_local >= 0)[:, None], item_table[jnp.maximum(neg_local, 0)], 0)
    packed_own = lax.dynamic_slice(packed, (0, core * B), (CSLOTS, B))
    packed_other = lax.dynamic_slice(packed, (0, (1 - core) * B), (CSLOTS, B))
    packed_own = packed_own + swap(packed_other)
    neg_own = chips_a2a(jnp.broadcast_to(packed_own[None], (NCHIPS, CSLOTS, B))).reshape(SLOTS, B)
    neg_other = swap(neg_own)
    match = slot_ids[:, None] == neg_slot[None, :]
    slot_neg_id = jnp.sum(jnp.where(match, neg_ids[None, :] + 1, 0), axis=1) - 1
    slot_count = jnp.sum(jnp.where(match, neg_counts[None, :], 0), axis=1)
    slot_logc = jnp.where(slot_count > 0, jnp.log(slot_count.astype(F32)), POS_INF)

    target_slot = chip_slots(targets)
    hot = (slot_ids[:, None] == target_slot[None, :]).astype(BF)
    chip_row = targets % (2 * ITEMS_DEV) + 1
    index = jnp.stack([chip_row // 64, chip_row % 64]).astype(F32)

    follow = jnp.concatenate([ev[1:], jnp.zeros((1, width), BF)], axis=0)
    hidden, positive, send_rows = call(
        layer_kernel,
        (
            jax.ShapeDtypeStruct((1024, width), BF),
            jax.ShapeDtypeStruct((1, 1024), F32),
            jax.ShapeDtypeStruct((SLOTS, width), BF),
        ),
        [SMEM] + [VMEM] * 6,
        scratch=[
            pltpu.VMEM((512, 2560), BF),
            pltpu.VMEM((1024, 2048), BF),
            pltpu.VMEM((B, width), F32),
        ],
        flops=9 << 30,
        nbytes=12 << 20,
    )(info, normed, w_own, w_other, ev, follow, hot)

    recv_rows = chips_a2a(send_rows.reshape(NCHIPS, CSLOTS, width))

    loss, term_own, term_other, meta = call(
        loss_kernel,
        (
            jax.ShapeDtypeStruct((1, 1024), F32),
            jax.ShapeDtypeStruct((SLOTS, B), F32),
            jax.ShapeDtypeStruct((SLOTS, B), BF),
            jax.ShapeDtypeStruct((16, SLOTS), BF),
        ),
        [SMEM] + [VMEM] * 9,
        scratch=[
            pltpu.VMEM((SLOTS, B), F32),
            pltpu.VMEM((SLOTS, 1024), BF),
            pltpu.VMEM((1, 1024), F32),
        ],
        flops=7 << 30,
        nbytes=12 << 20,
    )(
        info, hidden, neg_own, neg_other, slot_neg_id[:, None], slot_logc[:, None], positive,
        target_ids, hot, index,
    )
    term = (term_own + swap(term_other).astype(F32)).astype(BF).reshape(NCHIPS, CSLOTS, B)
    meta = meta[:8].reshape(8, NCHIPS, CSLOTS).transpose(1, 0, 2)
    meta = jnp.pad(meta, ((0, 0), (0, 0), (0, B - CSLOTS)))
    got = chips_a2a(jnp.concatenate([term, meta], axis=1))
    summed = jnp.sum(got[:, :CSLOTS].astype(F32), axis=0)
    got_meta = got[:, CSLOTS:, :CSLOTS].astype(F32)
    got_coef = got_meta[:, 0] + got_meta[:, 1] + got_meta[:, 2]
    got_row = got_meta[:, 3] * 64.0 + got_meta[:, 4]

    def split(v):
        first, second, last = v[:, :8], v[:, 8:16], v[:, 16:]
        keep = jnp.where(core == 0, first, second)
        give = jnp.where(core == 0, second, first)
        return jnp.concatenate([keep, last], axis=1), jnp.concatenate([give, last], axis=1)

    rows_keep, rows_give = split(recv_rows)
    coef_keep, coef_give = split(got_coef)
    row_keep, row_give = split(got_row)
    rows_got = swap(rows_give)
    small = jnp.concatenate([summed, coef_give.reshape(4, B), row_give.reshape(4, B)], axis=0)
    small = swap(small)
    summed_got = small[:CSLOTS]
    coef_all = jnp.concatenate([coef_keep.reshape(-1), small[CSLOTS : CSLOTS + 4].reshape(-1)])
    row_all = jnp.concatenate([row_keep.reshape(-1), small[CSLOTS + 4 :].reshape(-1)])
    row_at = row_all.astype(I32) - 1 - core * ITEMS_DEV
    rows = jnp.concatenate([rows_keep.reshape(-1, width), rows_got.reshape(-1, width)], axis=0)
    rows = (rows.astype(F32) * coef_all[:, None]).astype(BF)

    neg_sum = jnp.where(
        core == 0,
        jnp.concatenate([summed, summed_got], axis=1),
        jnp.concatenate([summed_got, summed], axis=1),
    )
    neg_high = neg_sum.astype(BF)
    neg_low = (neg_sum - neg_high.astype(F32)).astype(BF)
    rest = 128 - 2 * CSLOTS
    neg_rows = jnp.concatenate([neg_high, neg_low, jnp.zeros((rest, width), BF)], axis=0)
    neg_at = jnp.concatenate([neg_local, neg_local, jnp.full((rest,), -1, I32)])

    tile = 512
    whole = lambda shape: pl.BlockSpec(shape, lambda i: (0, 0))
    grad = pl.pallas_call(
        place_kernel,
        grid=(ITEMS_DEV // tile,),
        out_shape=jax.ShapeDtypeStruct((ITEMS_DEV, width), BF),
        in_specs=[whole((1, 2048)), whole((2048, width)), whole((1, 128)), whole((128, width))],
        out_specs=pl.BlockSpec((tile, width), lambda i: (i, 0)),
        cost_estimate=pl.CostEstimate(flops=9 << 30, bytes_accessed=8 << 20, transcendentals=0),
        compiler_params=pltpu.CompilerParams(vmem_limit_bytes=48 << 20),
    )(row_at[None], rows, neg_at[None], neg_rows)
    return loss, grad


def solution(mesh):
    fine = Mesh(mesh.devices.reshape(4, 4, 4, 2), ALL)
    in_specs = (P(ALL), P(ALL), P(ALL), P(), P(), P(ALL), P(MP), P(MP))
    return jax.shard_map(
        per_device, mesh=fine, in_specs=in_specs, out_specs=(P(ALL), P(ALL)), check_vma=False
    )
```

```python
import math

import jax
import jax.numpy as jnp
from jax import lax
from jax.experimental import pallas as pl
from jax.experimental.pallas import tpu as pltpu
from jax.sharding import Mesh, PartitionSpec as P

H = 4
EPSILON = 1e-05
ALL = ("y", "x", "z", "c")
CHIPS = ("y", "x", "z")
MP = ("x", "z", "c")
BF = jnp.bfloat16
F32 = jnp.float32
I32 = jnp.int32
DEVS = 128
NCHIPS = 64
CSLOTS = 24
SLOTS = NCHIPS * CSLOTS
ITEMS_DEV = 4096
B = 256
VMEM = pl.BlockSpec(memory_space=pltpu.VMEM)
SMEM = pl.BlockSpec(memory_space=pltpu.SMEM)
NT = (((1,), (1,)), ((), ()))
NEG_INF = float("-inf")
POS_INF = float("inf")
SWAP = ((0, 1), (1, 0))


def dot(a, b):
    return jnp.dot(a, b, preferred_element_type=F32)


def dot_nt(a, b):
    return lax.dot_general(a, b, NT, preferred_element_type=F32)


def iota(shape, dim):
    return lax.broadcasted_iota(I32, shape, dim)


def layer_norm(values):
    center = values - jnp.mean(values, axis=-1, keepdims=True)
    spread = jnp.mean(center * center, axis=-1, keepdims=True)
    return center * lax.rsqrt(spread + EPSILON)


def call(body, out_shape, in_specs, scratch=(), flops=0, nbytes=0):
    return pl.pallas_call(
        body,
        out_shape=out_shape,
        in_specs=in_specs,
        out_specs=jax.tree.map(lambda _: VMEM, out_shape),
        scratch_shapes=list(scratch),
        cost_estimate=pl.CostEstimate(flops=flops, bytes_accessed=nbytes, transcendentals=0),
        compiler_params=pltpu.CompilerParams(vmem_limit_bytes=56 << 20),
    )


def norm_kernel(events_ref, out_ref):
    @pl.loop(0, 4)
    def _(i):
        rows = pl.ds(pl.multiple_of(i * B, B), B)
        out_ref[rows, :] = layer_norm(events_ref[rows, :].astype(F32)).astype(BF)


def silu_of_half(h):
    return h + h * jnp.tanh(h)


def layer_kernel(
    info_ref, normed_ref, own_ref, other_ref, events_ref, follow_ref,
    hidden_ref, positive_ref, w_ref, act_ref, att_ref,
):
    core, length = info_ref[0], info_ref[1]
    for b in range(16):
        block = slice(b * 16, (b + 1) * 16)
        w_ref[pl.ds(pl.multiple_of(b * 32 + core * 16, 16), 16), :] = own_ref[block, :]
        w_ref[pl.ds(pl.multiple_of(b * 32 + (1 - core) * 16, 16), 16), :] = other_ref[block, :]

    @pl.loop(0, 4)
    def _(i):
        rows = pl.ds(pl.multiple_of(i * B, B), B)
        a = normed_ref[rows, :]
        live = iota((B, 512), 0) + i * B < length
        for n in range(4):
            cols = slice(n * 512, (n + 1) * 512)
            v = silu_of_half(0.5 * dot(a, w_ref[:, cols]))
            if n == 1:
                v = jnp.where(live, v, 0.0)
            act_ref[rows, cols] = v.astype(BF)

    causal = iota((B, B), 1) <= iota((B, B), 0)
    eye = iota((B, B), 1) == iota((B, B), 0)
    scale = 0.5 / math.sqrt(128)
    for i in range(4):
        rows = slice(i * B, (i + 1) * B)
        for h in range(H):
            q = act_ref[rows, 1024 + h * 128 : 1024 + (h + 1) * 128]
            total = None
            for j in range(i + 1):
                keys = slice(j * B, (j + 1) * B)
                s = dot_nt(q, act_ref[keys, 1536 + h * 128 : 1536 + (h + 1) * 128])
                w = silu_of_half(s * scale)
                if j == i:
                    w = jnp.where(causal, w, 0.0)
                t = dot(w.astype(BF), act_ref[keys, 512 + h * 128 : 512 + (h + 1) * 128])
                total = t if total is None else total + t
            att_ref[:, h * 128 : (h + 1) * 128] = total
        gated = (layer_norm(att_ref[...]) * act_ref[rows, :512].astype(F32)).astype(BF)
        hidden = (events_ref[rows, :].astype(F32) + dot(gated, w_ref[:, 2048:])).astype(BF)
        hidden_ref[rows, :] = hidden
        pos = jnp.sum(hidden.astype(F32) * follow_ref[rows, :].astype(F32), axis=1, keepdims=True)
        positive_ref[:, rows] = jnp.sum(jnp.where(eye, pos, 0.0), axis=0, keepdims=True)


def pack_kernel(hot_ref, hidden_ref, send_ref):
    @pl.loop(0, SLOTS // B)
    def _(m):
        rows = pl.ds(pl.multiple_of(m * B, B), B)
        send_ref[rows, :] = dot(hot_ref[rows, :], hidden_ref[...]).astype(BF)


def loss_kernel(
    info_ref, hidden_ref, own_ref, other_ref, ids_ref, logc_ref, positive_ref, targets_ref, hot_ref,
    index_ref, loss_ref, term_own_ref, term_other_ref, meta_ref, l_ref, probs_ref, coef_ref,
):
    core, length = info_ref[0], info_ref[1]
    own_cols = pl.ds(pl.multiple_of(core * B, B), B)
    other_cols = pl.ds(pl.multiple_of((1 - core) * B, B), B)
    chunks = [slice(m * B, (m + 1) * B) for m in range(SLOTS // B)]

    @pl.loop(0, 4)
    def _(t):
        at = pl.ds(pl.multiple_of(t * B, B), B)
        h_own = hidden_ref[at, own_cols]
        h_other = hidden_ref[at, other_cols]
        pos = positive_ref[:, at]
        target = targets_ref[:, at]
        top = pos
        for m in chunks:
            value = dot_nt(own_ref[m, :], h_own) + dot_nt(other_ref[m, :], h_other) - logc_ref[m, :]
            value = jnp.where(ids_ref[m, :] != target, value, NEG_INF)
            l_ref[m, :] = value
            top = jnp.maximum(top, jnp.max(value, axis=0, keepdims=True))
        total = jnp.exp(pos - top)
        for m in chunks:
            total = total + jnp.sum(jnp.exp(l_ref[m, :] - top), axis=0, keepdims=True)
        log_total = top + jnp.log(total)
        in_range = iota((1, B), 1) + t * B < length - 1
        loss_ref[:, at] = jnp.where(in_range, log_total - pos, 0.0)
        coef_ref[:, at] = jnp.where(in_range, jnp.exp(pos - log_total) - 1.0, 0.0)
        shift = jnp.where(in_range, log_total, POS_INF)
        for m in chunks:
            probs_ref[m, at] = jnp.exp(l_ref[m, :] - shift).astype(BF)

    coef = coef_ref[...]
    high = coef.astype(BF).astype(F32)
    middle = (coef - high).astype(BF).astype(F32)
    low = coef - high - middle
    pieces = jnp.concatenate(
        [high, middle, low, index_ref[...], jnp.zeros((11, 1024), F32)], axis=0
    ).astype(BF)
    for m in chunks:
        meta_ref[:, m] = dot_nt(pieces, hot_ref[m, :]).astype(BF)
        term_other_ref[m, :] = dot(probs_ref[m, :], hidden_ref[:, other_cols]).astype(BF)
        term_own_ref[m, :] = dot(probs_ref[m, :], hidden_ref[:, own_cols])


def place_kernel(index_ref, rows_ref, neg_index_ref, neg_ref, out_ref):
    tile = out_ref.shape[0]
    base = pl.program_id(0) * tile

    def onehot(index):
        return (iota((tile, index.shape[1]), 0) + base == index).astype(F32).astype(BF)

    out_ref[...] = (
        dot(onehot(index_ref[...]), rows_ref[...]) + dot(onehot(neg_index_ref[...]), neg_ref[...])
    ).astype(BF)


def chip_slots(ids):
    n = ids.shape[0]
    owner = ids // ITEMS_DEV
    hot = (iota((DEVS, n), 0) == owner[None, :]).astype(BF)
    tri = (iota((n, n), 0) < iota((n, n), 1)).astype(BF)
    rank = jnp.sum(dot(hot, tri) * hot.astype(F32), axis=0).astype(I32)
    within = jnp.where(rank < 8, (owner % 2) * 8 + rank, 8 + rank)
    return (owner // 2) * CSLOTS + within


def swap(v):
    return lax.ppermute(v, "c", SWAP)


def chips_a2a(v):
    return lax.all_to_all(v, CHIPS, split_axis=0, concat_axis=0, tiled=True)


def per_device(events, lengths, target_ids, neg_ids, neg_counts, item_table, w_uvqk, w_out):
    width = 512
    core = lax.axis_index("c")
    chip = lax.axis_index(CHIPS)
    info = jnp.stack([core, lengths[0]]).astype(I32)
    targets = target_ids[0]
    ev = events[0]

    w_mine = jnp.concatenate([w_uvqk, w_out], axis=1)
    w_own = lax.all_to_all(
        jnp.broadcast_to(w_mine[None], (16,) + w_mine.shape), ("x", "z"), split_axis=0, concat_axis=0, tiled=True
    ).reshape(256, 2560)
    normed = call(norm_kernel, jax.ShapeDtypeStruct((1024, 512), BF), [VMEM], nbytes=2 << 20, flops=1 << 20)(ev)

    neg_slot = chip_slots(neg_ids)
    slot_ids = jnp.arange(SLOTS, dtype=I32)
    here = iota((CSLOTS, 1), 0) + chip * CSLOTS == neg_slot[None, :]
    mine = here & ((neg_ids // ITEMS_DEV) % 2 == core)[None, :]
    neg_local = jnp.sum(jnp.where(mine, (neg_ids % ITEMS_DEV)[None, :] + 1, 0), axis=1) - 1
    packed = jnp.where((neg_local >= 0)[:, None], item_table[jnp.maximum(neg_local, 0)], 0)
    packed_own = lax.dynamic_slice(packed, (0, core * B), (CSLOTS, B))
    packed_other = lax.dynamic_slice(packed, (0, (1 - core) * B), (CSLOTS, B))
    packed_own = packed_own + swap(packed_other)
    match = slot_ids[:, None] == neg_slot[None, :]
    slot_neg_id = jnp.sum(jnp.where(match, neg_ids[None, :] + 1, 0), axis=1) - 1
    slot_count = jnp.sum(jnp.where(match, neg_counts[None, :], 0), axis=1)
    slot_logc = jnp.where(slot_count > 0, jnp.log(slot_count.astype(F32)), POS_INF)

    target_slot = chip_slots(targets)
    hot = (slot_ids[:, None] == target_slot[None, :]).astype(BF)
    chip_row = targets % (2 * ITEMS_DEV) + 1
    index = jnp.stack([chip_row // 64, chip_row % 64]).astype(F32)

    follow = jnp.concatenate([ev[1:], jnp.zeros((1, width), BF)], axis=0)
    ids_col, logc_col = slot_neg_id[:, None], slot_logc[:, None]
    w_own, normed, hot, ids_col, logc_col, follow, index, packed_own = lax.optimization_barrier(
        (w_own, normed, hot, ids_col, logc_col, follow, index, packed_own)
    )
    neg_own = chips_a2a(jnp.broadcast_to(packed_own[None], (NCHIPS, CSLOTS, B))).reshape(SLOTS, B)
    w_other = swap(w_own)
    hidden, positive = call(
        layer_kernel,
        (
            jax.ShapeDtypeStruct((1024, width), BF),
            jax.ShapeDtypeStruct((1, 1024), F32),
        ),
        [SMEM] + [VMEM] * 5,
        scratch=[
            pltpu.VMEM((512, 2560), BF),
            pltpu.VMEM((1024, 2048), BF),
            pltpu.VMEM((B, width), F32),
        ],
        flops=9 << 30,
        nbytes=12 << 20,
    )(info, normed, w_own, w_other, ev, follow)
    neg_own, hidden = lax.optimization_barrier((neg_own, hidden))
    neg_other = swap(neg_own)
    send_rows = call(
        pack_kernel, jax.ShapeDtypeStruct((SLOTS, width), BF), [VMEM] * 2, flops=2 << 30, nbytes=6 << 20
    )(hot, hidden)

    recv_rows = chips_a2a(send_rows.reshape(NCHIPS, CSLOTS, width))

    loss, term_own, term_other, meta = call(
        loss_kernel,
        (
            jax.ShapeDtypeStruct((1, 1024), F32),
            jax.ShapeDtypeStruct((SLOTS, B), F32),
            jax.ShapeDtypeStruct((SLOTS, B), BF),
            jax.ShapeDtypeStruct((16, SLOTS), BF),
        ),
        [SMEM] + [VMEM] * 9,
        scratch=[
            pltpu.VMEM((SLOTS, B), F32),
            pltpu.VMEM((SLOTS, 1024), BF),
            pltpu.VMEM((1, 1024), F32),
        ],
        flops=7 << 30,
        nbytes=12 << 20,
    )(
        info, hidden, neg_own, neg_other, ids_col, logc_col, positive,
        target_ids, hot, index,
    )
    term = (term_own + swap(term_other).astype(F32)).astype(BF).reshape(NCHIPS, CSLOTS, B)
    meta = meta[:8].reshape(8, NCHIPS, CSLOTS).transpose(1, 0, 2)
    meta = jnp.pad(meta, ((0, 0), (0, 0), (0, B - CSLOTS)))
    got = chips_a2a(jnp.concatenate([term, meta], axis=1))
    summed = jnp.sum(got[:, :CSLOTS].astype(F32), axis=0)
    got_meta = got[:, CSLOTS:, :CSLOTS].astype(F32)
    got_coef = got_meta[:, 0] + got_meta[:, 1] + got_meta[:, 2]
    got_row = got_meta[:, 3] * 64.0 + got_meta[:, 4]

    def split(v):
        first, second, last = v[:, :8], v[:, 8:16], v[:, 16:]
        keep = jnp.where(core == 0, first, second)
        give = jnp.where(core == 0, second, first)
        return jnp.concatenate([keep, last], axis=1), jnp.concatenate([give, last], axis=1)

    rows_keep, rows_give = split(recv_rows)
    coef_keep, coef_give = split(got_coef)
    row_keep, row_give = split(got_row)
    rows_got = swap(rows_give)
    small = jnp.concatenate([summed, coef_give.reshape(4, B), row_give.reshape(4, B)], axis=0)
    small = swap(small)
    summed_got = small[:CSLOTS]
    coef_all = jnp.concatenate([coef_keep.reshape(-1), small[CSLOTS : CSLOTS + 4].reshape(-1)])
    row_all = jnp.concatenate([row_keep.reshape(-1), small[CSLOTS + 4 :].reshape(-1)])
    row_at = row_all.astype(I32) - 1 - core * ITEMS_DEV
    rows = jnp.concatenate([rows_keep.reshape(-1, width), rows_got.reshape(-1, width)], axis=0)
    rows = (rows.astype(F32) * coef_all[:, None]).astype(BF)

    neg_sum = jnp.where(
        core == 0,
        jnp.concatenate([summed, summed_got], axis=1),
        jnp.concatenate([summed_got, summed], axis=1),
    )
    neg_high = neg_sum.astype(BF)
    neg_low = (neg_sum - neg_high.astype(F32)).astype(BF)
    rest = 128 - 2 * CSLOTS
    neg_rows = jnp.concatenate([neg_high, neg_low, jnp.zeros((rest, width), BF)], axis=0)
    neg_at = jnp.concatenate([neg_local, neg_local, jnp.full((rest,), -1, I32)])

    tile = 512
    whole = lambda shape: pl.BlockSpec(shape, lambda i: (0, 0))
    grad = pl.pallas_call(
        place_kernel,
        grid=(ITEMS_DEV // tile,),
        out_shape=jax.ShapeDtypeStruct((ITEMS_DEV, width), BF),
        in_specs=[whole((1, 2048)), whole((2048, width)), whole((1, 128)), whole((128, width))],
        out_specs=pl.BlockSpec((tile, width), lambda i: (i, 0)),
        cost_estimate=pl.CostEstimate(flops=9 << 30, bytes_accessed=8 << 20, transcendentals=0),
        compiler_params=pltpu.CompilerParams(vmem_limit_bytes=48 << 20),
    )(row_at[None], rows, neg_at[None], neg_rows)
    return loss, grad


def solution(mesh):
    fine = Mesh(mesh.devices.reshape(4, 4, 4, 2), ALL)
    in_specs = (P(ALL), P(ALL), P(ALL), P(), P(), P(ALL), P(MP), P(MP))
    return jax.shard_map(
        per_device, mesh=fine, in_specs=in_specs, out_specs=(P(ALL), P(ALL)), check_vma=False
    )
```

```python
import math

import jax
import jax.numpy as jnp
from jax import lax
from jax.experimental import pallas as pl
from jax.experimental.pallas import tpu as pltpu
from jax.sharding import Mesh, PartitionSpec as P

H = 4
EPSILON = 1e-05
ALL = ("y", "x", "z", "c")
CHIPS = ("y", "x", "z")
MP = ("x", "z", "c")
BF = jnp.bfloat16
F32 = jnp.float32
I32 = jnp.int32
DEVS = 128
NCHIPS = 64
CSLOTS = 24
SLOTS = NCHIPS * CSLOTS
ITEMS_DEV = 4096
B = 256
VMEM = pl.BlockSpec(memory_space=pltpu.VMEM)
SMEM = pl.BlockSpec(memory_space=pltpu.SMEM)
NT = (((1,), (1,)), ((), ()))
NEG_INF = float("-inf")
POS_INF = float("inf")
SWAP = ((0, 1), (1, 0))


def dot(a, b):
    return jnp.dot(a, b, preferred_element_type=F32)


def dot_nt(a, b):
    return lax.dot_general(a, b, NT, preferred_element_type=F32)


def iota(shape, dim):
    return lax.broadcasted_iota(I32, shape, dim)


def layer_norm(values):
    center = values - jnp.mean(values, axis=-1, keepdims=True)
    spread = jnp.mean(center * center, axis=-1, keepdims=True)
    return center * lax.rsqrt(spread + EPSILON)


def call(body, out_shape, in_specs, scratch=(), flops=0, nbytes=0, vmem=56):
    return pl.pallas_call(
        body,
        out_shape=out_shape,
        in_specs=in_specs,
        out_specs=jax.tree.map(lambda _: VMEM, out_shape),
        scratch_shapes=list(scratch),
        cost_estimate=pl.CostEstimate(flops=flops, bytes_accessed=nbytes, transcendentals=0),
        compiler_params=pltpu.CompilerParams(vmem_limit_bytes=vmem << 20),
    )


def onehot(base, count, index):
    return (iota((count, index.shape[1]), 0) + base == index).astype(F32).astype(BF)


def prep_kernel(
    info_ref, events_ref, targets_ref, negs_ref, counts_ref,
    normed_ref, ids_ref, logc_ref, slot_ref, index_ref, local_ref, tri_ref, owner_ref,
):
    core, chip = info_ref[0], info_ref[2]
    targets, negs = targets_ref[...], negs_ref[...]
    n = targets.shape[1]

    for k in range(4):
        rows = slice(k * B, (k + 1) * B)
        tri_ref[rows, :] = (iota((B, n), 0) + k * B < iota((B, n), 1)).astype(F32).astype(BF)
    t_owner, n_owner = targets >> 12, negs >> 12
    owner_ref[:DEVS, :] = onehot(0, DEVS, t_owner)
    owner_ref[DEVS:, :] = onehot(0, DEVS, n_owner)
    before = dot(owner_ref[...], tri_ref[...]) * owner_ref[...].astype(F32)
    t_rank = jnp.sum(before[:DEVS], axis=0, keepdims=True).astype(I32)
    n_rank = jnp.sum(before[DEVS:], axis=0, keepdims=True).astype(I32)

    def slot(owner, rank):
        return (owner >> 1) * CSLOTS + jnp.where(rank < 8, (owner & 1) * 8 + rank, 8 + rank)

    slot_ref[...] = slot(t_owner, t_rank)
    n_slot = slot(n_owner, n_rank)
    row = (targets & (2 * ITEMS_DEV - 1)) + 1
    index_ref[0:1, :] = (row >> 6).astype(F32)
    index_ref[1:2, :] = (row & 63).astype(F32)

    mine = (iota((32, n), 0) + chip * CSLOTS == n_slot) & ((n_owner & 1) == core)
    mine = mine & (iota((32, n), 0) < CSLOTS)
    local = jnp.max(jnp.where(mine, negs & (ITEMS_DEV - 1), -1), axis=1, keepdims=True)
    local_ref[...] = jnp.broadcast_to(local, (32, 128))
    logs = jnp.log(counts_ref[...].astype(F32))
    for m in range(SLOTS // B):
        rows = slice(m * B, (m + 1) * B)
        here = iota((B, n), 0) + m * B == n_slot
        ids = jnp.max(jnp.where(here, negs, -1), axis=1, keepdims=True)
        logc = jnp.min(jnp.where(here, logs, POS_INF), axis=1, keepdims=True)
        ids_ref[rows, :] = jnp.broadcast_to(ids, (B, 128))
        logc_ref[rows, :] = jnp.broadcast_to(logc, (B, 128))

    @pl.loop(0, 4)
    def _(i):
        rows = pl.ds(pl.multiple_of(i * B, B), B)
        normed_ref[rows, :] = layer_norm(events_ref[rows, :].astype(F32)).astype(BF)


def silu_of_half(h):
    return h + h * jnp.tanh(h)


def layer_kernel(
    info_ref, normed_ref, own_ref, other_ref, events_ref, follow_ref,
    hidden_ref, positive_ref, w_ref, act_ref, att_ref,
):
    core, length = info_ref[0], info_ref[1]
    for b in range(16):
        block = slice(b * 16, (b + 1) * 16)
        w_ref[pl.ds(pl.multiple_of(b * 32 + core * 16, 16), 16), :] = own_ref[block, :]
        w_ref[pl.ds(pl.multiple_of(b * 32 + (1 - core) * 16, 16), 16), :] = other_ref[block, :]

    @pl.loop(0, 4)
    def _(i):
        rows = pl.ds(pl.multiple_of(i * B, B), B)
        a = normed_ref[rows, :]
        live = iota((B, 512), 0) + i * B < length
        for n in range(4):
            cols = slice(n * 512, (n + 1) * 512)
            v = silu_of_half(0.5 * dot(a, w_ref[:, cols]))
            if n == 1:
                v = jnp.where(live, v, 0.0)
            act_ref[rows, cols] = v.astype(BF)

    causal = iota((B, B), 1) <= iota((B, B), 0)
    eye = iota((B, B), 1) == iota((B, B), 0)
    scale = 0.5 / math.sqrt(128)
    for i in range(4):
        rows = slice(i * B, (i + 1) * B)
        for h in range(H):
            q = act_ref[rows, 1024 + h * 128 : 1024 + (h + 1) * 128]
            total = None
            for j in range(i + 1):
                keys = slice(j * B, (j + 1) * B)
                s = dot_nt(q, act_ref[keys, 1536 + h * 128 : 1536 + (h + 1) * 128])
                w = silu_of_half(s * scale)
                if j == i:
                    w = jnp.where(causal, w, 0.0)
                t = dot(w.astype(BF), act_ref[keys, 512 + h * 128 : 512 + (h + 1) * 128])
                total = t if total is None else total + t
            att_ref[:, h * 128 : (h + 1) * 128] = total
        gated = (layer_norm(att_ref[...]) * act_ref[rows, :512].astype(F32)).astype(BF)
        hidden = (events_ref[rows, :].astype(F32) + dot(gated, w_ref[:, 2048:])).astype(BF)
        hidden_ref[rows, :] = hidden
        pos = jnp.sum(hidden.astype(F32) * follow_ref[rows, :].astype(F32), axis=1, keepdims=True)
        positive_ref[:, rows] = jnp.sum(jnp.where(eye, pos, 0.0), axis=0, keepdims=True)


def pack_kernel(slot_ref, hidden_ref, send_ref):
    base = pl.program_id(0) * send_ref.shape[0]
    send_ref[...] = dot(onehot(base, send_ref.shape[0], slot_ref[...]), hidden_ref[...]).astype(BF)


def loss_kernel(
    info_ref, hidden_ref, own_ref, other_ref, ids_ref, logc_ref, positive_ref, targets_ref, slot_ref,
    index_ref, loss_ref, term_own_ref, term_other_ref, meta_ref, l_ref, probs_ref, coef_ref,
):
    core, length = info_ref[0], info_ref[1]
    own_cols = pl.ds(pl.multiple_of(core * B, B), B)
    other_cols = pl.ds(pl.multiple_of((1 - core) * B, B), B)
    chunks = [slice(m * B, (m + 1) * B) for m in range(SLOTS // B)]

    @pl.loop(0, 4)
    def _(t):
        at = pl.ds(pl.multiple_of(t * B, B), B)
        h_own = hidden_ref[at, own_cols]
        h_other = hidden_ref[at, other_cols]
        pos = positive_ref[:, at]
        target = targets_ref[:, at]
        top = pos
        for m in chunks:
            logc, ids = logc_ref[m, :], ids_ref[m, :]
            value = dot_nt(own_ref[m, :], h_own) + dot_nt(other_ref[m, :], h_other)
            value = value - jnp.concatenate([logc, logc], axis=1)
            value = jnp.where(jnp.concatenate([ids, ids], axis=1) != target, value, NEG_INF)
            l_ref[m, :] = value
            top = jnp.maximum(top, jnp.max(value, axis=0, keepdims=True))
        total = jnp.exp(pos - top)
        for m in chunks:
            total = total + jnp.sum(jnp.exp(l_ref[m, :] - top), axis=0, keepdims=True)
        log_total = top + jnp.log(total)
        in_range = iota((1, B), 1) + t * B < length - 1
        loss_ref[:, at] = jnp.where(in_range, log_total - pos, 0.0)
        coef_ref[:, at] = jnp.where(in_range, jnp.exp(pos - log_total) - 1.0, 0.0)
        shift = jnp.where(in_range, log_total, POS_INF)
        for m in chunks:
            probs_ref[m, at] = jnp.exp(l_ref[m, :] - shift).astype(BF)

    coef = coef_ref[...]
    high = coef.astype(BF).astype(F32)
    middle = (coef - high).astype(BF).astype(F32)
    low = coef - high - middle
    pieces = jnp.concatenate(
        [high, middle, low, index_ref[...], jnp.zeros((11, 1024), F32)], axis=0
    ).astype(BF)
    for m in chunks:
        meta_ref[:, m] = dot_nt(pieces, onehot(m.start, B, slot_ref[...])).astype(BF)
        term_other_ref[m, :] = dot(probs_ref[m, :], hidden_ref[:, other_cols]).astype(BF)
        term_own_ref[m, :] = dot(probs_ref[m, :], hidden_ref[:, own_cols])


def place_kernel(index_ref, rows_ref, neg_index_ref, neg_ref, out_ref):
    tile = out_ref.shape[0]
    base = pl.program_id(0) * tile
    out_ref[...] = (
        dot(onehot(base, tile, index_ref[...]), rows_ref[...])
        + dot(onehot(base, tile, neg_index_ref[...]), neg_ref[...])
    ).astype(BF)


def swap(v):
    return lax.ppermute(v, "c", SWAP)


def chips_a2a(v):
    return lax.all_to_all(v, CHIPS, split_axis=0, concat_axis=0, tiled=True)


def per_device(events, lengths, target_ids, neg_ids, neg_counts, item_table, w_uvqk, w_out):
    width = 512
    core = lax.axis_index("c")
    chip = lax.axis_index(CHIPS)
    info = jnp.stack([core, lengths[0], chip]).astype(I32)
    ev = events[0]

    w_mine = jnp.concatenate([w_uvqk, w_out], axis=1)
    w_own = lax.all_to_all(
        jnp.broadcast_to(w_mine[None], (16,) + w_mine.shape), ("x", "z"), split_axis=0, concat_axis=0, tiled=True
    ).reshape(256, 2560)
    normed, ids, logc, target_slot, index, neg_local = call(
        prep_kernel,
        (
            jax.ShapeDtypeStruct((1024, width), BF),
            jax.ShapeDtypeStruct((SLOTS, 128), I32),
            jax.ShapeDtypeStruct((SLOTS, 128), F32),
            jax.ShapeDtypeStruct((1, 1024), I32),
            jax.ShapeDtypeStruct((2, 1024), F32),
            jax.ShapeDtypeStruct((32, 128), I32),
        ),
        [SMEM] + [VMEM] * 4,
        scratch=[pltpu.VMEM((1024, 1024), BF), pltpu.VMEM((2 * DEVS, 1024), BF)],
        vmem=16,
    )(info, ev, target_ids, neg_ids[None], neg_counts[None])

    neg_local = neg_local[:CSLOTS, 0]
    packed = jnp.where((neg_local >= 0)[:, None], item_table[jnp.maximum(neg_local, 0)], 0)
    packed_own = lax.dynamic_slice(packed, (0, core * B), (CSLOTS, B))
    packed_other = lax.dynamic_slice(packed, (0, (1 - core) * B), (CSLOTS, B))
    packed_own = packed_own + swap(packed_other)
    neg_block = jnp.broadcast_to(packed_own[None], (NCHIPS, CSLOTS, B))

    follow = jnp.concatenate([ev[1:], jnp.zeros((1, width), BF)], axis=0)
    w_own, normed, follow, neg_block = lax.optimization_barrier((w_own, normed, follow, neg_block))
    neg_own = chips_a2a(neg_block).reshape(SLOTS, B)
    w_other = swap(w_own)
    hidden, positive = call(
        layer_kernel,
        (
            jax.ShapeDtypeStruct((1024, width), BF),
            jax.ShapeDtypeStruct((1, 1024), F32),
        ),
        [SMEM] + [VMEM] * 5,
        scratch=[
            pltpu.VMEM((512, 2560), BF),
            pltpu.VMEM((1024, 2048), BF),
            pltpu.VMEM((B, width), F32),
        ],
        flops=9 << 30,
        nbytes=12 << 20,
        vmem=24,
    )(info, normed, w_own, w_other, ev, follow)
    whole = lambda shape: pl.BlockSpec(shape, lambda i: (0, 0))
    send_rows = pl.pallas_call(
        pack_kernel,
        grid=(SLOTS // B,),
        out_shape=jax.ShapeDtypeStruct((SLOTS, width), BF),
        in_specs=[whole((1, 1024)), whole((1024, width))],
        out_specs=pl.BlockSpec((B, width), lambda i: (i, 0)),
        cost_estimate=pl.CostEstimate(flops=2 << 30, bytes_accessed=3 << 20, transcendentals=0),
        compiler_params=pltpu.CompilerParams(vmem_limit_bytes=16 << 20),
    )(target_slot, hidden)
    neg_own, send_rows = lax.optimization_barrier((neg_own, send_rows))
    neg_other = swap(neg_own)

    recv_rows = chips_a2a(send_rows.reshape(NCHIPS, CSLOTS, width))

    loss, term_own, term_other, meta = call(
        loss_kernel,
        (
            jax.ShapeDtypeStruct((1, 1024), F32),
            jax.ShapeDtypeStruct((SLOTS, B), F32),
            jax.ShapeDtypeStruct((SLOTS, B), BF),
            jax.ShapeDtypeStruct((16, SLOTS), BF),
        ),
        [SMEM] + [VMEM] * 9,
        scratch=[
            pltpu.VMEM((SLOTS, B), F32),
            pltpu.VMEM((SLOTS, 1024), BF),
            pltpu.VMEM((1, 1024), F32),
        ],
        flops=7 << 30,
        nbytes=12 << 20,
        vmem=28,
    )(
        info, hidden, neg_own, neg_other, ids, logc, positive, target_ids, target_slot, index,
    )
    term = (term_own + swap(term_other).astype(F32)).astype(BF).reshape(NCHIPS, CSLOTS, B)
    meta = meta[:8].reshape(8, NCHIPS, CSLOTS).transpose(1, 0, 2)
    meta = jnp.pad(meta, ((0, 0), (0, 0), (0, B - CSLOTS)))
    got = chips_a2a(jnp.concatenate([term, meta], axis=1))
    summed = jnp.sum(got[:, :CSLOTS].astype(F32), axis=0)
    got_meta = got[:, CSLOTS:, :CSLOTS].astype(F32)
    got_coef = got_meta[:, 0] + got_meta[:, 1] + got_meta[:, 2]
    got_row = got_meta[:, 3] * 64.0 + got_meta[:, 4]

    def split(v):
        first, second, last = v[:, :8], v[:, 8:16], v[:, 16:]
        keep = jnp.where(core == 0, first, second)
        give = jnp.where(core == 0, second, first)
        return jnp.concatenate([keep, last], axis=1), jnp.concatenate([give, last], axis=1)

    rows_keep, rows_give = split(recv_rows)
    coef_keep, coef_give = split(got_coef)
    row_keep, row_give = split(got_row)
    rows_got = swap(rows_give)
    small = jnp.concatenate([summed, coef_give.reshape(4, B), row_give.reshape(4, B)], axis=0)
    small = swap(small)
    summed_got = small[:CSLOTS]
    coef_all = jnp.concatenate([coef_keep.reshape(-1), small[CSLOTS : CSLOTS + 4].reshape(-1)])
    row_all = jnp.concatenate([row_keep.reshape(-1), small[CSLOTS + 4 :].reshape(-1)])
    row_at = row_all.astype(I32) - 1 - core * ITEMS_DEV
    rows = jnp.concatenate([rows_keep.reshape(-1, width), rows_got.reshape(-1, width)], axis=0)
    rows = (rows.astype(F32) * coef_all[:, None]).astype(BF)

    neg_sum = jnp.where(
        core == 0,
        jnp.concatenate([summed, summed_got], axis=1),
        jnp.concatenate([summed_got, summed], axis=1),
    )
    neg_high = neg_sum.astype(BF)
    neg_low = (neg_sum - neg_high.astype(F32)).astype(BF)
    rest = 128 - 2 * CSLOTS
    neg_rows = jnp.concatenate([neg_high, neg_low, jnp.zeros((rest, width), BF)], axis=0)
    neg_at = jnp.concatenate([neg_local, neg_local, jnp.full((rest,), -1, I32)])

    tile = 512
    grad = pl.pallas_call(
        place_kernel,
        grid=(ITEMS_DEV // tile,),
        out_shape=jax.ShapeDtypeStruct((ITEMS_DEV, width), BF),
        in_specs=[whole((1, 2048)), whole((2048, width)), whole((1, 128)), whole((128, width))],
        out_specs=pl.BlockSpec((tile, width), lambda i: (i, 0)),
        cost_estimate=pl.CostEstimate(flops=9 << 30, bytes_accessed=8 << 20, transcendentals=0),
        compiler_params=pltpu.CompilerParams(vmem_limit_bytes=24 << 20),
    )(row_at[None], rows, neg_at[None], neg_rows)
    return loss, grad


def solution(mesh):
    fine = Mesh(mesh.devices.reshape(4, 4, 4, 2), ALL)
    in_specs = (P(ALL), P(ALL), P(ALL), P(), P(), P(ALL), P(MP), P(MP))
    return jax.shard_map(
        per_device, mesh=fine, in_specs=in_specs, out_specs=(P(ALL), P(ALL)), check_vma=False
    )
```

```python
import math

import jax
import jax.numpy as jnp
from jax import lax
from jax.experimental import pallas as pl
from jax.experimental.pallas import tpu as pltpu
from jax.sharding import Mesh, PartitionSpec as P

H = 4
EPSILON = 1e-05
ALL = ("y", "x", "z", "c")
CHIPS = ("y", "x", "z")
MP = ("x", "z", "c")
BF = jnp.bfloat16
F32 = jnp.float32
I32 = jnp.int32
DEVS = 128
NCHIPS = 64
CSLOTS = 24
SLOTS = NCHIPS * CSLOTS
BLOCK = 2 * CSLOTS + 8
GROUP = 8
ITEMS_DEV = 4096
B = 256
TILE = 512
VMEM = pl.BlockSpec(memory_space=pltpu.VMEM)
SMEM = pl.BlockSpec(memory_space=pltpu.SMEM)
NT = (((1,), (1,)), ((), ()))
NEG_INF = float("-inf")
POS_INF = float("inf")
SWAP = ((0, 1), (1, 0))


def dot(a, b):
    return jnp.dot(a, b, preferred_element_type=F32)


def dot_nt(a, b):
    return lax.dot_general(a, b, NT, preferred_element_type=F32)


def iota(shape, dim):
    return lax.broadcasted_iota(I32, shape, dim)


def layer_norm(values):
    center = values - jnp.mean(values, axis=-1, keepdims=True)
    spread = jnp.mean(center * center, axis=-1, keepdims=True)
    return center * lax.rsqrt(spread + EPSILON)


def call(body, out_shape, in_specs, scratch=(), flops=0, nbytes=0, vmem=56):
    return pl.pallas_call(
        body,
        out_shape=out_shape,
        in_specs=in_specs,
        out_specs=jax.tree.map(lambda _: VMEM, out_shape),
        scratch_shapes=list(scratch),
        cost_estimate=pl.CostEstimate(flops=flops, bytes_accessed=nbytes, transcendentals=0),
        compiler_params=pltpu.CompilerParams(vmem_limit_bytes=vmem << 20),
    )


def onehot(base, count, index):
    return (iota((count, index.shape[1]), 0) + base == index).astype(F32).astype(BF)


def by_place(high, low, pieces, count, weights=(1.0, 1.0, 1.0)):
    rows = iota((count, high.shape[1]), 0) == high
    cols = onehot(0, 128, low)
    return sum(
        w * dot_nt(jnp.where(rows, p.astype(F32), 0.0).astype(BF), cols) for p, w in zip(pieces, weights)
    )


def prep_kernel(
    info_ref, events_ref, targets_ref, negs_ref, counts_ref,
    normed_ref, ids_ref, logc_ref, slot_ref, row_ref, local_ref, tri_ref, owner_ref, order_ref,
):
    core, chip = info_ref[0], info_ref[2]
    targets, negs = targets_ref[...], negs_ref[...]
    n = targets.shape[1]

    for k in range(4):
        rows = slice(k * B, (k + 1) * B)
        tri_ref[rows, :] = (iota((B, n), 0) + k * B < iota((B, n), 1)).astype(F32).astype(BF)
    t_owner, n_owner = targets >> 12, negs >> 12
    owner_ref[:DEVS, :] = onehot(0, DEVS, t_owner)
    owner_ref[DEVS:, :] = onehot(0, DEVS, n_owner)
    before = dot(owner_ref[...], tri_ref[...]) * owner_ref[...].astype(F32)
    t_rank = jnp.sum(before[:DEVS], axis=0, keepdims=True).astype(I32)
    n_rank = jnp.sum(before[DEVS:], axis=0, keepdims=True).astype(I32)

    def within(owner, rank):
        return jnp.where(rank < 8, (owner & 1) * 8 + rank, 8 + rank)

    t_within = within(t_owner, t_rank)
    slot_ref[0:1, :] = (t_owner >> 1) * CSLOTS + t_within
    slot_ref[1:2, :] = t_owner >> 1
    slot_ref[2:3, :] = t_within
    n_slot = (n_owner >> 1) * CSLOTS + within(n_owner, n_rank)
    row = (targets & (2 * ITEMS_DEV - 1)) + 1
    row_ref[0] = by_place(t_owner >> 1, t_within, [row >> 6], NCHIPS)
    row_ref[1] = by_place(t_owner >> 1, t_within, [row & 63], NCHIPS)

    mine = (iota((32, n), 0) + chip * CSLOTS == n_slot) & ((n_owner & 1) == core)
    mine = mine & (iota((32, n), 0) < CSLOTS)
    local = jnp.max(jnp.where(mine, negs & (ITEMS_DEV - 1), -1), axis=1, keepdims=True)
    local_ref[...] = jnp.broadcast_to(local, (32, 128))
    logs = jnp.log(counts_ref[...].astype(F32))
    for m in range(SLOTS // B):
        rows = slice(m * B, (m + 1) * B)
        here = iota((B, n), 0) + m * B == n_slot
        ids = jnp.max(jnp.where(here, negs, -1), axis=1, keepdims=True)
        logc = jnp.min(jnp.where(here, logs, POS_INF), axis=1, keepdims=True)
        ids_ref[rows, :] = jnp.broadcast_to(ids, (B, 128))
        logc_ref[rows, :] = jnp.broadcast_to(logc, (B, 128))

    k = iota((512, 512), 1)
    source = ((k & 255) >> 4) * 32 + jnp.where(k < 256, core, 1 - core) * 16 + (k & 15)
    order_ref[...] = (iota((512, 512), 0) == source).astype(F32).astype(BF)

    @pl.loop(0, 4)
    def _(i):
        rows = pl.ds(pl.multiple_of(i * B, B), B)
        normed = layer_norm(events_ref[rows, :].astype(F32)).astype(BF)
        normed_ref[rows, :] = dot(normed, order_ref[...]).astype(BF)


def block_of(rows, pieces):
    chips = rows.shape[0]
    pieces = [p[:, None, :] for p in pieces] + [jnp.zeros((chips, 8 - len(pieces), 128), F32)]
    return jnp.concatenate([rows[:, :, :128], rows[:, :, 128:]] + pieces, axis=1).astype(BF)


def neg_block_kernel(mine_ref, other_ref, row_ref, out_ref):
    rows = mine_ref[...].astype(F32) + other_ref[...].astype(F32)
    rows = jnp.broadcast_to(rows[None, :CSLOTS], (GROUP, CSLOTS, B))
    for g in range(NCHIPS // GROUP):
        chips = slice(g * GROUP, (g + 1) * GROUP)
        out_ref[chips] = block_of(rows, [row_ref[0, chips, :], row_ref[1, chips, :]])


def term_block_kernel(own_ref, other_ref, meta_ref, out_ref):
    for g in range(NCHIPS // GROUP):
        chips = slice(g * GROUP, (g + 1) * GROUP)
        slots = slice(g * GROUP * CSLOTS, (g + 1) * GROUP * CSLOTS)
        rows = (own_ref[slots, :] + other_ref[slots, :].astype(F32)).reshape(GROUP, CSLOTS, B)
        out_ref[chips] = block_of(rows, [meta_ref[k, chips, :] for k in range(3)])


def unpack_kernel(own_ref, other_ref, own_out_ref, other_out_ref, row_ref):
    for k, (block_ref, out_ref) in enumerate(((own_ref, own_out_ref), (other_ref, other_out_ref))):
        for g in range(NCHIPS // GROUP):
            chips = slice(g * GROUP, (g + 1) * GROUP)
            block = block_ref[chips].astype(F32)
            halves = [
                block[:, h * CSLOTS : (h + 1) * CSLOTS].reshape(GROUP * CSLOTS, 128) for h in range(2)
            ]
            slots = slice(g * GROUP * CSLOTS, (g + 1) * GROUP * CSLOTS)
            out_ref[slots, :] = jnp.concatenate(halves, axis=1).astype(BF)
            numbers = block[:, 2 * CSLOTS :]
            row_ref[k, chips, :] = (numbers[:, 0] * 64.0 + numbers[:, 1]).astype(I32)


def silu_of_half(h):
    return h + h * jnp.tanh(h)


def layer_kernel(
    info_ref, slot_ref, own_hbm, normed_hbm, other_hbm, events_hbm, follow_hbm,
    positive_ref, hidden_hbm, send_hbm,
    w_ref, own_ref, other_ref, normed_ref, events_ref, follow_ref, act_ref, att_ref, hidden_ref, send_ref, in_sem, out_sem,
):
    core, length = info_ref[0], info_ref[1]
    pairs = (
        (normed_hbm, normed_ref), (own_hbm, own_ref), (other_hbm, other_ref),
        (events_hbm, events_ref), (follow_hbm, follow_ref),
    )
    inputs = [pltpu.make_async_copy(source, to, in_sem.at[k]) for k, (source, to) in enumerate(pairs)]
    for copy in inputs:
        copy.start()
    for copy in inputs[:3]:
        copy.wait()

    @pl.loop(0, 4)
    def _(i):
        rows = pl.ds(pl.multiple_of(i * B, B), B)
        a = normed_ref[rows, :B]
        b = normed_ref[rows, B:]
        live = iota((B, 512), 0) + i * B < length
        for n in range(4):
            cols = slice(n * 512, (n + 1) * 512)
            v = silu_of_half(0.5 * (dot(a, own_ref[:, cols]) + dot(b, other_ref[:, cols])))
            if n == 1:
                v = jnp.where(live, v, 0.0)
            act_ref[rows, cols] = v.astype(BF)

    for b in range(16):
        block = slice(b * 16, (b + 1) * 16)
        w_ref[pl.ds(pl.multiple_of(b * 32 + core * 16, 16), 16), :] = own_ref[block, 2048:]
        w_ref[pl.ds(pl.multiple_of(b * 32 + (1 - core) * 16, 16), 16), :] = other_ref[block, 2048:]
    for copy in inputs[3:]:
        copy.wait()
    causal = iota((B, B), 1) <= iota((B, B), 0)
    eye = iota((B, B), 1) == iota((B, B), 0)
    scale = 0.5 / math.sqrt(128)
    for i in range(4):
        rows = slice(i * B, (i + 1) * B)
        for h in range(H):
            q = act_ref[rows, 1024 + h * 128 : 1024 + (h + 1) * 128]
            total = None
            for j in range(i + 1):
                keys = slice(j * B, (j + 1) * B)
                s = dot_nt(q, act_ref[keys, 1536 + h * 128 : 1536 + (h + 1) * 128])
                w = silu_of_half(s * scale)
                if j == i:
                    w = jnp.where(causal, w, 0.0)
                t = dot(w.astype(BF), act_ref[keys, 512 + h * 128 : 512 + (h + 1) * 128])
                total = t if total is None else total + t
            att_ref[:, h * 128 : (h + 1) * 128] = total
        gated = (layer_norm(att_ref[...]) * act_ref[rows, :512].astype(F32)).astype(BF)
        hidden = (events_ref[rows, :].astype(F32) + dot(gated, w_ref[...])).astype(BF)
        hidden_ref[rows, :] = hidden
        pos = jnp.sum(hidden.astype(F32) * follow_ref[rows, :].astype(F32), axis=1, keepdims=True)
        positive_ref[:, rows] = jnp.sum(jnp.where(eye, pos, 0.0), axis=0, keepdims=True)

    hidden_out = pltpu.make_async_copy(hidden_ref, hidden_hbm, out_sem.at[0])
    hidden_out.start()
    outs = []
    for m in range(SLOTS // B):
        rows = slice(m * B, (m + 1) * B)
        send_ref[rows, :] = dot(onehot(m * B, B, slot_ref[0:1, :]), hidden_ref[...]).astype(BF)
        outs.append(pltpu.make_async_copy(send_ref.at[rows, :], send_hbm.at[rows, :], out_sem.at[1 + m]))
        outs[-1].start()
    hidden_out.wait()
    for copy in outs:
        copy.wait()


def loss_kernel(
    info_ref, hidden_ref, own_ref, other_ref, ids_ref, logc_ref, positive_ref, targets_ref, slot_ref,
    loss_ref, term_own_ref, term_other_ref, meta_ref, l_ref, probs_ref, coef_ref,
):
    core, length = info_ref[0], info_ref[1]
    own_cols = pl.ds(pl.multiple_of(core * B, B), B)
    other_cols = pl.ds(pl.multiple_of((1 - core) * B, B), B)
    chunks = [slice(m * B, (m + 1) * B) for m in range(SLOTS // B)]

    @pl.loop(0, 4)
    def _(t):
        at = pl.ds(pl.multiple_of(t * B, B), B)
        h_own = hidden_ref[at, own_cols]
        h_other = hidden_ref[at, other_cols]
        pos = positive_ref[:, at]
        target = targets_ref[:, at]
        top = pos
        for m in chunks:
            logc, ids = logc_ref[m, :], ids_ref[m, :]
            value = dot_nt(own_ref[m, :], h_own) + dot_nt(other_ref[m, :], h_other)
            value = value - jnp.concatenate([logc, logc], axis=1)
            value = jnp.where(jnp.concatenate([ids, ids], axis=1) != target, value, NEG_INF)
            l_ref[m, :] = value
            top = jnp.maximum(top, jnp.max(value, axis=0, keepdims=True))
        total = jnp.exp(pos - top)
        for m in chunks:
            total = total + jnp.sum(jnp.exp(l_ref[m, :] - top), axis=0, keepdims=True)
        log_total = top + jnp.log(total)
        in_range = iota((1, B), 1) + t * B < length - 1
        loss_ref[:, at] = jnp.where(in_range, log_total - pos, 0.0)
        coef_ref[:, at] = jnp.where(in_range, jnp.exp(pos - log_total) - 1.0, 0.0)
        shift = jnp.where(in_range, log_total, POS_INF)
        for m in chunks:
            probs_ref[m, at] = jnp.exp(l_ref[m, :] - shift).astype(BF)

    coef = coef_ref[...]
    high = coef.astype(BF).astype(F32)
    middle = (coef - high).astype(BF).astype(F32)
    low = coef - high - middle
    for k, piece in enumerate((high, middle, low)):
        meta_ref[k] = by_place(slot_ref[1:2, :], slot_ref[2:3, :], [piece], NCHIPS)
    for m in chunks:
        term_other_ref[m, :] = dot(probs_ref[m, :], hidden_ref[:, other_cols]).astype(BF)
        term_own_ref[m, :] = dot(probs_ref[m, :], hidden_ref[:, own_cols])


def order_kernel(key_ref, key_col_ref, rows_ref, sorted_ref, at_ref, sorted_key_ref, start_ref):
    n = key_ref.shape[1]
    key = key_ref[...]
    at = jnp.zeros((1, n), F32)
    for m in range(n // B):
        col = key_col_ref[m * B : (m + 1) * B, :]
        col = jnp.concatenate([col] * (n // 128), axis=1)
        at = at + jnp.sum((col < key).astype(F32), axis=0, keepdims=True)
    at = at.astype(I32)
    at_ref[...] = at
    row = key >> 11
    for i in range(ITEMS_DEV // TILE + 1):
        start_ref[i] = jnp.sum((row < i * TILE).astype(I32))
    sorted_key_ref[...] = by_place(at >> 7, at & 127, [row >> 6, row & 63], n // 128, (64.0, 1.0)).astype(I32)
    for m in range(n // B):
        block = slice(m * B, (m + 1) * B)
        sorted_ref[block, :] = dot(onehot(m * B, B, at), rows_ref[...]).astype(BF)


def place_kernel(
    start_ref, coef_ref, at_ref, key_ref, rows_ref, neg_index_ref, neg_ref, out_ref, scaled_ref, total_ref
):
    n = coef_ref.shape[1]
    i = pl.program_id(0)
    base = i * TILE

    @pl.when(i == 0)
    def _():
        coef = coef_ref[...]
        top = coef.astype(BF).astype(F32)
        middle = (coef - top).astype(BF).astype(F32)
        at = at_ref[...]
        coef = by_place(at >> 7, at & 127, [top, middle, coef - top - middle], n // 128)
        eye = iota((128, 128), 1) == iota((128, 128), 0)
        for m in range(n // 128):
            block = slice(m * 128, (m + 1) * 128)
            col = jnp.sum(jnp.where(eye, coef[m : m + 1, :], 0.0), axis=1, keepdims=True)
            scaled_ref[block, :] = (rows_ref[block, :].astype(F32) * col).astype(BF)

    total_ref[...] = dot(onehot(base, TILE, neg_index_ref[...]), neg_ref[...])

    @pl.loop(start_ref[i] // B, (start_ref[i + 1] + B - 1) // B)
    def _(j):
        block = pl.ds(pl.multiple_of(j * B, B), B)
        key = jnp.concatenate([key_ref[pl.ds(2 * j, 1), :], key_ref[pl.ds(2 * j + 1, 1), :]], axis=1)
        total_ref[...] += dot(onehot(base, TILE, key), scaled_ref[block, :])

    out_ref[...] = total_ref[...].astype(BF)


def swap(v):
    return lax.ppermute(v, "c", SWAP)


def chips_a2a(v):
    return lax.all_to_all(v, CHIPS, split_axis=0, concat_axis=0, tiled=True)


def per_device(events, lengths, target_ids, neg_ids, neg_counts, item_table, w_uvqk, w_out):
    width = 512
    core = lax.axis_index("c")
    chip = lax.axis_index(CHIPS)
    info = jnp.stack([core, lengths[0], chip]).astype(I32)
    ev = events[0]

    w_mine = jnp.concatenate([w_uvqk, w_out], axis=1)
    w_own = lax.all_to_all(
        jnp.broadcast_to(w_mine[None], (16,) + w_mine.shape), ("x", "z"), split_axis=0, concat_axis=0, tiled=True
    ).reshape(256, 2560)

    normed, ids, logc, target_slot, send_row, neg_local = call(
        prep_kernel,
        (
            jax.ShapeDtypeStruct((1024, width), BF),
            jax.ShapeDtypeStruct((SLOTS, 128), I32),
            jax.ShapeDtypeStruct((SLOTS, 128), F32),
            jax.ShapeDtypeStruct((3, 1024), I32),
            jax.ShapeDtypeStruct((2, NCHIPS, 128), F32),
            jax.ShapeDtypeStruct((32, 128), I32),
        ),
        [SMEM] + [VMEM] * 4,
        scratch=[pltpu.VMEM((1024, 1024), BF), pltpu.VMEM((2 * DEVS, 1024), BF), pltpu.VMEM((512, 512), BF)],
        vmem=16,
    )(info, ev, target_ids, neg_ids[None], neg_counts[None])

    neg_local = neg_local[:, 0]
    packed = jnp.where((neg_local >= 0)[:, None], item_table[jnp.maximum(neg_local, 0)], 0)
    packed_own = lax.dynamic_slice(packed, (0, core * B), (32, B))
    packed_other = lax.dynamic_slice(packed, (0, (1 - core) * B), (32, B))
    neg_block = call(
        neg_block_kernel, jax.ShapeDtypeStruct((NCHIPS, BLOCK, 128), BF), [VMEM] * 3, vmem=8
    )(packed_own, swap(packed_other), send_row)

    follow = jnp.concatenate([ev[1:], jnp.zeros((1, width), BF)], axis=0)
    w_own, normed, follow, neg_block = lax.optimization_barrier((w_own, normed, follow, neg_block))
    got_neg = chips_a2a(neg_block)
    w_other = swap(w_own)
    any_space = pl.BlockSpec(memory_space=pl.ANY)
    positive, hidden, send_rows = pl.pallas_call(
        layer_kernel,
        out_shape=(
            jax.ShapeDtypeStruct((1, 1024), F32),
            jax.ShapeDtypeStruct((1024, width), BF),
            jax.ShapeDtypeStruct((SLOTS, width), BF),
        ),
        in_specs=[SMEM, VMEM] + [any_space] * 5,
        out_specs=(VMEM, any_space, any_space),
        scratch_shapes=[
            pltpu.VMEM((512, 512), BF),
            pltpu.VMEM((256, 2560), BF),
            pltpu.VMEM((256, 2560), BF),
            pltpu.VMEM((1024, width), BF),
            pltpu.VMEM((1024, width), BF),
            pltpu.VMEM((1024, width), BF),
            pltpu.VMEM((1024, 2048), BF),
            pltpu.VMEM((B, width), F32),
            pltpu.VMEM((1024, width), BF),
            pltpu.VMEM((SLOTS, width), BF),
            pltpu.SemaphoreType.DMA((5,)),
            pltpu.SemaphoreType.DMA((7,)),
        ],
        cost_estimate=pl.CostEstimate(flops=0, bytes_accessed=0, transcendentals=0),
        compiler_params=pltpu.CompilerParams(vmem_limit_bytes=56 << 20),
    )(info, target_slot, w_own, normed, w_other, ev, follow)
    got_neg, send_rows = lax.optimization_barrier((got_neg, send_rows))
    other_neg = swap(got_neg)

    neg_own, neg_other, row_table = call(
        unpack_kernel,
        (
            jax.ShapeDtypeStruct((SLOTS, B), BF),
            jax.ShapeDtypeStruct((SLOTS, B), BF),
            jax.ShapeDtypeStruct((2, NCHIPS, 128), I32),
        ),
        [VMEM] * 2,
        vmem=16,
    )(got_neg, other_neg)

    recv_rows = chips_a2a(send_rows.reshape(NCHIPS, CSLOTS, width))

    loss, term_own, term_other, meta = call(
        loss_kernel,
        (
            jax.ShapeDtypeStruct((1, 1024), F32),
            jax.ShapeDtypeStruct((SLOTS, B), F32),
            jax.ShapeDtypeStruct((SLOTS, B), BF),
            jax.ShapeDtypeStruct((3, NCHIPS, 128), F32),
        ),
        [SMEM] + [VMEM] * 8,
        scratch=[
            pltpu.VMEM((SLOTS, B), F32),
            pltpu.VMEM((SLOTS, 1024), BF),
            pltpu.VMEM((1, 1024), F32),
        ],
        flops=0,
        nbytes=0,
        vmem=28,
    )(
        info, hidden, neg_own, neg_other, ids, logc, positive, target_ids, target_slot,
    )
    block = call(
        term_block_kernel, jax.ShapeDtypeStruct((NCHIPS, BLOCK, 128), BF), [VMEM] * 3, vmem=16
    )(term_own, swap(term_other), meta)
    recv_rows, block = lax.optimization_barrier((recv_rows, block))
    got = chips_a2a(block)

    def split(v):
        first, second, last = v[:, :8], v[:, 8:16], v[:, 16:]
        keep = jnp.where(core == 0, first, second)
        give = jnp.where(core == 0, second, first)
        return jnp.concatenate([keep, last], axis=1), jnp.concatenate([give, last], axis=1)

    rows_keep, rows_give = split(recv_rows)
    rows_got = swap(rows_give)
    rows = jnp.concatenate([rows_keep.reshape(-1, width), rows_got.reshape(-1, width)], axis=0)
    first, _ = split(row_table[0, :, :CSLOTS])
    second, _ = split(row_table[1, :, :CSLOTS])
    row_at = jnp.concatenate([first.reshape(-1), second.reshape(-1)]) - 1 - core * ITEMS_DEV
    row_at = jnp.where((row_at >= 0) & (row_at < ITEMS_DEV), row_at, 2 * ITEMS_DEV - 1)
    count = row_at.shape[0]
    key = row_at * count + jnp.arange(count, dtype=I32)
    rows, at, sorted_key, starts = pl.pallas_call(
        order_kernel,
        out_shape=(
            jax.ShapeDtypeStruct((count, width), BF),
            jax.ShapeDtypeStruct((1, count), I32),
            jax.ShapeDtypeStruct((count // 128, 128), I32),
            jax.ShapeDtypeStruct((32,), I32),
        ),
        in_specs=[VMEM] * 3,
        out_specs=(VMEM, VMEM, VMEM, SMEM),
        cost_estimate=pl.CostEstimate(flops=0, bytes_accessed=0, transcendentals=0),
        compiler_params=pltpu.CompilerParams(vmem_limit_bytes=24 << 20),
    )(key[None], jnp.broadcast_to(key[:, None], (count, 128)), rows)

    got, rows, at, sorted_key, starts = lax.optimization_barrier((got, rows, at, sorted_key, starts))
    summed = jnp.sum(got[:, : 2 * CSLOTS].astype(F32), axis=0)
    summed = jnp.concatenate([summed[:CSLOTS], summed[CSLOTS:]], axis=1)
    got_coef = jnp.sum(got[:, 2 * CSLOTS : 2 * CSLOTS + 3, :CSLOTS].astype(F32), axis=1)
    coef_keep, coef_give = split(got_coef)
    small = swap(jnp.concatenate([summed, coef_give.reshape(4, B)], axis=0))
    summed_got = small[:CSLOTS]
    coef_all = jnp.concatenate([coef_keep.reshape(-1), small[CSLOTS:].reshape(-1)])

    neg_sum = jnp.where(
        core == 0,
        jnp.concatenate([summed, summed_got], axis=1),
        jnp.concatenate([summed_got, summed], axis=1),
    )
    neg_high = neg_sum.astype(BF)
    neg_low = (neg_sum - neg_high.astype(F32)).astype(BF)
    rest = 128 - 2 * CSLOTS
    neg_rows = jnp.concatenate([neg_high, neg_low, jnp.zeros((rest, width), BF)], axis=0)
    neg_at = jnp.concatenate([neg_local[:CSLOTS], neg_local[:CSLOTS], jnp.full((rest,), -1, I32)])

    whole = lambda shape: pl.BlockSpec(shape, lambda i: (0, 0))
    grad = pl.pallas_call(
        place_kernel,
        grid=(ITEMS_DEV // TILE,),
        out_shape=jax.ShapeDtypeStruct((ITEMS_DEV, width), BF),
        in_specs=[SMEM] + [whole((1, count))] * 2 + [whole((count // 128, 128)), whole((count, width)), whole((1, 128)), whole((128, width))],
        out_specs=pl.BlockSpec((TILE, width), lambda i: (i, 0)),
        scratch_shapes=[pltpu.VMEM((count, width), BF), pltpu.VMEM((TILE, width), F32)],
        cost_estimate=pl.CostEstimate(flops=0, bytes_accessed=0, transcendentals=0),
        compiler_params=pltpu.CompilerParams(vmem_limit_bytes=24 << 20),
    )(starts, coef_all[None], at, sorted_key, rows, neg_at[None], neg_rows)
    return loss, grad


def solution(mesh):
    fine = Mesh(mesh.devices.reshape(4, 4, 4, 2), ALL)
    in_specs = (P(ALL), P(ALL), P(ALL), P(), P(), P(ALL), P(MP), P(MP))
    return jax.shard_map(
        per_device, mesh=fine, in_specs=in_specs, out_specs=(P(ALL), P(ALL)), check_vma=False
    )
```

```python
import math

import jax
import jax.numpy as jnp
from jax import lax
from jax.experimental import pallas as pl
from jax.experimental.pallas import tpu as pltpu
from jax.sharding import Mesh, PartitionSpec as P

H = 4
EPSILON = 1e-05
ALL = ("y", "x", "z", "c")
CHIPS = ("y", "x", "z")
MP = ("x", "z", "c")
BF = jnp.bfloat16
F32 = jnp.float32
I32 = jnp.int32
DEVS = 128
NCHIPS = 64
CSLOTS = 24
SLOTS = NCHIPS * CSLOTS
BLOCK = 2 * CSLOTS + 8
PLACES = 2048
GROUP = 8
ITEMS_DEV = 4096
B = 256
TILE = 512
VMEM = pl.BlockSpec(memory_space=pltpu.VMEM)
SMEM = pl.BlockSpec(memory_space=pltpu.SMEM)
NT = (((1,), (1,)), ((), ()))
NEG_INF = float("-inf")
POS_INF = float("inf")
SWAP = ((0, 1), (1, 0))


def dot(a, b):
    return jnp.dot(a, b, preferred_element_type=F32)


def dot_nt(a, b):
    return lax.dot_general(a, b, NT, preferred_element_type=F32)


def iota(shape, dim):
    return lax.broadcasted_iota(I32, shape, dim)


def layer_norm(values):
    center = values - jnp.mean(values, axis=-1, keepdims=True)
    spread = jnp.mean(center * center, axis=-1, keepdims=True)
    return center * lax.rsqrt(spread + EPSILON)


def call(body, out_shape, in_specs, scratch=(), flops=0, nbytes=0, vmem=56):
    return pl.pallas_call(
        body,
        out_shape=out_shape,
        in_specs=in_specs,
        out_specs=jax.tree.map(lambda _: VMEM, out_shape),
        scratch_shapes=list(scratch),
        cost_estimate=pl.CostEstimate(flops=flops, bytes_accessed=nbytes, transcendentals=0),
        compiler_params=pltpu.CompilerParams(vmem_limit_bytes=vmem << 20),
    )


def onehot(base, count, index):
    return (iota((count, index.shape[1]), 0) + base == index).astype(F32).astype(BF)


def by_place(high, low, pieces, count, weights=(1.0, 1.0, 1.0)):
    rows = iota((count, high.shape[1]), 0) == high
    cols = onehot(0, 128, low)
    return sum(
        w * dot_nt(jnp.where(rows, p.astype(F32), 0.0).astype(BF), cols) for p, w in zip(pieces, weights)
    )


def prep_kernel(
    info_ref, events_ref, targets_ref, negs_ref, counts_ref,
    normed_ref, ids_ref, logc_ref, slot_ref, row_ref, local_ref, tri_ref, owner_ref, order_ref,
):
    core, chip = info_ref[0], info_ref[2]
    targets, negs = targets_ref[...], negs_ref[...]
    n = targets.shape[1]

    for k in range(4):
        rows = slice(k * B, (k + 1) * B)
        tri_ref[rows, :] = (iota((B, n), 0) + k * B < iota((B, n), 1)).astype(F32).astype(BF)
    t_owner, n_owner = targets >> 12, negs >> 12
    owner_ref[:DEVS, :] = onehot(0, DEVS, t_owner)
    owner_ref[DEVS:, :] = onehot(0, DEVS, n_owner)
    before = dot(owner_ref[...], tri_ref[...]) * owner_ref[...].astype(F32)
    t_rank = jnp.sum(before[:DEVS], axis=0, keepdims=True).astype(I32)
    n_rank = jnp.sum(before[DEVS:], axis=0, keepdims=True).astype(I32)

    def within(owner, rank):
        return jnp.where(rank < 8, (owner & 1) * 8 + rank, 8 + rank)

    t_within = within(t_owner, t_rank)
    slot_ref[0:1, :] = (t_owner >> 1) * CSLOTS + t_within
    slot_ref[1:2, :] = t_owner >> 1
    slot_ref[2:3, :] = t_within
    n_slot = (n_owner >> 1) * CSLOTS + within(n_owner, n_rank)
    row = (targets & (2 * ITEMS_DEV - 1)) + 1
    row_ref[0] = by_place(t_owner >> 1, t_within, [row >> 6], NCHIPS)
    row_ref[1] = by_place(t_owner >> 1, t_within, [row & 63], NCHIPS)

    mine = (iota((32, n), 0) + chip * CSLOTS == n_slot) & ((n_owner & 1) == core)
    mine = mine & (iota((32, n), 0) < CSLOTS)
    local = jnp.max(jnp.where(mine, negs & (ITEMS_DEV - 1), -1), axis=1, keepdims=True)
    local_ref[...] = jnp.broadcast_to(local, (32, 128))
    logs = jnp.log(counts_ref[...].astype(F32))
    for m in range(SLOTS // B):
        rows = slice(m * B, (m + 1) * B)
        here = iota((B, n), 0) + m * B == n_slot
        ids = jnp.max(jnp.where(here, negs, -1), axis=1, keepdims=True)
        logc = jnp.min(jnp.where(here, logs, POS_INF), axis=1, keepdims=True)
        ids_ref[rows, :] = jnp.broadcast_to(ids, (B, 128))
        logc_ref[rows, :] = jnp.broadcast_to(logc, (B, 128))

    k = iota((512, 512), 1)
    source = ((k & 255) >> 4) * 32 + jnp.where(k < 256, core, 1 - core) * 16 + (k & 15)
    order_ref[...] = (iota((512, 512), 0) == source).astype(F32).astype(BF)

    @pl.loop(0, 4)
    def _(i):
        rows = pl.ds(pl.multiple_of(i * B, B), B)
        normed = layer_norm(events_ref[rows, :].astype(F32)).astype(BF)
        normed_ref[rows, :] = dot(normed, order_ref[...]).astype(BF)


def block_of(rows, pieces):
    chips = rows.shape[0]
    pieces = [p[:, None, :] for p in pieces] + [jnp.zeros((chips, 8 - len(pieces), 128), F32)]
    return jnp.concatenate([rows[:, :, :128], rows[:, :, 128:]] + pieces, axis=1).astype(BF)


def neg_block_kernel(mine_ref, other_ref, row_ref, out_ref):
    rows = mine_ref[...].astype(F32) + other_ref[...].astype(F32)
    rows = jnp.broadcast_to(rows[None, :CSLOTS], (GROUP, CSLOTS, B))
    for g in range(NCHIPS // GROUP):
        chips = slice(g * GROUP, (g + 1) * GROUP)
        out_ref[chips] = block_of(rows, [row_ref[0, chips, :], row_ref[1, chips, :]])


def term_block_kernel(own_ref, other_ref, meta_ref, out_ref):
    for g in range(NCHIPS // GROUP):
        chips = slice(g * GROUP, (g + 1) * GROUP)
        slots = slice(g * GROUP * CSLOTS, (g + 1) * GROUP * CSLOTS)
        rows = (own_ref[slots, :] + other_ref[slots, :].astype(F32)).reshape(GROUP, CSLOTS, B)
        out_ref[chips] = block_of(rows, [meta_ref[k, chips, :] for k in range(3)])


def unpack_kernel(own_ref, other_ref, own_out_ref, other_out_ref, row_ref):
    for k, (block_ref, out_ref) in enumerate(((own_ref, own_out_ref), (other_ref, other_out_ref))):
        for g in range(NCHIPS // GROUP):
            chips = slice(g * GROUP, (g + 1) * GROUP)
            block = block_ref[chips].astype(F32)
            halves = [
                block[:, h * CSLOTS : (h + 1) * CSLOTS].reshape(GROUP * CSLOTS, 128) for h in range(2)
            ]
            slots = slice(g * GROUP * CSLOTS, (g + 1) * GROUP * CSLOTS)
            out_ref[slots, :] = jnp.concatenate(halves, axis=1).astype(BF)
            numbers = block[:, 2 * CSLOTS :]
            row_ref[k, chips, :] = (numbers[:, 0] * 64.0 + numbers[:, 1]).astype(I32)


def silu_of_half(h):
    return h + h * jnp.tanh(h)


def layer_kernel(
    info_ref, slot_ref, own_hbm, normed_hbm, other_hbm, events_hbm, follow_hbm,
    positive_ref, hidden_hbm, send_hbm,
    w_ref, own_ref, other_ref, normed_ref, events_ref, follow_ref, act_ref, att_ref, hidden_ref, send_ref, in_sem, out_sem,
):
    core, length = info_ref[0], info_ref[1]
    pairs = (
        (normed_hbm, normed_ref), (own_hbm, own_ref), (other_hbm, other_ref),
        (events_hbm, events_ref), (follow_hbm, follow_ref),
    )
    inputs = [pltpu.make_async_copy(source, to, in_sem.at[k]) for k, (source, to) in enumerate(pairs)]
    for copy in inputs:
        copy.start()
    for copy in inputs[:3]:
        copy.wait()

    @pl.loop(0, 4)
    def _(i):
        rows = pl.ds(pl.multiple_of(i * B, B), B)
        a = normed_ref[rows, :B]
        b = normed_ref[rows, B:]
        live = iota((B, 512), 0) + i * B < length
        for n in range(4):
            cols = slice(n * 512, (n + 1) * 512)
            v = silu_of_half(0.5 * (dot(a, own_ref[:, cols]) + dot(b, other_ref[:, cols])))
            if n == 1:
                v = jnp.where(live, v, 0.0)
            act_ref[rows, cols] = v.astype(BF)

    for b in range(16):
        block = slice(b * 16, (b + 1) * 16)
        w_ref[pl.ds(pl.multiple_of(b * 32 + core * 16, 16), 16), :] = own_ref[block, 2048:]
        w_ref[pl.ds(pl.multiple_of(b * 32 + (1 - core) * 16, 16), 16), :] = other_ref[block, 2048:]
    for copy in inputs[3:]:
        copy.wait()
    causal = iota((B, B), 1) <= iota((B, B), 0)
    eye = iota((B, B), 1) == iota((B, B), 0)
    scale = 0.5 / math.sqrt(128)
    for i in range(4):
        rows = slice(i * B, (i + 1) * B)
        for h in range(H):
            q = act_ref[rows, 1024 + h * 128 : 1024 + (h + 1) * 128]
            total = None
            for j in range(i + 1):
                keys = slice(j * B, (j + 1) * B)
                s = dot_nt(q, act_ref[keys, 1536 + h * 128 : 1536 + (h + 1) * 128])
                w = silu_of_half(s * scale)
                if j == i:
                    w = jnp.where(causal, w, 0.0)
                t = dot(w.astype(BF), act_ref[keys, 512 + h * 128 : 512 + (h + 1) * 128])
                total = t if total is None else total + t
            att_ref[:, h * 128 : (h + 1) * 128] = total
        gated = (layer_norm(att_ref[...]) * act_ref[rows, :512].astype(F32)).astype(BF)
        hidden = (events_ref[rows, :].astype(F32) + dot(gated, w_ref[...])).astype(BF)
        hidden_ref[rows, :] = hidden
        pos = jnp.sum(hidden.astype(F32) * follow_ref[rows, :].astype(F32), axis=1, keepdims=True)
        positive_ref[:, rows] = jnp.sum(jnp.where(eye, pos, 0.0), axis=0, keepdims=True)

    hidden_out = pltpu.make_async_copy(hidden_ref, hidden_hbm, out_sem.at[0])
    hidden_out.start()
    outs = []
    for m in range(SLOTS // B):
        rows = slice(m * B, (m + 1) * B)
        send_ref[rows, :] = dot(onehot(m * B, B, slot_ref[0:1, :]), hidden_ref[...]).astype(BF)
        outs.append(pltpu.make_async_copy(send_ref.at[rows, :], send_hbm.at[rows, :], out_sem.at[1 + m]))
        outs[-1].start()
    hidden_out.wait()
    for copy in outs:
        copy.wait()


def loss_kernel(
    info_ref, hidden_ref, own_ref, other_ref, ids_ref, logc_ref, positive_ref, targets_ref, slot_ref,
    loss_ref, term_own_ref, term_other_ref, meta_ref, l_ref, probs_ref, coef_ref,
):
    core, length = info_ref[0], info_ref[1]
    own_cols = pl.ds(pl.multiple_of(core * B, B), B)
    other_cols = pl.ds(pl.multiple_of((1 - core) * B, B), B)
    chunks = [slice(m * B, (m + 1) * B) for m in range(SLOTS // B)]

    @pl.loop(0, 4)
    def _(t):
        at = pl.ds(pl.multiple_of(t * B, B), B)
        h_own = hidden_ref[at, own_cols]
        h_other = hidden_ref[at, other_cols]
        pos = positive_ref[:, at]
        target = targets_ref[:, at]
        top = pos
        for m in chunks:
            logc, ids = logc_ref[m, :], ids_ref[m, :]
            value = dot_nt(own_ref[m, :], h_own) + dot_nt(other_ref[m, :], h_other)
            value = value - jnp.concatenate([logc, logc], axis=1)
            value = jnp.where(jnp.concatenate([ids, ids], axis=1) != target, value, NEG_INF)
            l_ref[m, :] = value
            top = jnp.maximum(top, jnp.max(value, axis=0, keepdims=True))
        total = jnp.exp(pos - top)
        for m in chunks:
            total = total + jnp.sum(jnp.exp(l_ref[m, :] - top), axis=0, keepdims=True)
        log_total = top + jnp.log(total)
        in_range = iota((1, B), 1) + t * B < length - 1
        loss_ref[:, at] = jnp.where(in_range, log_total - pos, 0.0)
        coef_ref[:, at] = jnp.where(in_range, jnp.exp(pos - log_total) - 1.0, 0.0)
        shift = jnp.where(in_range, log_total, POS_INF)
        for m in chunks:
            probs_ref[m, at] = jnp.exp(l_ref[m, :] - shift).astype(BF)

    coef = coef_ref[...]
    high = coef.astype(BF).astype(F32)
    middle = (coef - high).astype(BF).astype(F32)
    low = coef - high - middle
    for k, piece in enumerate((high, middle, low)):
        meta_ref[k] = by_place(slot_ref[1:2, :], slot_ref[2:3, :], [piece], NCHIPS)
    for m in chunks:
        term_other_ref[m, :] = dot(probs_ref[m, :], hidden_ref[:, other_cols]).astype(BF)
        term_own_ref[m, :] = dot(probs_ref[m, :], hidden_ref[:, own_cols])


def rank_kernel(info_ref, row_ref, neg_ref, at_ref, sorted_key_ref, start_ref, neg_at_ref):
    core = info_ref[0]
    row = row_ref[...] - 1 - core * ITEMS_DEV
    row = jnp.where((row >= 0) & (row < ITEMS_DEV), row, 2 * ITEMS_DEV - 1)
    n = row.shape[1]
    key = row * 4096 + iota((1, n), 1)
    eye = iota((128, 128), 1) == iota((128, 128), 0)
    at = jnp.zeros((1, n), F32)
    for m in range(n // 128):
        col = jnp.sum(jnp.where(eye, key[:, m * 128 : (m + 1) * 128], 0), axis=1, keepdims=True)
        at = at + jnp.sum((col < key).astype(F32), axis=0, keepdims=True)
    at = at.astype(I32)
    at_ref[...] = at
    for i in range(ITEMS_DEV // TILE + 1):
        start_ref[i] = jnp.sum((row < i * TILE).astype(I32))
    start_ref[31] = core
    neg = neg_ref[:, :1]
    neg = jnp.where(neg < 0, 2 * ITEMS_DEV, neg) * 64 + iota((32, 1), 0)
    small_eye = iota((32, 32), 1) == iota((32, 32), 0)
    neg_row = jnp.sum(jnp.where(small_eye, neg, 0), axis=0, keepdims=True)
    neg_rank = jnp.sum((neg < neg_row).astype(I32), axis=0, keepdims=True)
    for p in range(16):
        found = jnp.sum(jnp.where(neg_rank == p, neg_row, 0))
        neg_at_ref[p] = found & 63
        neg_at_ref[16 + p] = found >> 6
    for i in range(ITEMS_DEV // TILE + 1):
        neg_at_ref[32 + i] = jnp.sum(((neg_row >> 6) < i * TILE).astype(I32))
    sorted_key_ref[...] = by_place(at >> 7, at & 127, [row >> 6, row & 63], PLACES // 128, (64.0, 1.0)).astype(I32)


def sort_kernel(at_ref, own_ref, other_ref, sorted_ref):
    for m in range(PLACES // B):
        block = slice(m * B, (m + 1) * B)
        sorted_ref[block, :] = (
            dot(onehot(m * B, B, at_ref[:, :SLOTS]), own_ref[...])
            + dot(onehot(m * B, B, at_ref[:, SLOTS:]), other_ref[...])
        ).astype(BF)


def collect_kernel(got_ref, small_ref):
    total = jnp.zeros((2 * CSLOTS, 128), F32)
    for g in range(NCHIPS // GROUP):
        block = got_ref[g * GROUP : (g + 1) * GROUP].astype(F32)
        total = total + jnp.sum(block[:, : 2 * CSLOTS], axis=0)
    small_ref[:CSLOTS, :] = jnp.concatenate([total[:CSLOTS], total[CSLOTS:]], axis=1)
    k = iota((1, SLOTS), 1)
    chip = ((k.astype(F32) + 0.5) * (1.0 / CSLOTS)).astype(I32)
    spread = (iota((128, SLOTS), 0) == k - chip * CSLOTS).astype(F32).astype(BF)
    mine = iota((NCHIPS, SLOTS), 0) == chip
    row = jnp.zeros((1, SLOTS), F32)
    for p in range(3):
        piece = got_ref[:, 2 * CSLOTS + p, :]
        row = row + jnp.sum(jnp.where(mine, dot(piece, spread), 0.0), axis=0, keepdims=True)
    for r in range(SLOTS // B):
        small_ref[CSLOTS + r : CSLOTS + r + 1, :] = row[:, r * B : (r + 1) * B]
    small_ref[CSLOTS + SLOTS // B :, :] = jnp.zeros((8 - SLOTS // B, B), F32)


def place_kernel(
    start_ref, neg_at_ref, small_ref, small_other_ref, at_ref, key_ref, rows_ref, out_hbm,
    scaled_ref, neg_ref, total_ref, out_ref, sems,
):
    coef = jnp.concatenate(
        [ref[CSLOTS + r : CSLOTS + r + 1, :] for ref in (small_ref, small_other_ref) for r in range(SLOTS // B)],
        axis=1,
    )
    top = coef.astype(BF).astype(F32)
    middle = (coef - top).astype(BF).astype(F32)
    at = at_ref[...]
    coef = by_place(at >> 7, at & 127, [top, middle, coef - top - middle], PLACES // 128)
    eye = iota((128, 128), 1) == iota((128, 128), 0)
    for m in range(PLACES // 128):
        block = slice(m * 128, (m + 1) * 128)
        col = jnp.sum(jnp.where(eye, coef[m : m + 1, :], 0.0), axis=1, keepdims=True)
        scaled_ref[block, :] = (rows_ref[block, :].astype(F32) * col).astype(BF)
    own, other = small_ref[:CSLOTS, :], small_other_ref[:CSLOTS, :]
    first = start_ref[31] == 0
    neg_ref[...] = jnp.concatenate([jnp.where(first, own, other), jnp.where(first, other, own)], axis=1)

    def part(base, j):
        block = pl.ds(pl.multiple_of(j * B, B), B)
        key = jnp.concatenate([key_ref[pl.ds(2 * j, 1), :], key_ref[pl.ds(2 * j + 1, 1), :]], axis=1)
        return dot(onehot(base, TILE, key), scaled_ref[block, :])

    copies = []
    for i in range(ITEMS_DEV // TILE):
        base = i * TILE
        tile = slice(base, base + TILE)
        first = jnp.minimum(start_ref[i] // B, PLACES // B - 1)
        total_ref[...] = part(base, first)

        @pl.loop(first + 1, (start_ref[i + 1] + B - 1) // B)
        def _(j):
            total_ref[...] += part(base, j)

        @pl.loop(neg_at_ref[32 + i], neg_at_ref[33 + i])
        def _(p):
            total_ref[pl.ds(neg_at_ref[16 + p] - base, 1), :] += neg_ref[pl.ds(neg_at_ref[p], 1), :]

        out_ref[tile, :] = total_ref[...].astype(BF)
        copies.append(pltpu.make_async_copy(out_ref.at[tile, :], out_hbm.at[tile, :], sems.at[i]))
        copies[-1].start()
    for copy in copies:
        copy.wait()


def swap(v):
    return lax.ppermute(v, "c", SWAP)


def chips_a2a(v):
    return lax.all_to_all(v, CHIPS, split_axis=0, concat_axis=0, tiled=True)


def per_device(events, lengths, target_ids, neg_ids, neg_counts, item_table, w_uvqk, w_out):
    width = 512
    core = lax.axis_index("c")
    chip = lax.axis_index(CHIPS)
    info = jnp.stack([core, lengths[0], chip]).astype(I32)
    ev = events[0]

    w_mine = jnp.concatenate([w_uvqk, w_out], axis=1)
    w_own = lax.all_to_all(
        jnp.broadcast_to(w_mine[None], (16,) + w_mine.shape), ("x", "z"), split_axis=0, concat_axis=0, tiled=True
    ).reshape(256, 2560)

    normed, ids, logc, target_slot, send_row, neg_table = call(
        prep_kernel,
        (
            jax.ShapeDtypeStruct((1024, width), BF),
            jax.ShapeDtypeStruct((SLOTS, 128), I32),
            jax.ShapeDtypeStruct((SLOTS, 128), F32),
            jax.ShapeDtypeStruct((3, 1024), I32),
            jax.ShapeDtypeStruct((2, NCHIPS, 128), F32),
            jax.ShapeDtypeStruct((32, 128), I32),
        ),
        [SMEM] + [VMEM] * 4,
        scratch=[pltpu.VMEM((1024, 1024), BF), pltpu.VMEM((2 * DEVS, 1024), BF), pltpu.VMEM((512, 512), BF)],
        vmem=16,
    )(info, ev, target_ids, neg_ids[None], neg_counts[None])

    neg_local = neg_table[:, 0]
    packed = jnp.where((neg_local >= 0)[:, None], item_table[jnp.maximum(neg_local, 0)], 0)
    packed_own = lax.dynamic_slice(packed, (0, core * B), (32, B))
    packed_other = lax.dynamic_slice(packed, (0, (1 - core) * B), (32, B))
    neg_block = call(
        neg_block_kernel, jax.ShapeDtypeStruct((NCHIPS, BLOCK, 128), BF), [VMEM] * 3, vmem=8
    )(packed_own, swap(packed_other), send_row)

    follow = jnp.concatenate([ev[1:], jnp.zeros((1, width), BF)], axis=0)
    w_own, normed, follow, neg_block = lax.optimization_barrier((w_own, normed, follow, neg_block))
    got_neg = chips_a2a(neg_block)
    w_other = swap(w_own)
    any_space = pl.BlockSpec(memory_space=pl.ANY)
    positive, hidden, send_rows = pl.pallas_call(
        layer_kernel,
        out_shape=(
            jax.ShapeDtypeStruct((1, 1024), F32),
            jax.ShapeDtypeStruct((1024, width), BF),
            jax.ShapeDtypeStruct((SLOTS, width), BF),
        ),
        in_specs=[SMEM, VMEM] + [any_space] * 5,
        out_specs=(VMEM, any_space, any_space),
        scratch_shapes=[
            pltpu.VMEM((512, 512), BF),
            pltpu.VMEM((256, 2560), BF),
            pltpu.VMEM((256, 2560), BF),
            pltpu.VMEM((1024, width), BF),
            pltpu.VMEM((1024, width), BF),
            pltpu.VMEM((1024, width), BF),
            pltpu.VMEM((1024, 2048), BF),
            pltpu.VMEM((B, width), F32),
            pltpu.VMEM((1024, width), BF),
            pltpu.VMEM((SLOTS, width), BF),
            pltpu.SemaphoreType.DMA((5,)),
            pltpu.SemaphoreType.DMA((7,)),
        ],
        cost_estimate=pl.CostEstimate(flops=0, bytes_accessed=0, transcendentals=0),
        compiler_params=pltpu.CompilerParams(vmem_limit_bytes=56 << 20),
    )(info, target_slot, w_own, normed, w_other, ev, follow)
    got_neg, send_rows = lax.optimization_barrier((got_neg, send_rows))
    other_neg = swap(got_neg)

    neg_own, neg_other, row_table = call(
        unpack_kernel,
        (
            jax.ShapeDtypeStruct((SLOTS, B), BF),
            jax.ShapeDtypeStruct((SLOTS, B), BF),
            jax.ShapeDtypeStruct((2, NCHIPS, 128), I32),
        ),
        [VMEM] * 2,
        vmem=16,
    )(got_neg, other_neg)

    recv_rows = chips_a2a(send_rows.reshape(NCHIPS, CSLOTS, width)).reshape(SLOTS, width)

    loss, term_own, term_other, meta = call(
        loss_kernel,
        (
            jax.ShapeDtypeStruct((1, 1024), F32),
            jax.ShapeDtypeStruct((SLOTS, B), F32),
            jax.ShapeDtypeStruct((SLOTS, B), BF),
            jax.ShapeDtypeStruct((3, NCHIPS, 128), F32),
        ),
        [SMEM] + [VMEM] * 8,
        scratch=[
            pltpu.VMEM((SLOTS, B), F32),
            pltpu.VMEM((SLOTS, 1024), BF),
            pltpu.VMEM((1, 1024), F32),
        ],
        flops=0,
        nbytes=0,
        vmem=28,
    )(
        info, hidden, neg_own, neg_other, ids, logc, positive, target_ids, target_slot,
    )
    block = call(
        term_block_kernel, jax.ShapeDtypeStruct((NCHIPS, BLOCK, 128), BF), [VMEM] * 3, vmem=16
    )(term_own, swap(term_other), meta)
    recv_rows, block = lax.optimization_barrier((recv_rows, block))
    got = chips_a2a(block)

    recv_other = swap(recv_rows)
    at, sorted_key, starts, neg_at = pl.pallas_call(
        rank_kernel,
        out_shape=(
            jax.ShapeDtypeStruct((1, 2 * SLOTS), I32),
            jax.ShapeDtypeStruct((PLACES // 128, 128), I32),
            jax.ShapeDtypeStruct((32,), I32),
            jax.ShapeDtypeStruct((48,), I32),
        ),
        in_specs=[SMEM, VMEM, VMEM],
        out_specs=(VMEM, VMEM, SMEM, SMEM),
        cost_estimate=pl.CostEstimate(flops=0, bytes_accessed=0, transcendentals=0),
        compiler_params=pltpu.CompilerParams(vmem_limit_bytes=16 << 20),
    )(info, row_table[:, :, :CSLOTS].reshape(1, 2 * SLOTS), neg_table)
    rows = call(sort_kernel, jax.ShapeDtypeStruct((PLACES, width), BF), [VMEM] * 3, vmem=24)(
        at, recv_rows, recv_other
    )

    got, rows = lax.optimization_barrier((got, rows))
    small = call(collect_kernel, jax.ShapeDtypeStruct((32, B), F32), [VMEM], vmem=8)(got)
    small_other = swap(small)
    tiles = ITEMS_DEV // TILE
    grad = pl.pallas_call(
        place_kernel,
        out_shape=jax.ShapeDtypeStruct((ITEMS_DEV, width), BF),
        in_specs=[SMEM] * 2 + [VMEM] * 5,
        out_specs=pl.BlockSpec(memory_space=pl.ANY),
        scratch_shapes=[
            pltpu.VMEM((PLACES, width), BF),
            pltpu.VMEM((CSLOTS, width), F32),
            pltpu.VMEM((TILE, width), F32),
            pltpu.VMEM((ITEMS_DEV, width), BF),
            pltpu.SemaphoreType.DMA((tiles,)),
        ],
        cost_estimate=pl.CostEstimate(flops=0, bytes_accessed=0, transcendentals=0),
        compiler_params=pltpu.CompilerParams(vmem_limit_bytes=24 << 20),
    )(starts, neg_at, small, small_other, at, sorted_key, rows)
    return loss, grad


def solution(mesh):
    fine = Mesh(mesh.devices.reshape(4, 4, 4, 2), ALL)
    in_specs = (P(ALL), P(ALL), P(ALL), P(), P(), P(ALL), P(MP), P(MP))
    return jax.shard_map(
        per_device, mesh=fine, in_specs=in_specs, out_specs=(P(ALL), P(ALL)), check_vma=False
    )
```

```python
import math

import jax
import jax.numpy as jnp
from jax import lax
from jax.experimental import pallas as pl
from jax.experimental.pallas import tpu as pltpu
from jax.sharding import Mesh, PartitionSpec as P

H = 4
EPSILON = 1e-05
ALL = ("y", "x", "z", "c")
CHIPS = ("y", "x", "z")
MP = ("x", "z", "c")
BF = jnp.bfloat16
F32 = jnp.float32
I32 = jnp.int32
DEVS = 128
NCHIPS = 64
CSLOTS = 24
SLOTS = NCHIPS * CSLOTS
BLOCK = 2 * CSLOTS + 8
PLACES = 2048
GROUP = 8
ITEMS_DEV = 4096
B = 256
TILE = 512
VMEM = pl.BlockSpec(memory_space=pltpu.VMEM)
SMEM = pl.BlockSpec(memory_space=pltpu.SMEM)
NT = (((1,), (1,)), ((), ()))
NEG_INF = float("-inf")
POS_INF = float("inf")
SWAP = ((0, 1), (1, 0))


def dot(a, b):
    return jnp.dot(a, b, preferred_element_type=F32)


def dot_nt(a, b):
    return lax.dot_general(a, b, NT, preferred_element_type=F32)


def iota(shape, dim):
    return lax.broadcasted_iota(I32, shape, dim)


def layer_norm(values):
    center = values - jnp.mean(values, axis=-1, keepdims=True)
    spread = jnp.mean(center * center, axis=-1, keepdims=True)
    return center * lax.rsqrt(spread + EPSILON)


def call(body, out_shape, in_specs, scratch=(), flops=0, nbytes=0, vmem=56):
    return pl.pallas_call(
        body,
        out_shape=out_shape,
        in_specs=in_specs,
        out_specs=jax.tree.map(lambda _: VMEM, out_shape),
        scratch_shapes=list(scratch),
        cost_estimate=pl.CostEstimate(flops=flops, bytes_accessed=nbytes, transcendentals=0),
        compiler_params=pltpu.CompilerParams(vmem_limit_bytes=vmem << 20),
    )


def onehot(base, count, index):
    return (iota((count, index.shape[1]), 0) + base == index).astype(F32).astype(BF)


def by_place(high, low, pieces, count, weights=(1.0, 1.0, 1.0)):
    rows = iota((count, high.shape[1]), 0) == high
    cols = onehot(0, 128, low)
    return sum(
        w * dot_nt(jnp.where(rows, p.astype(F32), 0.0).astype(BF), cols) for p, w in zip(pieces, weights)
    )


def prep_kernel(
    info_ref, events_ref, targets_ref, negs_ref, counts_ref,
    normed_ref, ids_ref, logc_ref, slot_ref, row_ref, local_ref, tri_ref, owner_ref, order_ref,
):
    core, chip = info_ref[0], info_ref[2]
    targets, negs = targets_ref[...], negs_ref[...]
    n = targets.shape[1]

    for k in range(4):
        rows = slice(k * B, (k + 1) * B)
        tri_ref[rows, :] = (iota((B, n), 0) + k * B < iota((B, n), 1)).astype(F32).astype(BF)
    t_owner, n_owner = targets >> 12, negs >> 12
    owner_ref[:DEVS, :] = onehot(0, DEVS, t_owner)
    owner_ref[DEVS:, :] = onehot(0, DEVS, n_owner)
    before = dot(owner_ref[...], tri_ref[...]) * owner_ref[...].astype(F32)
    t_rank = jnp.sum(before[:DEVS], axis=0, keepdims=True).astype(I32)
    n_rank = jnp.sum(before[DEVS:], axis=0, keepdims=True).astype(I32)

    def within(owner, rank):
        return jnp.where(rank < 8, (owner & 1) * 8 + rank, 8 + rank)

    t_within = within(t_owner, t_rank)
    slot_ref[0:1, :] = (t_owner >> 1) * CSLOTS + t_within
    slot_ref[1:2, :] = t_owner >> 1
    slot_ref[2:3, :] = t_within
    n_slot = (n_owner >> 1) * CSLOTS + within(n_owner, n_rank)
    row = (targets & (2 * ITEMS_DEV - 1)) + 1
    row_ref[0] = by_place(t_owner >> 1, t_within, [row >> 6], NCHIPS)
    row_ref[1] = by_place(t_owner >> 1, t_within, [row & 63], NCHIPS)

    mine = (iota((32, n), 0) + chip * CSLOTS == n_slot) & ((n_owner & 1) == core)
    mine = mine & (iota((32, n), 0) < CSLOTS)
    local = jnp.max(jnp.where(mine, negs & (ITEMS_DEV - 1), -1), axis=1, keepdims=True)
    local_ref[...] = jnp.broadcast_to(local, (32, 128))
    logs = jnp.log(counts_ref[...].astype(F32))
    for m in range(SLOTS // B):
        rows = slice(m * B, (m + 1) * B)
        here = iota((B, n), 0) + m * B == n_slot
        ids = jnp.max(jnp.where(here, negs, -1), axis=1, keepdims=True)
        logc = jnp.min(jnp.where(here, logs, POS_INF), axis=1, keepdims=True)
        ids_ref[rows, :] = jnp.broadcast_to(ids, (B, 128))
        logc_ref[rows, :] = jnp.broadcast_to(logc, (B, 128))

    k = iota((512, 512), 1)
    source = ((k & 255) >> 4) * 32 + jnp.where(k < 256, core, 1 - core) * 16 + (k & 15)
    order_ref[...] = (iota((512, 512), 0) == source).astype(F32).astype(BF)

    @pl.loop(0, 4)
    def _(i):
        rows = pl.ds(pl.multiple_of(i * B, B), B)
        normed = layer_norm(events_ref[rows, :].astype(F32)).astype(BF)
        normed_ref[rows, :] = dot(normed, order_ref[...]).astype(BF)


def block_of(rows, pieces):
    chips = rows.shape[0]
    pieces = [p[:, None, :] for p in pieces] + [jnp.zeros((chips, 8 - len(pieces), 128), F32)]
    return jnp.concatenate([rows[:, :, :128], rows[:, :, 128:]] + pieces, axis=1).astype(BF)


def neg_block_kernel(mine_ref, other_ref, row_ref, out_ref):
    rows = mine_ref[...].astype(F32) + other_ref[...].astype(F32)
    rows = jnp.broadcast_to(rows[None, :CSLOTS], (GROUP, CSLOTS, B))
    for g in range(NCHIPS // GROUP):
        chips = slice(g * GROUP, (g + 1) * GROUP)
        out_ref[chips] = block_of(rows, [row_ref[0, chips, :], row_ref[1, chips, :]])


def term_block_kernel(own_ref, other_ref, meta_ref, out_ref):
    for g in range(NCHIPS // GROUP):
        chips = slice(g * GROUP, (g + 1) * GROUP)
        slots = slice(g * GROUP * CSLOTS, (g + 1) * GROUP * CSLOTS)
        rows = (own_ref[slots, :] + other_ref[slots, :].astype(F32)).reshape(GROUP, CSLOTS, B)
        out_ref[chips] = block_of(rows, [meta_ref[k, chips, :] for k in range(3)])


def unpack_kernel(own_ref, other_ref, own_out_ref, other_out_ref, row_ref):
    for k, (block_ref, out_ref) in enumerate(((own_ref, own_out_ref), (other_ref, other_out_ref))):
        for g in range(NCHIPS // GROUP):
            chips = slice(g * GROUP, (g + 1) * GROUP)
            block = block_ref[chips].astype(F32)
            halves = [
                block[:, h * CSLOTS : (h + 1) * CSLOTS].reshape(GROUP * CSLOTS, 128) for h in range(2)
            ]
            slots = slice(g * GROUP * CSLOTS, (g + 1) * GROUP * CSLOTS)
            out_ref[slots, :] = jnp.concatenate(halves, axis=1).astype(BF)
            numbers = block[:, 2 * CSLOTS :]
            row_ref[k, chips, :] = (numbers[:, 0] * 64.0 + numbers[:, 1]).astype(I32)


def silu_of_half(h):
    return h + h * jnp.tanh(h)


def layer_kernel(
    info_ref, slot_ref, own_hbm, normed_hbm, other_hbm, events_hbm, follow_hbm,
    positive_ref, hidden_hbm, send_hbm,
    w_ref, all_ref, normed_ref, events_ref, follow_ref, act_ref, att_ref, hidden_ref, send_ref, in_sem, out_sem,
):
    core, length = info_ref[0], info_ref[1]
    blocks = [slice(i * B, (i + 1) * B) for i in range(4)]

    def fetch(k, source, to):
        return [pltpu.make_async_copy(source.at[r, :], to.at[r, :], in_sem.at[k, i]) for i, r in enumerate(blocks)]

    w_in = [
        pltpu.make_async_copy(source, all_ref.at[pl.ds(k * B, B), :], in_sem.at[3, k])
        for k, source in enumerate((own_hbm, other_hbm))
    ]
    normed_in = fetch(0, normed_hbm, normed_ref)
    events_in = fetch(1, events_hbm, events_ref)
    follow_in = fetch(2, follow_hbm, follow_ref)
    for copy in normed_in[:1] + w_in + normed_in[1:] + [c for p in zip(events_in, follow_in) for c in p]:
        copy.start()
    for copy in w_in:
        copy.wait()

    @pl.loop(0, 4)
    def _(i):
        rows = pl.ds(pl.multiple_of(i * B, B), B)
        pltpu.make_async_copy(normed_hbm.at[rows, :], normed_ref.at[rows, :], in_sem.at[0, i]).wait()
        a = normed_ref[rows, :]
        live = iota((B, 512), 0) + i * B < length
        for n in range(4):
            cols = slice(n * 512, (n + 1) * 512)
            v = silu_of_half(0.5 * dot(a, all_ref[:, cols]))
            if n == 1:
                v = jnp.where(live, v, 0.0)
            act_ref[rows, cols] = v.astype(BF)

    for b in range(16):
        own, other = slice(b * 16, (b + 1) * 16), slice(B + b * 16, B + (b + 1) * 16)
        w_ref[pl.ds(pl.multiple_of(b * 32 + core * 16, 16), 16), :] = all_ref[own, 2048:]
        w_ref[pl.ds(pl.multiple_of(b * 32 + (1 - core) * 16, 16), 16), :] = all_ref[other, 2048:]

    causal = iota((B, B), 1) <= iota((B, B), 0)
    eye = iota((B, B), 1) == iota((B, B), 0)
    scale = 0.5 / math.sqrt(128)
    hidden_out = []
    for i, rows in enumerate(blocks):

        def scores(h, j):
            q = act_ref[rows, 1024 + h * 128 : 1024 + (h + 1) * 128]
            return dot_nt(q, act_ref[blocks[j], 1536 + h * 128 : 1536 + (h + 1) * 128])

        work = [(h, j) for h in range(H) for j in range(i + 1)]
        ahead = [scores(*work[0]), scores(*work[1])]
        for n, (h, j) in enumerate(work):
            s = ahead.pop(0)
            if n + 2 < len(work):
                ahead.append(scores(*work[n + 2]))
            w = silu_of_half(s * scale)
            if j == i:
                w = jnp.where(causal, w, 0.0)
            t = dot(w.astype(BF), act_ref[blocks[j], 512 + h * 128 : 512 + (h + 1) * 128])
            total = t if j == 0 else total + t
            if j == i:
                att_ref[:, h * 128 : (h + 1) * 128] = total
        gated = (layer_norm(att_ref[...]) * act_ref[rows, :512].astype(F32)).astype(BF)
        events_in[i].wait()
        follow_in[i].wait()
        hidden = (events_ref[rows, :].astype(F32) + dot(gated, w_ref[...])).astype(BF)
        hidden_ref[rows, :] = hidden
        hidden_out.append(pltpu.make_async_copy(hidden_ref.at[rows, :], hidden_hbm.at[rows, :], out_sem.at[6 + i]))
        hidden_out[-1].start()
        pos = jnp.sum(hidden.astype(F32) * follow_ref[rows, :].astype(F32), axis=1, keepdims=True)
        positive_ref[:, rows] = jnp.sum(jnp.where(eye, pos, 0.0), axis=0, keepdims=True)

    outs = []
    for m in range(SLOTS // B):
        rows = slice(m * B, (m + 1) * B)
        send_ref[rows, :] = dot(onehot(m * B, B, slot_ref[0:1, :]), hidden_ref[...]).astype(BF)
        outs.append(pltpu.make_async_copy(send_ref.at[rows, :], send_hbm.at[rows, :], out_sem.at[m]))
        outs[-1].start()
    for copy in hidden_out + outs:
        copy.wait()


def loss_kernel(
    info_ref, hidden_ref, own_ref, other_ref, ids_ref, logc_ref, positive_ref, targets_ref, slot_ref,
    loss_ref, term_own_ref, term_other_ref, meta_ref, l_ref, probs_ref, coef_ref,
):
    core, length = info_ref[0], info_ref[1]
    own_cols = pl.ds(pl.multiple_of(core * B, B), B)
    other_cols = pl.ds(pl.multiple_of((1 - core) * B, B), B)
    chunks = [slice(m * B, (m + 1) * B) for m in range(SLOTS // B)]

    @pl.loop(0, 4)
    def _(t):
        at = pl.ds(pl.multiple_of(t * B, B), B)
        h_own = hidden_ref[at, own_cols]
        h_other = hidden_ref[at, other_cols]
        pos = positive_ref[:, at]
        target = targets_ref[:, at]
        top = pos
        for m in chunks:
            logc, ids = logc_ref[m, :], ids_ref[m, :]
            value = dot_nt(own_ref[m, :], h_own) + dot_nt(other_ref[m, :], h_other)
            value = value - jnp.concatenate([logc, logc], axis=1)
            value = jnp.where(jnp.concatenate([ids, ids], axis=1) != target, value, NEG_INF)
            l_ref[m, :] = value
            top = jnp.maximum(top, jnp.max(value, axis=0, keepdims=True))
        total = jnp.exp(pos - top)
        for m in chunks:
            total = total + jnp.sum(jnp.exp(l_ref[m, :] - top), axis=0, keepdims=True)
        log_total = top + jnp.log(total)
        in_range = iota((1, B), 1) + t * B < length - 1
        loss_ref[:, at] = jnp.where(in_range, log_total - pos, 0.0)
        coef_ref[:, at] = jnp.where(in_range, jnp.exp(pos - log_total) - 1.0, 0.0)
        shift = jnp.where(in_range, log_total, POS_INF)
        for m in chunks:
            probs_ref[m, at] = jnp.exp(l_ref[m, :] - shift).astype(BF)

    coef = coef_ref[...]
    high = coef.astype(BF).astype(F32)
    middle = (coef - high).astype(BF).astype(F32)
    low = coef - high - middle
    for k, piece in enumerate((high, middle, low)):
        meta_ref[k] = by_place(slot_ref[1:2, :], slot_ref[2:3, :], [piece], NCHIPS)
    for m in chunks:
        term_other_ref[m, :] = dot(probs_ref[m, :], hidden_ref[:, other_cols]).astype(BF)
        term_own_ref[m, :] = dot(probs_ref[m, :], hidden_ref[:, own_cols])


def rank_kernel(info_ref, row_ref, neg_ref, at_ref, sorted_key_ref, start_ref, neg_at_ref):
    core = info_ref[0]
    row = row_ref[...] - 1 - core * ITEMS_DEV
    row = jnp.where((row >= 0) & (row < ITEMS_DEV), row, 2 * ITEMS_DEV - 1)
    n = row.shape[1]
    key = row * 4096 + iota((1, n), 1)
    eye = iota((128, 128), 1) == iota((128, 128), 0)
    at = jnp.zeros((1, n), F32)
    for m in range(n // 128):
        col = jnp.sum(jnp.where(eye, key[:, m * 128 : (m + 1) * 128], 0), axis=1, keepdims=True)
        at = at + jnp.sum((col < key).astype(F32), axis=0, keepdims=True)
    at = at.astype(I32)
    at_ref[...] = at
    for i in range(ITEMS_DEV // TILE + 1):
        start_ref[i] = jnp.sum((row < i * TILE).astype(I32))
    start_ref[31] = core
    neg = neg_ref[:, :1]
    neg = jnp.where(neg < 0, 2 * ITEMS_DEV, neg) * 64 + iota((32, 1), 0)
    small_eye = iota((32, 32), 1) == iota((32, 32), 0)
    neg_row = jnp.sum(jnp.where(small_eye, neg, 0), axis=0, keepdims=True)
    neg_rank = jnp.sum((neg < neg_row).astype(I32), axis=0, keepdims=True)
    for p in range(16):
        found = jnp.sum(jnp.where(neg_rank == p, neg_row, 0))
        neg_at_ref[p] = found & 63
        neg_at_ref[16 + p] = found >> 6
    for i in range(ITEMS_DEV // TILE + 1):
        neg_at_ref[32 + i] = jnp.sum(((neg_row >> 6) < i * TILE).astype(I32))
    sorted_key_ref[...] = by_place(at >> 7, at & 127, [row >> 6, row & 63], PLACES // 128, (64.0, 1.0)).astype(I32)


def sort_kernel(at_ref, own_ref, other_ref, sorted_ref):
    for m in range(PLACES // B):
        block = slice(m * B, (m + 1) * B)
        sorted_ref[block, :] = (
            dot(onehot(m * B, B, at_ref[:, :SLOTS]), own_ref[...])
            + dot(onehot(m * B, B, at_ref[:, SLOTS:]), other_ref[...])
        ).astype(BF)


def collect_kernel(got_ref, small_ref):
    total = jnp.zeros((2 * CSLOTS, 128), F32)
    for g in range(NCHIPS // GROUP):
        block = got_ref[g * GROUP : (g + 1) * GROUP].astype(F32)
        total = total + jnp.sum(block[:, : 2 * CSLOTS], axis=0)
    small_ref[:CSLOTS, :] = jnp.concatenate([total[:CSLOTS], total[CSLOTS:]], axis=1)
    k = iota((1, SLOTS), 1)
    chip = ((k.astype(F32) + 0.5) * (1.0 / CSLOTS)).astype(I32)
    spread = (iota((128, SLOTS), 0) == k - chip * CSLOTS).astype(F32).astype(BF)
    mine = iota((NCHIPS, SLOTS), 0) == chip
    row = jnp.zeros((1, SLOTS), F32)
    for p in range(3):
        piece = got_ref[:, 2 * CSLOTS + p, :]
        row = row + jnp.sum(jnp.where(mine, dot(piece, spread), 0.0), axis=0, keepdims=True)
    for r in range(SLOTS // B):
        small_ref[CSLOTS + r : CSLOTS + r + 1, :] = row[:, r * B : (r + 1) * B]
    small_ref[CSLOTS + SLOTS // B :, :] = jnp.zeros((8 - SLOTS // B, B), F32)


def place_kernel(
    start_ref, neg_at_ref, small_ref, small_other_ref, at_ref, key_ref, rows_ref, out_hbm,
    scaled_ref, neg_ref, total_ref, out_ref, sems,
):
    coef = jnp.concatenate(
        [ref[CSLOTS + r : CSLOTS + r + 1, :] for ref in (small_ref, small_other_ref) for r in range(SLOTS // B)],
        axis=1,
    )
    top = coef.astype(BF).astype(F32)
    middle = (coef - top).astype(BF).astype(F32)
    at = at_ref[...]
    coef = by_place(at >> 7, at & 127, [top, middle, coef - top - middle], PLACES // 128)
    eye = iota((128, 128), 1) == iota((128, 128), 0)
    for m in range(PLACES // 128):
        block = slice(m * 128, (m + 1) * 128)
        col = jnp.sum(jnp.where(eye, coef[m : m + 1, :], 0.0), axis=1, keepdims=True)
        scaled_ref[block, :] = (rows_ref[block, :].astype(F32) * col).astype(BF)
    own, other = small_ref[:CSLOTS, :], small_other_ref[:CSLOTS, :]
    first = start_ref[31] == 0
    neg_ref[...] = jnp.concatenate([jnp.where(first, own, other), jnp.where(first, other, own)], axis=1)

    def part(base, j):
        block = pl.ds(pl.multiple_of(j * B, B), B)
        key = jnp.concatenate([key_ref[pl.ds(2 * j, 1), :], key_ref[pl.ds(2 * j + 1, 1), :]], axis=1)
        return dot(onehot(base, TILE, key), scaled_ref[block, :])

    copies = []
    for i in range(ITEMS_DEV // TILE):
        base = i * TILE
        tile = slice(base, base + TILE)
        first = jnp.minimum(start_ref[i] // B, PLACES // B - 1)
        total_ref[...] = part(base, first)

        @pl.loop(first + 1, (start_ref[i + 1] + B - 1) // B)
        def _(j):
            total_ref[...] += part(base, j)

        @pl.loop(neg_at_ref[32 + i], neg_at_ref[33 + i])
        def _(p):
            total_ref[pl.ds(neg_at_ref[16 + p] - base, 1), :] += neg_ref[pl.ds(neg_at_ref[p], 1), :]

        out_ref[tile, :] = total_ref[...].astype(BF)
        copies.append(pltpu.make_async_copy(out_ref.at[tile, :], out_hbm.at[tile, :], sems.at[i]))
        copies[-1].start()
    for copy in copies:
        copy.wait()


def swap(v):
    return lax.ppermute(v, "c", SWAP)


def chips_a2a(v):
    return lax.all_to_all(v, CHIPS, split_axis=0, concat_axis=0, tiled=True)


def per_device(events, lengths, target_ids, neg_ids, neg_counts, item_table, w_uvqk, w_out):
    width = 512
    core = lax.axis_index("c")
    chip = lax.axis_index(CHIPS)
    info = jnp.stack([core, lengths[0], chip]).astype(I32)
    ev = events[0]

    w_mine = jnp.concatenate([w_uvqk, w_out], axis=1)
    w_own = lax.all_to_all(
        jnp.broadcast_to(w_mine[None], (16,) + w_mine.shape), ("x", "z"), split_axis=0, concat_axis=0, tiled=True
    ).reshape(256, 2560)

    normed, ids, logc, target_slot, send_row, neg_table = call(
        prep_kernel,
        (
            jax.ShapeDtypeStruct((1024, width), BF),
            jax.ShapeDtypeStruct((SLOTS, 128), I32),
            jax.ShapeDtypeStruct((SLOTS, 128), F32),
            jax.ShapeDtypeStruct((3, 1024), I32),
            jax.ShapeDtypeStruct((2, NCHIPS, 128), F32),
            jax.ShapeDtypeStruct((32, 128), I32),
        ),
        [SMEM] + [VMEM] * 4,
        scratch=[pltpu.VMEM((1024, 1024), BF), pltpu.VMEM((2 * DEVS, 1024), BF), pltpu.VMEM((512, 512), BF)],
        vmem=16,
    )(info, ev, target_ids, neg_ids[None], neg_counts[None])

    neg_local = neg_table[:, 0]
    packed = jnp.where((neg_local >= 0)[:, None], item_table[jnp.maximum(neg_local, 0)], 0)
    packed_own = lax.dynamic_slice(packed, (0, core * B), (32, B))
    packed_other = lax.dynamic_slice(packed, (0, (1 - core) * B), (32, B))
    neg_block = call(
        neg_block_kernel, jax.ShapeDtypeStruct((NCHIPS, BLOCK, 128), BF), [VMEM] * 3, vmem=8
    )(packed_own, swap(packed_other), send_row)

    follow = jnp.concatenate([ev[1:], jnp.zeros((1, width), BF)], axis=0)
    w_own, normed, follow, neg_block = lax.optimization_barrier((w_own, normed, follow, neg_block))
    got_neg = chips_a2a(neg_block)
    w_other = swap(w_own)
    any_space = pl.BlockSpec(memory_space=pl.ANY)
    positive, hidden, send_rows = pl.pallas_call(
        layer_kernel,
        out_shape=(
            jax.ShapeDtypeStruct((1, 1024), F32),
            jax.ShapeDtypeStruct((1024, width), BF),
            jax.ShapeDtypeStruct((SLOTS, width), BF),
        ),
        in_specs=[SMEM, VMEM] + [any_space] * 5,
        out_specs=(VMEM, any_space, any_space),
        scratch_shapes=[
            pltpu.VMEM((512, 512), BF),
            pltpu.VMEM((512, 2560), BF),
            pltpu.VMEM((1024, width), BF),
            pltpu.VMEM((1024, width), BF),
            pltpu.VMEM((1024, width), BF),
            pltpu.VMEM((1024, 2048), BF),
            pltpu.VMEM((B, width), F32),
            pltpu.VMEM((1024, width), BF),
            pltpu.VMEM((SLOTS, width), BF),
            pltpu.SemaphoreType.DMA((4, 4)),
            pltpu.SemaphoreType.DMA((10,)),
        ],
        cost_estimate=pl.CostEstimate(flops=0, bytes_accessed=0, transcendentals=0),
        compiler_params=pltpu.CompilerParams(vmem_limit_bytes=52 << 20),
    )(info, target_slot, w_own, normed, w_other, ev, follow)
    got_neg, send_rows = lax.optimization_barrier((got_neg, send_rows))
    other_neg = swap(got_neg)

    neg_own, neg_other, row_table = call(
        unpack_kernel,
        (
            jax.ShapeDtypeStruct((SLOTS, B), BF),
            jax.ShapeDtypeStruct((SLOTS, B), BF),
            jax.ShapeDtypeStruct((2, NCHIPS, 128), I32),
        ),
        [VMEM] * 2,
        vmem=16,
    )(got_neg, other_neg)

    recv_rows = chips_a2a(send_rows.reshape(NCHIPS, CSLOTS, width)).reshape(SLOTS, width)

    loss, term_own, term_other, meta = call(
        loss_kernel,
        (
            jax.ShapeDtypeStruct((1, 1024), F32),
            jax.ShapeDtypeStruct((SLOTS, B), F32),
            jax.ShapeDtypeStruct((SLOTS, B), BF),
            jax.ShapeDtypeStruct((3, NCHIPS, 128), F32),
        ),
        [SMEM] + [VMEM] * 8,
        scratch=[
            pltpu.VMEM((SLOTS, B), F32),
            pltpu.VMEM((SLOTS, 1024), BF),
            pltpu.VMEM((1, 1024), F32),
        ],
        flops=0,
        nbytes=0,
        vmem=28,
    )(
        info, hidden, neg_own, neg_other, ids, logc, positive, target_ids, target_slot,
    )
    block = call(
        term_block_kernel, jax.ShapeDtypeStruct((NCHIPS, BLOCK, 128), BF), [VMEM] * 3, vmem=16
    )(term_own, swap(term_other), meta)
    recv_rows, block = lax.optimization_barrier((recv_rows, block))
    got = chips_a2a(block)

    recv_other = swap(recv_rows)
    at, sorted_key, starts, neg_at = pl.pallas_call(
        rank_kernel,
        out_shape=(
            jax.ShapeDtypeStruct((1, 2 * SLOTS), I32),
            jax.ShapeDtypeStruct((PLACES // 128, 128), I32),
            jax.ShapeDtypeStruct((32,), I32),
            jax.ShapeDtypeStruct((48,), I32),
        ),
        in_specs=[SMEM, VMEM, VMEM],
        out_specs=(VMEM, VMEM, SMEM, SMEM),
        cost_estimate=pl.CostEstimate(flops=0, bytes_accessed=0, transcendentals=0),
        compiler_params=pltpu.CompilerParams(vmem_limit_bytes=16 << 20),
    )(info, row_table[:, :, :CSLOTS].reshape(1, 2 * SLOTS), neg_table)
    rows = call(sort_kernel, jax.ShapeDtypeStruct((PLACES, width), BF), [VMEM] * 3, vmem=24)(
        at, recv_rows, recv_other
    )

    got, rows = lax.optimization_barrier((got, rows))
    small = call(collect_kernel, jax.ShapeDtypeStruct((32, B), F32), [VMEM], vmem=8)(got)
    small_other = swap(small)
    tiles = ITEMS_DEV // TILE
    grad = pl.pallas_call(
        place_kernel,
        out_shape=jax.ShapeDtypeStruct((ITEMS_DEV, width), BF),
        in_specs=[SMEM] * 2 + [VMEM] * 5,
        out_specs=pl.BlockSpec(memory_space=pl.ANY),
        scratch_shapes=[
            pltpu.VMEM((PLACES, width), BF),
            pltpu.VMEM((CSLOTS, width), F32),
            pltpu.VMEM((TILE, width), F32),
            pltpu.VMEM((ITEMS_DEV, width), BF),
            pltpu.SemaphoreType.DMA((tiles,)),
        ],
        cost_estimate=pl.CostEstimate(flops=0, bytes_accessed=0, transcendentals=0),
        compiler_params=pltpu.CompilerParams(vmem_limit_bytes=24 << 20),
    )(starts, neg_at, small, small_other, at, sorted_key, rows)
    return loss, grad


def solution(mesh):
    fine = Mesh(mesh.devices.reshape(4, 4, 4, 2), ALL)
    in_specs = (P(ALL), P(ALL), P(ALL), P(), P(), P(ALL), P(MP), P(MP))
    return jax.shard_map(
        per_device, mesh=fine, in_specs=in_specs, out_specs=(P(ALL), P(ALL)), check_vma=False
    )
```

```python
import math

import jax
import jax.numpy as jnp
from jax import lax
from jax.experimental import pallas as pl
from jax.experimental.pallas import tpu as pltpu
from jax.sharding import Mesh, PartitionSpec as P

H = 4
EPSILON = 1e-05
ALL = ("y", "x", "z", "c")
CHIPS = ("y", "x", "z")
MP = ("x", "z", "c")
BF = jnp.bfloat16
F32 = jnp.float32
I32 = jnp.int32
DEVS = 128
NCHIPS = 64
CSLOTS = 24
SLOTS = NCHIPS * CSLOTS
BLOCK = 2 * CSLOTS + 8
PLACES = 2048
GROUP = 8
ITEMS_DEV = 4096
B = 256
TILE = 512
VMEM = pl.BlockSpec(memory_space=pltpu.VMEM)
SMEM = pl.BlockSpec(memory_space=pltpu.SMEM)
NT = (((1,), (1,)), ((), ()))
NEG_INF = float("-inf")
POS_INF = float("inf")
SWAP = ((0, 1), (1, 0))


def dot(a, b):
    return jnp.dot(a, b, preferred_element_type=F32)


def dot_nt(a, b):
    return lax.dot_general(a, b, NT, preferred_element_type=F32)


def iota(shape, dim):
    return lax.broadcasted_iota(I32, shape, dim)


def layer_norm(values):
    center = values - jnp.mean(values, axis=-1, keepdims=True)
    spread = jnp.mean(center * center, axis=-1, keepdims=True)
    return center * lax.rsqrt(spread + EPSILON)


def call(body, out_shape, in_specs, scratch=(), flops=0, nbytes=0, vmem=56):
    return pl.pallas_call(
        body,
        out_shape=out_shape,
        in_specs=in_specs,
        out_specs=jax.tree.map(lambda _: VMEM, out_shape),
        scratch_shapes=list(scratch),
        cost_estimate=pl.CostEstimate(flops=flops, bytes_accessed=nbytes, transcendentals=0),
        compiler_params=pltpu.CompilerParams(vmem_limit_bytes=vmem << 20),
    )


def onehot(base, count, index):
    return (iota((count, index.shape[1]), 0) + base == index).astype(F32).astype(BF)


def by_place(high, low, pieces, count):
    rows = iota((count, high.shape[1]), 0) == high
    stacked = jnp.concatenate([jnp.where(rows, p.astype(F32), 0.0) for p in pieces], axis=0).astype(BF)
    got = dot_nt(stacked, onehot(0, 128, low))
    return [got[k * count : (k + 1) * count] for k in range(len(pieces))]


def prep_kernel(
    info_ref, events_ref, targets_ref, negs_ref, counts_ref,
    normed_ref, ids_ref, logc_ref, slot_ref, row_ref, local_ref, tri_ref, owner_ref, order_ref,
):
    core, chip = info_ref[0], info_ref[2]
    targets, negs = targets_ref[...], negs_ref[...]
    n = targets.shape[1]

    for k in range(4):
        rows = slice(k * B, (k + 1) * B)
        tri_ref[rows, :] = (iota((B, n), 0) + k * B < iota((B, n), 1)).astype(F32).astype(BF)
    t_owner, n_owner = targets >> 12, negs >> 12
    owner_ref[:DEVS, :] = onehot(0, DEVS, t_owner)
    owner_ref[DEVS:, :] = onehot(0, DEVS, n_owner)
    before = dot(owner_ref[...], tri_ref[...]) * owner_ref[...].astype(F32)
    t_rank = jnp.sum(before[:DEVS], axis=0, keepdims=True).astype(I32)
    n_rank = jnp.sum(before[DEVS:], axis=0, keepdims=True).astype(I32)

    def within(owner, rank):
        return jnp.where(rank < 8, (owner & 1) * 8 + rank, 8 + rank)

    t_within = within(t_owner, t_rank)
    slot_ref[0:1, :] = (t_owner >> 1) * CSLOTS + t_within
    slot_ref[1:2, :] = t_owner >> 1
    slot_ref[2:3, :] = t_within
    n_slot = (n_owner >> 1) * CSLOTS + within(n_owner, n_rank)
    row = (targets & (2 * ITEMS_DEV - 1)) + 1
    row_ref[0], row_ref[1] = by_place(t_owner >> 1, t_within, [row >> 6, row & 63], NCHIPS)

    mine = (iota((32, n), 0) + chip * CSLOTS == n_slot) & ((n_owner & 1) == core)
    mine = mine & (iota((32, n), 0) < CSLOTS)
    local = jnp.max(jnp.where(mine, negs & (ITEMS_DEV - 1), -1), axis=1, keepdims=True)
    local_ref[...] = jnp.broadcast_to(local, (32, 128))
    logs = jnp.log(counts_ref[...].astype(F32))
    for m in range(SLOTS // B):
        rows = slice(m * B, (m + 1) * B)
        here = iota((B, n), 0) + m * B == n_slot
        ids = jnp.max(jnp.where(here, negs, -1), axis=1, keepdims=True)
        logc = jnp.min(jnp.where(here, logs, POS_INF), axis=1, keepdims=True)
        ids_ref[rows, :] = jnp.broadcast_to(ids, (B, 128))
        logc_ref[rows, :] = jnp.broadcast_to(logc, (B, 128))

    k = iota((512, 512), 1)
    source = ((k & 255) >> 4) * 32 + jnp.where(k < 256, core, 1 - core) * 16 + (k & 15)
    order_ref[...] = (iota((512, 512), 0) == source).astype(F32).astype(BF)

    @pl.loop(0, 4)
    def _(i):
        rows = pl.ds(pl.multiple_of(i * B, B), B)
        normed = layer_norm(events_ref[rows, :].astype(F32)).astype(BF)
        normed_ref[rows, :] = dot(normed, order_ref[...]).astype(BF)


def block_of(rows, pieces):
    chips = rows.shape[0]
    pieces = [p[:, None, :] for p in pieces] + [jnp.zeros((chips, 8 - len(pieces), 128), F32)]
    return jnp.concatenate([rows[:, :, :128], rows[:, :, 128:]] + pieces, axis=1).astype(BF)


def neg_block_kernel(mine_ref, other_ref, row_ref, out_ref):
    rows = mine_ref[...].astype(F32) + other_ref[...].astype(F32)
    rows = jnp.broadcast_to(rows[None, :CSLOTS], (GROUP, CSLOTS, B))
    for g in range(NCHIPS // GROUP):
        chips = slice(g * GROUP, (g + 1) * GROUP)
        out_ref[chips] = block_of(rows, [row_ref[0, chips, :], row_ref[1, chips, :]])


def term_block_kernel(own_ref, other_ref, meta_ref, out_ref):
    for g in range(NCHIPS // GROUP):
        chips = slice(g * GROUP, (g + 1) * GROUP)
        slots = slice(g * GROUP * CSLOTS, (g + 1) * GROUP * CSLOTS)
        rows = (own_ref[slots, :] + other_ref[slots, :].astype(F32)).reshape(GROUP, CSLOTS, B)
        out_ref[chips] = block_of(rows, [meta_ref[k, chips, :] for k in range(3)])


def unpack_kernel(own_ref, other_ref, own_out_ref, other_out_ref, row_ref):
    for k, (block_ref, out_ref) in enumerate(((own_ref, own_out_ref), (other_ref, other_out_ref))):
        for g in range(NCHIPS // GROUP):
            chips = slice(g * GROUP, (g + 1) * GROUP)
            block = block_ref[chips].astype(F32)
            halves = [
                block[:, h * CSLOTS : (h + 1) * CSLOTS].reshape(GROUP * CSLOTS, 128) for h in range(2)
            ]
            slots = slice(g * GROUP * CSLOTS, (g + 1) * GROUP * CSLOTS)
            out_ref[slots, :] = jnp.concatenate(halves, axis=1).astype(BF)
            numbers = block[:, 2 * CSLOTS :]
            row_ref[k, chips, :] = (numbers[:, 0] * 64.0 + numbers[:, 1]).astype(I32)


def silu_of_half(h):
    return h + h * jnp.tanh(h)


def layer_kernel(
    info_ref, slot_ref, own_hbm, normed_hbm, other_hbm, events_hbm, follow_hbm,
    positive_ref, hidden_hbm, send_hbm,
    w_ref, all_ref, normed_ref, events_ref, follow_ref, act_ref, att_ref, hidden_ref, send_ref, in_sem, out_sem,
):
    core, length = info_ref[0], info_ref[1]
    blocks = [slice(i * B, (i + 1) * B) for i in range(4)]

    def fetch(k, source, to):
        return [pltpu.make_async_copy(source.at[r, :], to.at[r, :], in_sem.at[k, i]) for i, r in enumerate(blocks)]

    w_in = [
        pltpu.make_async_copy(source, all_ref.at[pl.ds(k * B, B), :], in_sem.at[3, k])
        for k, source in enumerate((own_hbm, other_hbm))
    ]
    normed_in = fetch(0, normed_hbm, normed_ref)
    events_in = fetch(1, events_hbm, events_ref)
    follow_in = fetch(2, follow_hbm, follow_ref)
    for copy in normed_in[:1] + w_in + normed_in[1:] + [c for p in zip(events_in, follow_in) for c in p]:
        copy.start()
    for copy in w_in:
        copy.wait()

    @pl.loop(0, 4)
    def _(i):
        rows = pl.ds(pl.multiple_of(i * B, B), B)
        pltpu.make_async_copy(normed_hbm.at[rows, :], normed_ref.at[rows, :], in_sem.at[0, i]).wait()
        a = normed_ref[rows, :]
        live = iota((B, 512), 0) + i * B < length
        for n in range(4):
            cols = slice(n * 512, (n + 1) * 512)
            v = silu_of_half(0.5 * dot(a, all_ref[:, cols]))
            if n == 1:
                v = jnp.where(live, v, 0.0)
            act_ref[rows, cols] = v.astype(BF)

    for b in range(16):
        own, other = slice(b * 16, (b + 1) * 16), slice(B + b * 16, B + (b + 1) * 16)
        w_ref[pl.ds(pl.multiple_of(b * 32 + core * 16, 16), 16), :] = all_ref[own, 2048:]
        w_ref[pl.ds(pl.multiple_of(b * 32 + (1 - core) * 16, 16), 16), :] = all_ref[other, 2048:]

    causal = iota((B, B), 1) <= iota((B, B), 0)
    eye = iota((B, B), 1) == iota((B, B), 0)
    scale = 0.5 / math.sqrt(128)
    hidden_out = []
    for i, rows in enumerate(blocks):

        def scores(h, j):
            q = act_ref[rows, 1024 + h * 128 : 1024 + (h + 1) * 128]
            return dot_nt(q, act_ref[blocks[j], 1536 + h * 128 : 1536 + (h + 1) * 128])

        work = [(h, j) for h in range(H) for j in range(i + 1)]
        ahead = [scores(*work[0]), scores(*work[1])]
        for n, (h, j) in enumerate(work):
            s = ahead.pop(0)
            if n + 2 < len(work):
                ahead.append(scores(*work[n + 2]))
            w = silu_of_half(s * scale)
            if j == i:
                w = jnp.where(causal, w, 0.0)
            t = dot(w.astype(BF), act_ref[blocks[j], 512 + h * 128 : 512 + (h + 1) * 128])
            total = t if j == 0 else total + t
            if j == i:
                att_ref[:, h * 128 : (h + 1) * 128] = total
        gated = (layer_norm(att_ref[...]) * act_ref[rows, :512].astype(F32)).astype(BF)
        events_in[i].wait()
        follow_in[i].wait()
        hidden = (events_ref[rows, :].astype(F32) + dot(gated, w_ref[...])).astype(BF)
        hidden_ref[rows, :] = hidden
        hidden_out.append(pltpu.make_async_copy(hidden_ref.at[rows, :], hidden_hbm.at[rows, :], out_sem.at[6 + i]))
        hidden_out[-1].start()
        pos = jnp.sum(hidden.astype(F32) * follow_ref[rows, :].astype(F32), axis=1, keepdims=True)
        positive_ref[:, rows] = jnp.sum(jnp.where(eye, pos, 0.0), axis=0, keepdims=True)

    outs = []
    for m in range(SLOTS // B):
        rows = slice(m * B, (m + 1) * B)
        send_ref[rows, :] = dot(onehot(m * B, B, slot_ref[0:1, :]), hidden_ref[...]).astype(BF)
        outs.append(pltpu.make_async_copy(send_ref.at[rows, :], send_hbm.at[rows, :], out_sem.at[m]))
        outs[-1].start()
    for copy in hidden_out + outs:
        copy.wait()


def loss_kernel(
    info_ref, hidden_ref, own_ref, other_ref, ids_ref, logc_ref, positive_ref, targets_ref, slot_ref,
    loss_ref, term_own_ref, term_other_ref, meta_ref, l_ref, probs_ref, coef_ref,
):
    core, length = info_ref[0], info_ref[1]
    own_cols = pl.ds(pl.multiple_of(core * B, B), B)
    other_cols = pl.ds(pl.multiple_of((1 - core) * B, B), B)
    chunks = [slice(m * B, (m + 1) * B) for m in range(SLOTS // B)]

    @pl.loop(0, 4)
    def _(t):
        at = pl.ds(pl.multiple_of(t * B, B), B)
        h_own = hidden_ref[at, own_cols]
        h_other = hidden_ref[at, other_cols]
        pos = positive_ref[:, at]
        target = targets_ref[:, at]
        top = pos
        for m in chunks:
            logc, ids = logc_ref[m, :], ids_ref[m, :]
            value = dot_nt(own_ref[m, :], h_own) + dot_nt(other_ref[m, :], h_other)
            value = value - jnp.concatenate([logc, logc], axis=1)
            value = jnp.where(jnp.concatenate([ids, ids], axis=1) != target, value, NEG_INF)
            l_ref[m, :] = value
            top = jnp.maximum(top, jnp.max(value, axis=0, keepdims=True))
        total = jnp.exp(pos - top)
        for m in chunks:
            total = total + jnp.sum(jnp.exp(l_ref[m, :] - top), axis=0, keepdims=True)
        log_total = top + jnp.log(total)
        in_range = iota((1, B), 1) + t * B < length - 1
        loss_ref[:, at] = jnp.where(in_range, log_total - pos, 0.0)
        coef_ref[:, at] = jnp.where(in_range, jnp.exp(pos - log_total) - 1.0, 0.0)
        shift = jnp.where(in_range, log_total, POS_INF)
        for m in chunks:
            probs_ref[m, at] = jnp.exp(l_ref[m, :] - shift).astype(BF)

    coef = coef_ref[...]
    high = coef.astype(BF).astype(F32)
    middle = (coef - high).astype(BF).astype(F32)
    low = coef - high - middle
    pieces = by_place(slot_ref[1:2, :], slot_ref[2:3, :], [high, middle, low], NCHIPS)
    for k, piece in enumerate(pieces):
        meta_ref[k] = piece
    for m in chunks:
        term_other_ref[m, :] = dot(probs_ref[m, :], hidden_ref[:, other_cols]).astype(BF)
        term_own_ref[m, :] = dot(probs_ref[m, :], hidden_ref[:, own_cols])


def rank_kernel(info_ref, row_ref, neg_ref, at_ref, sorted_key_ref, start_ref, neg_at_ref):
    core = info_ref[0]
    row = row_ref[...] - 1 - core * ITEMS_DEV
    row = jnp.where((row >= 0) & (row < ITEMS_DEV), row, 2 * ITEMS_DEV - 1)
    n = row.shape[1]
    key = row * 4096 + iota((1, n), 1)
    eye = iota((128, 128), 1) == iota((128, 128), 0)
    at = jnp.zeros((1, n), F32)
    for m in range(n // 128):
        col = jnp.sum(jnp.where(eye, key[:, m * 128 : (m + 1) * 128], 0), axis=1, keepdims=True)
        at = at + jnp.sum((col < key).astype(F32), axis=0, keepdims=True)
    at = at.astype(I32)
    at_ref[...] = at
    for i in range(ITEMS_DEV // TILE + 1):
        start_ref[i] = jnp.sum((row < i * TILE).astype(I32))
    start_ref[31] = core
    neg = neg_ref[:, :1]
    neg = jnp.where(neg < 0, 2 * ITEMS_DEV, neg) * 64 + iota((32, 1), 0)
    small_eye = iota((32, 32), 1) == iota((32, 32), 0)
    neg_row = jnp.sum(jnp.where(small_eye, neg, 0), axis=0, keepdims=True)
    neg_rank = jnp.sum((neg < neg_row).astype(I32), axis=0, keepdims=True)
    for p in range(16):
        found = jnp.sum(jnp.where(neg_rank == p, neg_row, 0))
        neg_at_ref[p] = found & 63
        neg_at_ref[16 + p] = found >> 6
    for i in range(ITEMS_DEV // TILE + 1):
        neg_at_ref[32 + i] = jnp.sum(((neg_row >> 6) < i * TILE).astype(I32))
    key_high, key_low = by_place(at >> 7, at & 127, [row >> 6, row & 63], PLACES // 128)
    sorted_key_ref[...] = (key_high * 64.0 + key_low).astype(I32)


def sort_kernel(at_ref, own_ref, other_ref, sorted_ref):
    for m in range(PLACES // B):
        block = slice(m * B, (m + 1) * B)
        sorted_ref[block, :] = (
            dot(onehot(m * B, B, at_ref[:, :SLOTS]), own_ref[...])
            + dot(onehot(m * B, B, at_ref[:, SLOTS:]), other_ref[...])
        ).astype(BF)


def collect_kernel(got_ref, small_ref):
    total = jnp.zeros((2 * CSLOTS, 128), F32)
    for g in range(NCHIPS // GROUP):
        block = got_ref[g * GROUP : (g + 1) * GROUP].astype(F32)
        total = total + jnp.sum(block[:, : 2 * CSLOTS], axis=0)
    small_ref[:CSLOTS, :] = jnp.concatenate([total[:CSLOTS], total[CSLOTS:]], axis=1)
    k = iota((1, SLOTS), 1)
    chip = ((k.astype(F32) + 0.5) * (1.0 / CSLOTS)).astype(I32)
    spread = (iota((128, SLOTS), 0) == k - chip * CSLOTS).astype(F32).astype(BF)
    mine = iota((NCHIPS, SLOTS), 0) == chip
    row = jnp.zeros((1, SLOTS), F32)
    for p in range(3):
        piece = got_ref[:, 2 * CSLOTS + p, :]
        row = row + jnp.sum(jnp.where(mine, dot(piece, spread), 0.0), axis=0, keepdims=True)
    for r in range(SLOTS // B):
        small_ref[CSLOTS + r : CSLOTS + r + 1, :] = row[:, r * B : (r + 1) * B]
    small_ref[CSLOTS + SLOTS // B :, :] = jnp.zeros((8 - SLOTS // B, B), F32)


def place_kernel(
    start_ref, neg_at_ref, small_ref, small_other_ref, at_ref, key_ref, rows_ref, out_hbm,
    scaled_ref, neg_ref, total_ref, out_ref, sems,
):
    coef = jnp.concatenate(
        [ref[CSLOTS + r : CSLOTS + r + 1, :] for ref in (small_ref, small_other_ref) for r in range(SLOTS // B)],
        axis=1,
    )
    top = coef.astype(BF).astype(F32)
    middle = (coef - top).astype(BF).astype(F32)
    at = at_ref[...]
    top, middle, low = by_place(at >> 7, at & 127, [top, middle, coef - top - middle], PLACES // 128)
    coef = top + middle + low
    cols = jnp.transpose(jnp.concatenate([coef, jnp.zeros((128 - coef.shape[0], 128), F32)], axis=0))
    for m in range(PLACES // 128):
        block = slice(m * 128, (m + 1) * 128)
        scaled_ref[block, :] = (rows_ref[block, :].astype(F32) * cols[:, m : m + 1]).astype(BF)
    own, other = small_ref[:CSLOTS, :], small_other_ref[:CSLOTS, :]
    first = start_ref[31] == 0
    neg_ref[...] = jnp.concatenate([jnp.where(first, own, other), jnp.where(first, other, own)], axis=1)

    def part(base, j):
        block = pl.ds(pl.multiple_of(j * B, B), B)
        key = jnp.concatenate([key_ref[pl.ds(2 * j, 1), :], key_ref[pl.ds(2 * j + 1, 1), :]], axis=1)
        return dot(onehot(base, TILE, key), scaled_ref[block, :])

    copies = []
    for i in range(ITEMS_DEV // TILE):
        base = i * TILE
        tile = slice(base, base + TILE)
        first = jnp.minimum(start_ref[i] // B, PLACES // B - 1)
        total_ref[...] = part(base, first)

        @pl.loop(first + 1, (start_ref[i + 1] + B - 1) // B)
        def _(j):
            total_ref[...] += part(base, j)

        @pl.loop(neg_at_ref[32 + i], neg_at_ref[33 + i])
        def _(p):
            total_ref[pl.ds(neg_at_ref[16 + p] - base, 1), :] += neg_ref[pl.ds(neg_at_ref[p], 1), :]

        out_ref[tile, :] = total_ref[...].astype(BF)
        copies.append(pltpu.make_async_copy(out_ref.at[tile, :], out_hbm.at[tile, :], sems.at[i]))
        copies[-1].start()
    for copy in copies:
        copy.wait()


def swap(v):
    return lax.ppermute(v, "c", SWAP)


def chips_a2a(v):
    return lax.all_to_all(v, CHIPS, split_axis=0, concat_axis=0, tiled=True)


def per_device(events, lengths, target_ids, neg_ids, neg_counts, item_table, w_uvqk, w_out):
    width = 512
    core = lax.axis_index("c")
    chip = lax.axis_index(CHIPS)
    info = jnp.stack([core, lengths[0], chip]).astype(I32)
    ev = events[0]

    w_mine = jnp.concatenate([w_uvqk, w_out], axis=1)
    w_own = lax.all_to_all(
        jnp.broadcast_to(w_mine[None], (16,) + w_mine.shape), ("x", "z"), split_axis=0, concat_axis=0, tiled=True
    ).reshape(256, 2560)

    normed, ids, logc, target_slot, send_row, neg_table = call(
        prep_kernel,
        (
            jax.ShapeDtypeStruct((1024, width), BF),
            jax.ShapeDtypeStruct((SLOTS, 128), I32),
            jax.ShapeDtypeStruct((SLOTS, 128), F32),
            jax.ShapeDtypeStruct((3, 1024), I32),
            jax.ShapeDtypeStruct((2, NCHIPS, 128), F32),
            jax.ShapeDtypeStruct((32, 128), I32),
        ),
        [SMEM] + [VMEM] * 4,
        scratch=[pltpu.VMEM((1024, 1024), BF), pltpu.VMEM((2 * DEVS, 1024), BF), pltpu.VMEM((512, 512), BF)],
        vmem=16,
    )(info, ev, target_ids, neg_ids[None], neg_counts[None])

    neg_local = neg_table[:, 0]
    packed = jnp.where((neg_local >= 0)[:, None], item_table[jnp.maximum(neg_local, 0)], 0)
    packed_own = lax.dynamic_slice(packed, (0, core * B), (32, B))
    packed_other = lax.dynamic_slice(packed, (0, (1 - core) * B), (32, B))
    neg_block = call(
        neg_block_kernel, jax.ShapeDtypeStruct((NCHIPS, BLOCK, 128), BF), [VMEM] * 3, vmem=8
    )(packed_own, swap(packed_other), send_row)

    follow = jnp.concatenate([ev[1:], jnp.zeros((1, width), BF)], axis=0)
    w_own, normed, follow, neg_block = lax.optimization_barrier((w_own, normed, follow, neg_block))
    got_neg = chips_a2a(neg_block)
    w_other = swap(w_own)
    any_space = pl.BlockSpec(memory_space=pl.ANY)
    positive, hidden, send_rows = pl.pallas_call(
        layer_kernel,
        out_shape=(
            jax.ShapeDtypeStruct((1, 1024), F32),
            jax.ShapeDtypeStruct((1024, width), BF),
            jax.ShapeDtypeStruct((SLOTS, width), BF),
        ),
        in_specs=[SMEM, VMEM] + [any_space] * 5,
        out_specs=(VMEM, any_space, any_space),
        scratch_shapes=[
            pltpu.VMEM((512, 512), BF),
            pltpu.VMEM((512, 2560), BF),
            pltpu.VMEM((1024, width), BF),
            pltpu.VMEM((1024, width), BF),
            pltpu.VMEM((1024, width), BF),
            pltpu.VMEM((1024, 2048), BF),
            pltpu.VMEM((B, width), F32),
            pltpu.VMEM((1024, width), BF),
            pltpu.VMEM((SLOTS, width), BF),
            pltpu.SemaphoreType.DMA((4, 4)),
            pltpu.SemaphoreType.DMA((10,)),
        ],
        cost_estimate=pl.CostEstimate(flops=0, bytes_accessed=0, transcendentals=0),
        compiler_params=pltpu.CompilerParams(vmem_limit_bytes=52 << 20),
    )(info, target_slot, w_own, normed, w_other, ev, follow)
    got_neg, send_rows = lax.optimization_barrier((got_neg, send_rows))
    other_neg = swap(got_neg)

    neg_own, neg_other, row_table = call(
        unpack_kernel,
        (
            jax.ShapeDtypeStruct((SLOTS, B), BF),
            jax.ShapeDtypeStruct((SLOTS, B), BF),
            jax.ShapeDtypeStruct((2, NCHIPS, 128), I32),
        ),
        [VMEM] * 2,
        vmem=16,
    )(got_neg, other_neg)

    recv_rows = chips_a2a(send_rows.reshape(NCHIPS, CSLOTS, width)).reshape(SLOTS, width)

    loss, term_own, term_other, meta = call(
        loss_kernel,
        (
            jax.ShapeDtypeStruct((1, 1024), F32),
            jax.ShapeDtypeStruct((SLOTS, B), F32),
            jax.ShapeDtypeStruct((SLOTS, B), BF),
            jax.ShapeDtypeStruct((3, NCHIPS, 128), F32),
        ),
        [SMEM] + [VMEM] * 8,
        scratch=[
            pltpu.VMEM((SLOTS, B), F32),
            pltpu.VMEM((SLOTS, 1024), BF),
            pltpu.VMEM((1, 1024), F32),
        ],
        flops=0,
        nbytes=0,
        vmem=28,
    )(
        info, hidden, neg_own, neg_other, ids, logc, positive, target_ids, target_slot,
    )
    block = call(
        term_block_kernel, jax.ShapeDtypeStruct((NCHIPS, BLOCK, 128), BF), [VMEM] * 3, vmem=16
    )(term_own, swap(term_other), meta)
    recv_rows, block = lax.optimization_barrier((recv_rows, block))
    got = chips_a2a(block)

    recv_other = swap(recv_rows)
    at, sorted_key, starts, neg_at = pl.pallas_call(
        rank_kernel,
        out_shape=(
            jax.ShapeDtypeStruct((1, 2 * SLOTS), I32),
            jax.ShapeDtypeStruct((PLACES // 128, 128), I32),
            jax.ShapeDtypeStruct((32,), I32),
            jax.ShapeDtypeStruct((64,), I32),
        ),
        in_specs=[SMEM, VMEM, VMEM],
        out_specs=(VMEM, VMEM, SMEM, SMEM),
        cost_estimate=pl.CostEstimate(flops=0, bytes_accessed=0, transcendentals=0),
        compiler_params=pltpu.CompilerParams(vmem_limit_bytes=16 << 20),
    )(info, row_table[:, :, :CSLOTS].reshape(1, 2 * SLOTS), neg_table)
    rows = call(sort_kernel, jax.ShapeDtypeStruct((PLACES, width), BF), [VMEM] * 3, vmem=24)(
        at, recv_rows, recv_other
    )

    got, rows = lax.optimization_barrier((got, rows))
    small = call(collect_kernel, jax.ShapeDtypeStruct((32, B), F32), [VMEM], vmem=8)(got)
    small_other = swap(small)
    tiles = ITEMS_DEV // TILE
    grad = pl.pallas_call(
        place_kernel,
        out_shape=jax.ShapeDtypeStruct((ITEMS_DEV, width), BF),
        in_specs=[SMEM] * 2 + [VMEM] * 5,
        out_specs=pl.BlockSpec(memory_space=pl.ANY),
        scratch_shapes=[
            pltpu.VMEM((PLACES, width), BF),
            pltpu.VMEM((CSLOTS, width), F32),
            pltpu.VMEM((TILE, width), F32),
            pltpu.VMEM((ITEMS_DEV, width), BF),
            pltpu.SemaphoreType.DMA((tiles,)),
        ],
        cost_estimate=pl.CostEstimate(flops=0, bytes_accessed=0, transcendentals=0),
        compiler_params=pltpu.CompilerParams(vmem_limit_bytes=24 << 20),
    )(starts, neg_at, small, small_other, at, sorted_key, rows)
    return loss, grad


def solution(mesh):
    fine = Mesh(mesh.devices.reshape(4, 4, 4, 2), ALL)
    in_specs = (P(ALL), P(ALL), P(ALL), P(), P(), P(ALL), P(MP), P(MP))
    return jax.shard_map(
        per_device, mesh=fine, in_specs=in_specs, out_specs=(P(ALL), P(ALL)), check_vma=False
    )
```

```python
import math

import jax
import jax.numpy as jnp
from jax import lax
from jax.experimental import pallas as pl
from jax.experimental.pallas import tpu as pltpu
from jax.sharding import Mesh, PartitionSpec as P

H = 4
EPSILON = 1e-05
ALL = ("y", "x", "z", "c")
CHIPS = ("y", "x", "z")
MP = ("x", "z", "c")
BF = jnp.bfloat16
F32 = jnp.float32
I32 = jnp.int32
DEVS = 128
NCHIPS = 64
CSLOTS = 24
SLOTS = NCHIPS * CSLOTS
BLOCK = 2 * CSLOTS + 8
PLACES = 2048
GROUP = 8
ITEMS_DEV = 4096
B = 256
TILE = 512
VMEM = pl.BlockSpec(memory_space=pltpu.VMEM)
SMEM = pl.BlockSpec(memory_space=pltpu.SMEM)
NT = (((1,), (1,)), ((), ()))
NEG_INF = float("-inf")
POS_INF = float("inf")
SWAP = ((0, 1), (1, 0))


def dot(a, b):
    return jnp.dot(a, b, preferred_element_type=F32)


def dot_nt(a, b):
    return lax.dot_general(a, b, NT, preferred_element_type=F32)


def iota(shape, dim):
    return lax.broadcasted_iota(I32, shape, dim)


def layer_norm(values):
    center = values - jnp.mean(values, axis=-1, keepdims=True)
    spread = jnp.mean(center * center, axis=-1, keepdims=True)
    return center * lax.rsqrt(spread + EPSILON)


def call(body, out_shape, in_specs, scratch=(), flops=0, nbytes=0, vmem=56):
    return pl.pallas_call(
        body,
        out_shape=out_shape,
        in_specs=in_specs,
        out_specs=jax.tree.map(lambda _: VMEM, out_shape),
        scratch_shapes=list(scratch),
        cost_estimate=pl.CostEstimate(flops=flops, bytes_accessed=nbytes, transcendentals=0),
        compiler_params=pltpu.CompilerParams(vmem_limit_bytes=vmem << 20),
    )


def onehot(base, count, index):
    return (iota((count, index.shape[1]), 0) + base == index).astype(F32).astype(BF)


def by_place(high, low, pieces, count):
    rows = iota((count, high.shape[1]), 0) == high
    stacked = jnp.concatenate([jnp.where(rows, p.astype(F32), 0.0) for p in pieces], axis=0).astype(BF)
    got = dot_nt(stacked, onehot(0, 128, low))
    return [got[k * count : (k + 1) * count] for k in range(len(pieces))]


def prep_kernel(
    info_ref, events_ref, targets_ref, negs_ref, counts_ref,
    normed_ref, ids_ref, logc_ref, slot_ref, row_ref, local_ref, tri_ref, owner_ref, order_ref,
):
    core, chip = info_ref[0], info_ref[2]
    targets, negs = targets_ref[...], negs_ref[...]
    n = targets.shape[1]

    for k in range(4):
        rows = slice(k * B, (k + 1) * B)
        tri_ref[rows, :] = (iota((B, n), 0) + k * B < iota((B, n), 1)).astype(F32).astype(BF)
    t_owner, n_owner = targets >> 12, negs >> 12
    owner_ref[:DEVS, :] = onehot(0, DEVS, t_owner)
    owner_ref[DEVS:, :] = onehot(0, DEVS, n_owner)
    before = dot(owner_ref[...], tri_ref[...]) * owner_ref[...].astype(F32)
    t_rank = jnp.sum(before[:DEVS], axis=0, keepdims=True).astype(I32)
    n_rank = jnp.sum(before[DEVS:], axis=0, keepdims=True).astype(I32)

    def within(owner, rank):
        return jnp.where(rank < 8, (owner & 1) * 8 + rank, 8 + rank)

    t_within = within(t_owner, t_rank)
    slot_ref[0:1, :] = (t_owner >> 1) * CSLOTS + t_within
    slot_ref[1:2, :] = t_owner >> 1
    slot_ref[2:3, :] = t_within
    n_slot = (n_owner >> 1) * CSLOTS + within(n_owner, n_rank)
    row = (targets & (2 * ITEMS_DEV - 1)) + 1
    row_ref[0], row_ref[1] = by_place(t_owner >> 1, t_within, [row >> 6, row & 63], NCHIPS)

    mine = (iota((32, n), 0) + chip * CSLOTS == n_slot) & ((n_owner & 1) == core)
    mine = mine & (iota((32, n), 0) < CSLOTS)
    local = jnp.max(jnp.where(mine, negs & (ITEMS_DEV - 1), -1), axis=1, keepdims=True)
    local_ref[...] = jnp.broadcast_to(local, (32, 128))
    logs = jnp.log(counts_ref[...].astype(F32))
    for m in range(SLOTS // B):
        rows = slice(m * B, (m + 1) * B)
        here = iota((B, n), 0) + m * B == n_slot
        ids = jnp.max(jnp.where(here, negs, -1), axis=1, keepdims=True)
        logc = jnp.min(jnp.where(here, logs, POS_INF), axis=1, keepdims=True)
        ids_ref[rows, :] = jnp.broadcast_to(ids, (B, 128))
        logc_ref[rows, :] = jnp.broadcast_to(logc, (B, 128))

    k = iota((512, 512), 1)
    source = ((k & 255) >> 4) * 32 + jnp.where(k < 256, core, 1 - core) * 16 + (k & 15)
    order_ref[...] = (iota((512, 512), 0) == source).astype(F32).astype(BF)

    @pl.loop(0, 4)
    def _(i):
        rows = pl.ds(pl.multiple_of(i * B, B), B)
        normed = layer_norm(events_ref[rows, :].astype(F32)).astype(BF)
        normed_ref[rows, :] = dot(normed, order_ref[...]).astype(BF)


def block_of(rows, pieces):
    chips = rows.shape[0]
    pieces = [p[:, None, :] for p in pieces] + [jnp.zeros((chips, 8 - len(pieces), 128), F32)]
    return jnp.concatenate([rows[:, :, :128], rows[:, :, 128:]] + pieces, axis=1).astype(BF)


def neg_block_kernel(mine_ref, other_ref, row_ref, out_ref):
    rows = mine_ref[...].astype(F32) + other_ref[...].astype(F32)
    rows = jnp.broadcast_to(rows[None, :CSLOTS], (GROUP, CSLOTS, B))
    for g in range(NCHIPS // GROUP):
        chips = slice(g * GROUP, (g + 1) * GROUP)
        out_ref[chips] = block_of(rows, [row_ref[0, chips, :], row_ref[1, chips, :]])


def term_block_kernel(own_ref, other_ref, meta_ref, out_ref):
    for g in range(NCHIPS // GROUP):
        chips = slice(g * GROUP, (g + 1) * GROUP)
        slots = slice(g * GROUP * CSLOTS, (g + 1) * GROUP * CSLOTS)
        rows = (own_ref[slots, :] + other_ref[slots, :].astype(F32)).reshape(GROUP, CSLOTS, B)
        out_ref[chips] = block_of(rows, [meta_ref[k, chips, :] for k in range(3)])


def unpack_kernel(own_ref, other_ref, own_out_ref, other_out_ref, row_ref):
    for k, (block_ref, out_ref) in enumerate(((own_ref, own_out_ref), (other_ref, other_out_ref))):
        for g in range(NCHIPS // GROUP):
            chips = slice(g * GROUP, (g + 1) * GROUP)
            block = block_ref[chips].astype(F32)
            halves = [
                block[:, h * CSLOTS : (h + 1) * CSLOTS].reshape(GROUP * CSLOTS, 128) for h in range(2)
            ]
            slots = slice(g * GROUP * CSLOTS, (g + 1) * GROUP * CSLOTS)
            out_ref[slots, :] = jnp.concatenate(halves, axis=1).astype(BF)
            numbers = block[:, 2 * CSLOTS :]
            row_ref[k, chips, :] = (numbers[:, 0] * 64.0 + numbers[:, 1]).astype(I32)


def silu_of_half(h):
    return h + h * jnp.tanh(h)


def layer_kernel(
    info_ref, slot_ref, own_hbm, normed_hbm, other_hbm, events_hbm, follow_hbm,
    positive_ref, hidden_hbm, send_hbm,
    w_ref, all_ref, normed_ref, events_ref, follow_ref, act_ref, att_ref, hidden_ref, send_ref, in_sem, out_sem,
):
    core, length = info_ref[0], info_ref[1]
    blocks = [slice(i * B, (i + 1) * B) for i in range(4)]

    def fetch(k, source, to):
        return [pltpu.make_async_copy(source.at[r, :], to.at[r, :], in_sem.at[k, i]) for i, r in enumerate(blocks)]

    w_in = [
        pltpu.make_async_copy(source, all_ref.at[pl.ds(k * B, B), :], in_sem.at[3, k])
        for k, source in enumerate((own_hbm, other_hbm))
    ]
    normed_in = fetch(0, normed_hbm, normed_ref)
    events_in = fetch(1, events_hbm, events_ref)
    follow_in = fetch(2, follow_hbm, follow_ref)
    for copy in normed_in[:1] + w_in + normed_in[1:] + [c for p in zip(events_in, follow_in) for c in p]:
        copy.start()
    for copy in w_in:
        copy.wait()

    @pl.loop(0, 4)
    def _(i):
        rows = pl.ds(pl.multiple_of(i * B, B), B)
        pltpu.make_async_copy(normed_hbm.at[rows, :], normed_ref.at[rows, :], in_sem.at[0, i]).wait()
        a = normed_ref[rows, :]
        live = iota((B, 512), 0) + i * B < length
        for n in range(4):
            cols = slice(n * 512, (n + 1) * 512)
            v = silu_of_half(0.5 * dot(a, all_ref[:, cols]))
            if n == 1:
                v = jnp.where(live, v, 0.0)
            act_ref[rows, cols] = v.astype(BF)

    for b in range(16):
        own, other = slice(b * 16, (b + 1) * 16), slice(B + b * 16, B + (b + 1) * 16)
        w_ref[pl.ds(pl.multiple_of(b * 32 + core * 16, 16), 16), :] = all_ref[own, 2048:]
        w_ref[pl.ds(pl.multiple_of(b * 32 + (1 - core) * 16, 16), 16), :] = all_ref[other, 2048:]

    causal = iota((B, B), 1) <= iota((B, B), 0)
    eye = iota((B, B), 1) == iota((B, B), 0)
    scale = 0.5 / math.sqrt(128)
    hidden_out = []
    for i, rows in enumerate(blocks):

        def scores(h, j):
            q = act_ref[rows, 1024 + h * 128 : 1024 + (h + 1) * 128]
            return dot_nt(q, act_ref[blocks[j], 1536 + h * 128 : 1536 + (h + 1) * 128])

        work = [(h, j) for h in range(H) for j in range(i + 1)]
        ahead = [scores(*work[0]), scores(*work[1])]
        for n, (h, j) in enumerate(work):
            s = ahead.pop(0)
            if n + 2 < len(work):
                ahead.append(scores(*work[n + 2]))
            w = silu_of_half(s * scale)
            if j == i:
                w = jnp.where(causal, w, 0.0)
            t = dot(w.astype(BF), act_ref[blocks[j], 512 + h * 128 : 512 + (h + 1) * 128])
            total = t if j == 0 else total + t
            if j == i:
                att_ref[:, h * 128 : (h + 1) * 128] = total
        gated = (layer_norm(att_ref[...]) * act_ref[rows, :512].astype(F32)).astype(BF)
        events_in[i].wait()
        follow_in[i].wait()
        hidden = (events_ref[rows, :].astype(F32) + dot(gated, w_ref[...])).astype(BF)
        hidden_ref[rows, :] = hidden
        hidden_out.append(pltpu.make_async_copy(hidden_ref.at[rows, :], hidden_hbm.at[rows, :], out_sem.at[6 + i]))
        hidden_out[-1].start()
        pos = jnp.sum(hidden.astype(F32) * follow_ref[rows, :].astype(F32), axis=1, keepdims=True)
        positive_ref[:, rows] = jnp.sum(jnp.where(eye, pos, 0.0), axis=0, keepdims=True)

    outs = []
    for m in range(SLOTS // B):
        rows = slice(m * B, (m + 1) * B)
        send_ref[rows, :] = dot(onehot(m * B, B, slot_ref[0:1, :]), hidden_ref[...]).astype(BF)
        outs.append(pltpu.make_async_copy(send_ref.at[rows, :], send_hbm.at[rows, :], out_sem.at[m]))
        outs[-1].start()
    for copy in hidden_out + outs:
        copy.wait()


def loss_kernel(
    info_ref, hidden_ref, own_ref, other_ref, ids_ref, logc_ref, positive_ref, targets_ref, slot_ref,
    loss_ref, term_own_ref, term_other_ref, meta_ref, l_ref, probs_ref, coef_ref,
):
    core, length = info_ref[0], info_ref[1]
    own_cols = pl.ds(pl.multiple_of(core * B, B), B)
    other_cols = pl.ds(pl.multiple_of((1 - core) * B, B), B)
    chunks = [slice(m * B, (m + 1) * B) for m in range(SLOTS // B)]

    @pl.loop(0, 4)
    def _(t):
        at = pl.ds(pl.multiple_of(t * B, B), B)
        h_own = hidden_ref[at, own_cols]
        h_other = hidden_ref[at, other_cols]
        pos = positive_ref[:, at]
        target = targets_ref[:, at]
        top = pos
        for m in chunks:
            logc, ids = logc_ref[m, :], ids_ref[m, :]
            value = dot_nt(own_ref[m, :], h_own) + dot_nt(other_ref[m, :], h_other)
            value = value - jnp.concatenate([logc, logc], axis=1)
            value = jnp.where(jnp.concatenate([ids, ids], axis=1) != target, value, NEG_INF)
            l_ref[m, :] = value
            top = jnp.maximum(top, jnp.max(value, axis=0, keepdims=True))
        total = jnp.exp(pos - top)
        for m in chunks:
            total = total + jnp.sum(jnp.exp(l_ref[m, :] - top), axis=0, keepdims=True)
        log_total = top + jnp.log(total)
        in_range = iota((1, B), 1) + t * B < length - 1
        loss_ref[:, at] = jnp.where(in_range, log_total - pos, 0.0)
        coef_ref[:, at] = jnp.where(in_range, jnp.exp(pos - log_total) - 1.0, 0.0)
        shift = jnp.where(in_range, log_total, POS_INF)
        for m in chunks:
            probs_ref[m, at] = jnp.exp(l_ref[m, :] - shift).astype(BF)

    coef = coef_ref[...]
    high = coef.astype(BF).astype(F32)
    middle = (coef - high).astype(BF).astype(F32)
    low = coef - high - middle
    pieces = by_place(slot_ref[1:2, :], slot_ref[2:3, :], [high, middle, low], NCHIPS)
    for k, piece in enumerate(pieces):
        meta_ref[k] = piece
    for m in chunks:
        term_other_ref[m, :] = dot(probs_ref[m, :], hidden_ref[:, other_cols]).astype(BF)
        term_own_ref[m, :] = dot(probs_ref[m, :], hidden_ref[:, own_cols])


def rank_kernel(info_ref, row_ref, neg_ref, at_ref, sorted_key_ref, start_ref, neg_at_ref):
    core = info_ref[0]
    row = row_ref[...] - 1 - core * ITEMS_DEV
    row = jnp.where((row >= 0) & (row < ITEMS_DEV), row, 2 * ITEMS_DEV - 1)
    n = row.shape[1]
    key = row * 4096 + iota((1, n), 1)
    eye = iota((128, 128), 1) == iota((128, 128), 0)
    at = jnp.zeros((1, n), F32)
    for m in range(n // 128):
        col = jnp.sum(jnp.where(eye, key[:, m * 128 : (m + 1) * 128], 0), axis=1, keepdims=True)
        at = at + jnp.sum((col < key).astype(F32), axis=0, keepdims=True)
    at = at.astype(I32)
    at_ref[...] = at
    for i in range(ITEMS_DEV // TILE + 1):
        start_ref[i] = jnp.sum((row < i * TILE).astype(I32))
    start_ref[31] = core
    neg = neg_ref[:, :1]
    neg = jnp.where(neg < 0, 2 * ITEMS_DEV, neg) * 64 + iota((32, 1), 0)
    small_eye = iota((32, 32), 1) == iota((32, 32), 0)
    neg_row = jnp.sum(jnp.where(small_eye, neg, 0), axis=0, keepdims=True)
    neg_rank = jnp.sum((neg < neg_row).astype(I32), axis=0, keepdims=True)
    for p in range(16):
        found = jnp.sum(jnp.where(neg_rank == p, neg_row, 0))
        neg_at_ref[p] = found & 63
        neg_at_ref[16 + p] = found >> 6
    for i in range(ITEMS_DEV // TILE + 1):
        neg_at_ref[32 + i] = jnp.sum(((neg_row >> 6) < i * TILE).astype(I32))
    key_high, key_low = by_place(at >> 7, at & 127, [row >> 6, row & 63], PLACES // 128)
    sorted_key_ref[...] = (key_high * 64.0 + key_low).astype(I32)


def sort_kernel(at_ref, own_ref, other_ref, sorted_ref):
    for m in range(PLACES // B):
        block = slice(m * B, (m + 1) * B)
        sorted_ref[block, :] = (
            dot(onehot(m * B, B, at_ref[:, :SLOTS]), own_ref[...])
            + dot(onehot(m * B, B, at_ref[:, SLOTS:]), other_ref[...])
        ).astype(BF)


def collect_kernel(got_ref, small_ref):
    total = jnp.zeros((2 * CSLOTS, 128), F32)
    parts = [[], [], []]
    for g in range(NCHIPS // GROUP):
        block = got_ref[g * GROUP : (g + 1) * GROUP].astype(F32)
        total = total + jnp.sum(block[:, : 2 * CSLOTS], axis=0)
        for p in range(3):
            parts[p].append(block[:, 2 * CSLOTS + p])
    small_ref[:CSLOTS, :] = jnp.concatenate([total[:CSLOTS], total[CSLOTS:]], axis=1)
    k = iota((1, SLOTS), 1)
    chip = ((k.astype(F32) + 0.5) * (1.0 / CSLOTS)).astype(I32)
    spread = (iota((128, SLOTS), 0) == k - chip * CSLOTS).astype(F32).astype(BF)
    mine = iota((NCHIPS, SLOTS), 0) == chip
    row = jnp.zeros((1, SLOTS), F32)
    for p in range(3):
        piece = jnp.concatenate(parts[p], axis=0).astype(BF)
        row = row + jnp.sum(jnp.where(mine, dot(piece, spread), 0.0), axis=0, keepdims=True)
    for r in range(SLOTS // B):
        small_ref[CSLOTS + r : CSLOTS + r + 1, :] = row[:, r * B : (r + 1) * B]
    small_ref[CSLOTS + SLOTS // B :, :] = jnp.zeros((8 - SLOTS // B, B), F32)


def place_kernel(
    start_ref, neg_at_ref, small_ref, small_other_ref, at_ref, key_ref, rows_ref, out_hbm,
    scaled_ref, neg_ref, total_ref, out_ref, sems,
):
    coef = jnp.concatenate(
        [ref[CSLOTS + r : CSLOTS + r + 1, :] for ref in (small_ref, small_other_ref) for r in range(SLOTS // B)],
        axis=1,
    )
    top = coef.astype(BF).astype(F32)
    middle = (coef - top).astype(BF).astype(F32)
    at = at_ref[...]
    top, middle, low = by_place(at >> 7, at & 127, [top, middle, coef - top - middle], PLACES // 128)
    coef = top + middle + low
    cols = jnp.transpose(jnp.concatenate([coef, jnp.zeros((128 - coef.shape[0], 128), F32)], axis=0))
    for m in range(PLACES // 128):
        block = slice(m * 128, (m + 1) * 128)
        scaled_ref[block, :] = (rows_ref[block, :].astype(F32) * cols[:, m : m + 1]).astype(BF)
    own, other = small_ref[:CSLOTS, :], small_other_ref[:CSLOTS, :]
    first = start_ref[31] == 0
    neg_ref[...] = jnp.concatenate([jnp.where(first, own, other), jnp.where(first, other, own)], axis=1)

    def part(base, j):
        block = pl.ds(pl.multiple_of(j * B, B), B)
        key = jnp.concatenate([key_ref[pl.ds(2 * j, 1), :], key_ref[pl.ds(2 * j + 1, 1), :]], axis=1)
        return dot(onehot(base, TILE, key), scaled_ref[block, :])

    copies = []
    for i in range(ITEMS_DEV // TILE):
        base = i * TILE
        tile = slice(base, base + TILE)
        first = jnp.minimum(start_ref[i] // B, PLACES // B - 1)
        total_ref[...] = part(base, first)

        @pl.loop(first + 1, (start_ref[i + 1] + B - 1) // B)
        def _(j):
            total_ref[...] += part(base, j)

        @pl.loop(neg_at_ref[32 + i], neg_at_ref[33 + i])
        def _(p):
            total_ref[pl.ds(neg_at_ref[16 + p] - base, 1), :] += neg_ref[pl.ds(neg_at_ref[p], 1), :]

        out_ref[tile, :] = total_ref[...].astype(BF)
        copies.append(pltpu.make_async_copy(out_ref.at[tile, :], out_hbm.at[tile, :], sems.at[i]))
        copies[-1].start()
    for copy in copies:
        copy.wait()


def swap(v):
    return lax.ppermute(v, "c", SWAP)


def chips_a2a(v):
    return lax.all_to_all(v, CHIPS, split_axis=0, concat_axis=0, tiled=True)


def per_device(events, lengths, target_ids, neg_ids, neg_counts, item_table, w_uvqk, w_out):
    width = 512
    core = lax.axis_index("c")
    chip = lax.axis_index(CHIPS)
    info = jnp.stack([core, lengths[0], chip]).astype(I32)
    ev = events[0]

    w_mine = jnp.concatenate([w_uvqk, w_out], axis=1)
    w_own = lax.all_to_all(
        jnp.broadcast_to(w_mine[None], (16,) + w_mine.shape), ("x", "z"), split_axis=0, concat_axis=0, tiled=True
    ).reshape(256, 2560)

    normed, ids, logc, target_slot, send_row, neg_table = call(
        prep_kernel,
        (
            jax.ShapeDtypeStruct((1024, width), BF),
            jax.ShapeDtypeStruct((SLOTS, 128), I32),
            jax.ShapeDtypeStruct((SLOTS, 128), F32),
            jax.ShapeDtypeStruct((3, 1024), I32),
            jax.ShapeDtypeStruct((2, NCHIPS, 128), F32),
            jax.ShapeDtypeStruct((32, 128), I32),
        ),
        [SMEM] + [VMEM] * 4,
        scratch=[pltpu.VMEM((1024, 1024), BF), pltpu.VMEM((2 * DEVS, 1024), BF), pltpu.VMEM((512, 512), BF)],
        vmem=16,
    )(info, ev, target_ids, neg_ids[None], neg_counts[None])

    neg_local = neg_table[:, 0]
    packed = jnp.where((neg_local >= 0)[:, None], item_table[jnp.maximum(neg_local, 0)], 0)
    packed_own = lax.dynamic_slice(packed, (0, core * B), (32, B))
    packed_other = lax.dynamic_slice(packed, (0, (1 - core) * B), (32, B))
    neg_block = call(
        neg_block_kernel, jax.ShapeDtypeStruct((NCHIPS, BLOCK, 128), BF), [VMEM] * 3, vmem=8
    )(packed_own, swap(packed_other), send_row)

    follow = jnp.concatenate([ev[1:], jnp.zeros((1, width), BF)], axis=0)
    w_own, normed, follow, neg_block = lax.optimization_barrier((w_own, normed, follow, neg_block))
    got_neg = chips_a2a(neg_block)
    w_other = swap(w_own)
    any_space = pl.BlockSpec(memory_space=pl.ANY)
    positive, hidden, send_rows = pl.pallas_call(
        layer_kernel,
        out_shape=(
            jax.ShapeDtypeStruct((1, 1024), F32),
            jax.ShapeDtypeStruct((1024, width), BF),
            jax.ShapeDtypeStruct((SLOTS, width), BF),
        ),
        in_specs=[SMEM, VMEM] + [any_space] * 5,
        out_specs=(VMEM, any_space, any_space),
        scratch_shapes=[
            pltpu.VMEM((512, 512), BF),
            pltpu.VMEM((512, 2560), BF),
            pltpu.VMEM((1024, width), BF),
            pltpu.VMEM((1024, width), BF),
            pltpu.VMEM((1024, width), BF),
            pltpu.VMEM((1024, 2048), BF),
            pltpu.VMEM((B, width), F32),
            pltpu.VMEM((1024, width), BF),
            pltpu.VMEM((SLOTS, width), BF),
            pltpu.SemaphoreType.DMA((4, 4)),
            pltpu.SemaphoreType.DMA((10,)),
        ],
        cost_estimate=pl.CostEstimate(flops=0, bytes_accessed=0, transcendentals=0),
        compiler_params=pltpu.CompilerParams(vmem_limit_bytes=52 << 20),
    )(info, target_slot, w_own, normed, w_other, ev, follow)
    got_neg, send_rows = lax.optimization_barrier((got_neg, send_rows))
    other_neg = swap(got_neg)

    neg_own, neg_other, row_table = call(
        unpack_kernel,
        (
            jax.ShapeDtypeStruct((SLOTS, B), BF),
            jax.ShapeDtypeStruct((SLOTS, B), BF),
            jax.ShapeDtypeStruct((2, NCHIPS, 128), I32),
        ),
        [VMEM] * 2,
        vmem=16,
    )(got_neg, other_neg)

    recv_rows = chips_a2a(send_rows.reshape(NCHIPS, CSLOTS, width)).reshape(SLOTS, width)

    loss, term_own, term_other, meta = call(
        loss_kernel,
        (
            jax.ShapeDtypeStruct((1, 1024), F32),
            jax.ShapeDtypeStruct((SLOTS, B), F32),
            jax.ShapeDtypeStruct((SLOTS, B), BF),
            jax.ShapeDtypeStruct((3, NCHIPS, 128), F32),
        ),
        [SMEM] + [VMEM] * 8,
        scratch=[
            pltpu.VMEM((SLOTS, B), F32),
            pltpu.VMEM((SLOTS, 1024), BF),
            pltpu.VMEM((1, 1024), F32),
        ],
        flops=0,
        nbytes=0,
        vmem=28,
    )(
        info, hidden, neg_own, neg_other, ids, logc, positive, target_ids, target_slot,
    )
    block = call(
        term_block_kernel, jax.ShapeDtypeStruct((NCHIPS, BLOCK, 128), BF), [VMEM] * 3, vmem=16
    )(term_own, swap(term_other), meta)
    recv_rows, block = lax.optimization_barrier((recv_rows, block))
    got = chips_a2a(block)

    recv_other = swap(recv_rows)
    at, sorted_key, starts, neg_at = pl.pallas_call(
        rank_kernel,
        out_shape=(
            jax.ShapeDtypeStruct((1, 2 * SLOTS), I32),
            jax.ShapeDtypeStruct((PLACES // 128, 128), I32),
            jax.ShapeDtypeStruct((32,), I32),
            jax.ShapeDtypeStruct((64,), I32),
        ),
        in_specs=[SMEM, VMEM, VMEM],
        out_specs=(VMEM, VMEM, SMEM, SMEM),
        cost_estimate=pl.CostEstimate(flops=0, bytes_accessed=0, transcendentals=0),
        compiler_params=pltpu.CompilerParams(vmem_limit_bytes=16 << 20),
    )(info, row_table[:, :, :CSLOTS].reshape(1, 2 * SLOTS), neg_table)
    rows = call(sort_kernel, jax.ShapeDtypeStruct((PLACES, width), BF), [VMEM] * 3, vmem=24)(
        at, recv_rows, recv_other
    )

    got, rows = lax.optimization_barrier((got, rows))
    small = call(collect_kernel, jax.ShapeDtypeStruct((32, B), F32), [VMEM], vmem=8)(got)
    small_other = swap(small)
    tiles = ITEMS_DEV // TILE
    grad = pl.pallas_call(
        place_kernel,
        out_shape=jax.ShapeDtypeStruct((ITEMS_DEV, width), BF),
        in_specs=[SMEM] * 2 + [VMEM] * 5,
        out_specs=pl.BlockSpec(memory_space=pl.ANY),
        scratch_shapes=[
            pltpu.VMEM((PLACES, width), BF),
            pltpu.VMEM((CSLOTS, width), F32),
            pltpu.VMEM((TILE, width), F32),
            pltpu.VMEM((ITEMS_DEV, width), BF),
            pltpu.SemaphoreType.DMA((tiles,)),
        ],
        cost_estimate=pl.CostEstimate(flops=0, bytes_accessed=0, transcendentals=0),
        compiler_params=pltpu.CompilerParams(vmem_limit_bytes=24 << 20),
    )(starts, neg_at, small, small_other, at, sorted_key, rows)
    return loss, grad


def solution(mesh):
    fine = Mesh(mesh.devices.reshape(4, 4, 4, 2), ALL)
    in_specs = (P(ALL), P(ALL), P(ALL), P(), P(), P(ALL), P(MP), P(MP))
    return jax.shard_map(
        per_device, mesh=fine, in_specs=in_specs, out_specs=(P(ALL), P(ALL)), check_vma=False
    )
```

```python
import math

import jax
import jax.numpy as jnp
from jax import lax
from jax.experimental import pallas as pl
from jax.experimental.pallas import tpu as pltpu
from jax.sharding import Mesh, PartitionSpec as P

H = 4
EPSILON = 1e-05
ALL = ("y", "x", "z", "c")
CHIPS = ("y", "x", "z")
MP = ("x", "z", "c")
BF = jnp.bfloat16
F32 = jnp.float32
I32 = jnp.int32
DEVS = 128
NCHIPS = 64
CSLOTS = 24
SLOTS = NCHIPS * CSLOTS
BLOCK = 2 * CSLOTS + 8
PLACES = 2048
GROUP = 8
ITEMS_DEV = 4096
B = 256
TILE = 512
VMEM = pl.BlockSpec(memory_space=pltpu.VMEM)
SMEM = pl.BlockSpec(memory_space=pltpu.SMEM)
NT = (((1,), (1,)), ((), ()))
NEG_INF = float("-inf")
POS_INF = float("inf")
SWAP = ((0, 1), (1, 0))


def dot(a, b):
    return jnp.dot(a, b, preferred_element_type=F32)


def dot_nt(a, b):
    return lax.dot_general(a, b, NT, preferred_element_type=F32)


def iota(shape, dim):
    return lax.broadcasted_iota(I32, shape, dim)


def layer_norm(values):
    center = values - jnp.mean(values, axis=-1, keepdims=True)
    spread = jnp.mean(center * center, axis=-1, keepdims=True)
    return center * lax.rsqrt(spread + EPSILON)


def call(body, out_shape, in_specs, scratch=(), flops=0, nbytes=0, vmem=56):
    return pl.pallas_call(
        body,
        out_shape=out_shape,
        in_specs=in_specs,
        out_specs=jax.tree.map(lambda _: VMEM, out_shape),
        scratch_shapes=list(scratch),
        cost_estimate=pl.CostEstimate(flops=flops, bytes_accessed=nbytes, transcendentals=0),
        compiler_params=pltpu.CompilerParams(vmem_limit_bytes=vmem << 20),
    )


def onehot(base, count, index):
    return (iota((count, index.shape[1]), 0) + base == index).astype(F32).astype(BF)


def by_place(high, low, pieces, count):
    rows = iota((count, high.shape[1]), 0) == high
    stacked = jnp.concatenate([jnp.where(rows, p.astype(F32), 0.0) for p in pieces], axis=0).astype(BF)
    got = dot_nt(stacked, onehot(0, 128, low))
    return [got[k * count : (k + 1) * count] for k in range(len(pieces))]


def prep_kernel(
    info_ref, events_ref, targets_ref, negs_ref, counts_ref,
    normed_ref, ids_ref, logc_ref, slot_ref, row_ref, local_ref, tri_ref, owner_ref, order_ref,
):
    core, chip = info_ref[0], info_ref[2]
    targets, negs = targets_ref[...], negs_ref[...]
    n = targets.shape[1]

    for k in range(4):
        rows = slice(k * B, (k + 1) * B)
        tri_ref[rows, :] = (iota((B, n), 0) + k * B < iota((B, n), 1)).astype(F32).astype(BF)
    t_owner, n_owner = targets >> 12, negs >> 12
    owner_ref[:DEVS, :] = onehot(0, DEVS, t_owner)
    owner_ref[DEVS:, :] = onehot(0, DEVS, n_owner)
    before = dot(owner_ref[...], tri_ref[...]) * owner_ref[...].astype(F32)
    t_rank = jnp.sum(before[:DEVS], axis=0, keepdims=True).astype(I32)
    n_rank = jnp.sum(before[DEVS:], axis=0, keepdims=True).astype(I32)

    def within(owner, rank):
        return jnp.where(rank < 8, (owner & 1) * 8 + rank, 8 + rank)

    t_within = within(t_owner, t_rank)
    slot_ref[0:1, :] = (t_owner >> 1) * CSLOTS + t_within
    slot_ref[1:2, :] = t_owner >> 1
    slot_ref[2:3, :] = t_within
    n_slot = (n_owner >> 1) * CSLOTS + within(n_owner, n_rank)
    row = (targets & (2 * ITEMS_DEV - 1)) + 1
    row_ref[0], row_ref[1] = by_place(t_owner >> 1, t_within, [row >> 6, row & 63], NCHIPS)

    mine = (iota((32, n), 0) + chip * CSLOTS == n_slot) & ((n_owner & 1) == core)
    mine = mine & (iota((32, n), 0) < CSLOTS)
    local = jnp.max(jnp.where(mine, negs & (ITEMS_DEV - 1), -1), axis=1, keepdims=True)
    local_ref[...] = jnp.broadcast_to(local, (32, 128))
    logs = jnp.log(counts_ref[...].astype(F32))
    for m in range(SLOTS // B):
        rows = slice(m * B, (m + 1) * B)
        here = iota((B, n), 0) + m * B == n_slot
        ids = jnp.max(jnp.where(here, negs, -1), axis=1, keepdims=True)
        logc = jnp.min(jnp.where(here, logs, POS_INF), axis=1, keepdims=True)
        ids_ref[rows, :] = jnp.broadcast_to(ids, (B, 128))
        logc_ref[rows, :] = jnp.broadcast_to(logc, (B, 128))

    k = iota((512, 512), 1)
    source = ((k & 255) >> 4) * 32 + jnp.where(k < 256, core, 1 - core) * 16 + (k & 15)
    order_ref[...] = (iota((512, 512), 0) == source).astype(F32).astype(BF)

    @pl.loop(0, 4)
    def _(i):
        rows = pl.ds(pl.multiple_of(i * B, B), B)
        normed = layer_norm(events_ref[rows, :].astype(F32)).astype(BF)
        normed_ref[rows, :] = dot(normed, order_ref[...]).astype(BF)


def block_of(rows, pieces):
    chips = rows.shape[0]
    pieces = [p[:, None, :] for p in pieces] + [jnp.zeros((chips, 8 - len(pieces), 128), F32)]
    return jnp.concatenate([rows[:, :, :128], rows[:, :, 128:]] + pieces, axis=1).astype(BF)


def neg_block_kernel(mine_ref, other_ref, row_ref, out_ref):
    rows = mine_ref[...].astype(F32) + other_ref[...].astype(F32)
    rows = jnp.broadcast_to(rows[None, :CSLOTS], (GROUP, CSLOTS, B))
    for g in range(NCHIPS // GROUP):
        chips = slice(g * GROUP, (g + 1) * GROUP)
        out_ref[chips] = block_of(rows, [row_ref[0, chips, :], row_ref[1, chips, :]])


def term_block_kernel(own_ref, other_ref, meta_ref, out_ref):
    for g in range(NCHIPS // GROUP):
        chips = slice(g * GROUP, (g + 1) * GROUP)
        slots = slice(g * GROUP * CSLOTS, (g + 1) * GROUP * CSLOTS)
        rows = (own_ref[slots, :] + other_ref[slots, :].astype(F32)).reshape(GROUP, CSLOTS, B)
        out_ref[chips] = block_of(rows, [meta_ref[k, chips, :] for k in range(3)])


def unpack_kernel(own_ref, other_ref, own_out_ref, other_out_ref, row_ref):
    for k, (block_ref, out_ref) in enumerate(((own_ref, own_out_ref), (other_ref, other_out_ref))):
        for g in range(NCHIPS // GROUP):
            chips = slice(g * GROUP, (g + 1) * GROUP)
            block = block_ref[chips].astype(F32)
            halves = [
                block[:, h * CSLOTS : (h + 1) * CSLOTS].reshape(GROUP * CSLOTS, 128) for h in range(2)
            ]
            slots = slice(g * GROUP * CSLOTS, (g + 1) * GROUP * CSLOTS)
            out_ref[slots, :] = jnp.concatenate(halves, axis=1).astype(BF)
            numbers = block[:, 2 * CSLOTS :]
            row_ref[k, chips, :] = (numbers[:, 0] * 64.0 + numbers[:, 1]).astype(I32)


def silu_of_half(h):
    return h + h * jnp.tanh(h)


def layer_kernel(
    info_ref, slot_ref, own_hbm, normed_hbm, other_hbm, events_hbm, follow_hbm,
    positive_ref, hidden_hbm, send_hbm,
    w_ref, all_ref, normed_ref, events_ref, follow_ref, act_ref, att_ref, hidden_ref, send_ref, in_sem, out_sem,
):
    core, length = info_ref[0], info_ref[1]
    blocks = [slice(i * B, (i + 1) * B) for i in range(4)]

    def fetch(k, source, to):
        return [pltpu.make_async_copy(source.at[r, :], to.at[r, :], in_sem.at[k, i]) for i, r in enumerate(blocks)]

    w_in = [
        pltpu.make_async_copy(source, all_ref.at[pl.ds(k * B, B), :], in_sem.at[3, k])
        for k, source in enumerate((own_hbm, other_hbm))
    ]
    normed_in = fetch(0, normed_hbm, normed_ref)
    events_in = fetch(1, events_hbm, events_ref)
    follow_in = fetch(2, follow_hbm, follow_ref)
    for copy in normed_in[:1] + w_in + normed_in[1:] + [c for p in zip(events_in, follow_in) for c in p]:
        copy.start()
    for copy in w_in:
        copy.wait()

    @pl.loop(0, 4)
    def _(i):
        rows = pl.ds(pl.multiple_of(i * B, B), B)
        pltpu.make_async_copy(normed_hbm.at[rows, :], normed_ref.at[rows, :], in_sem.at[0, i]).wait()
        a = normed_ref[rows, :]
        live = iota((B, 512), 0) + i * B < length
        for n in range(4):
            cols = slice(n * 512, (n + 1) * 512)
            v = silu_of_half(0.5 * dot(a, all_ref[:, cols]))
            if n == 1:
                v = jnp.where(live, v, 0.0)
            act_ref[rows, cols] = v.astype(BF)

    for b in range(16):
        own, other = slice(b * 16, (b + 1) * 16), slice(B + b * 16, B + (b + 1) * 16)
        w_ref[pl.ds(pl.multiple_of(b * 32 + core * 16, 16), 16), :] = all_ref[own, 2048:]
        w_ref[pl.ds(pl.multiple_of(b * 32 + (1 - core) * 16, 16), 16), :] = all_ref[other, 2048:]

    causal = iota((B, B), 1) <= iota((B, B), 0)
    eye = iota((B, B), 1) == iota((B, B), 0)
    scale = 0.5 / math.sqrt(128)
    hidden_out = []
    for i, rows in enumerate(blocks):

        def scores(h, j):
            q = act_ref[rows, 1024 + h * 128 : 1024 + (h + 1) * 128]
            return dot_nt(q, act_ref[blocks[j], 1536 + h * 128 : 1536 + (h + 1) * 128])

        work = [(h, j) for h in range(H) for j in range(i + 1)]
        ahead = [scores(*work[0]), scores(*work[1])]
        for n, (h, j) in enumerate(work):
            s = ahead.pop(0)
            if n + 2 < len(work):
                ahead.append(scores(*work[n + 2]))
            w = silu_of_half(s * scale)
            if j == i:
                w = jnp.where(causal, w, 0.0)
            t = dot(w.astype(BF), act_ref[blocks[j], 512 + h * 128 : 512 + (h + 1) * 128])
            total = t if j == 0 else total + t
            if j == i:
                att_ref[:, h * 128 : (h + 1) * 128] = total
        gated = (layer_norm(att_ref[...]) * act_ref[rows, :512].astype(F32)).astype(BF)
        events_in[i].wait()
        follow_in[i].wait()
        hidden = (events_ref[rows, :].astype(F32) + dot(gated, w_ref[...])).astype(BF)
        hidden_ref[rows, :] = hidden
        hidden_out.append(pltpu.make_async_copy(hidden_ref.at[rows, :], hidden_hbm.at[rows, :], out_sem.at[6 + i]))
        hidden_out[-1].start()
        pos = jnp.sum(hidden.astype(F32) * follow_ref[rows, :].astype(F32), axis=1, keepdims=True)
        positive_ref[:, rows] = jnp.sum(jnp.where(eye, pos, 0.0), axis=0, keepdims=True)

    outs = []
    for m in range(SLOTS // B):
        rows = slice(m * B, (m + 1) * B)
        send_ref[rows, :] = dot(onehot(m * B, B, slot_ref[0:1, :]), hidden_ref[...]).astype(BF)
        outs.append(pltpu.make_async_copy(send_ref.at[rows, :], send_hbm.at[rows, :], out_sem.at[m]))
        outs[-1].start()
    for copy in hidden_out + outs:
        copy.wait()


def loss_kernel(
    info_ref, hidden_ref, own_ref, other_ref, ids_ref, logc_ref, positive_ref, targets_ref, slot_ref,
    loss_ref, term_own_ref, term_other_ref, meta_ref, l_ref, probs_ref, coef_ref,
):
    core, length = info_ref[0], info_ref[1]
    own_cols = pl.ds(pl.multiple_of(core * B, B), B)
    other_cols = pl.ds(pl.multiple_of((1 - core) * B, B), B)
    chunks = [slice(m * B, (m + 1) * B) for m in range(SLOTS // B)]

    @pl.loop(0, 4)
    def _(t):
        at = pl.ds(pl.multiple_of(t * B, B), B)
        h_own = hidden_ref[at, own_cols]
        h_other = hidden_ref[at, other_cols]
        pos = positive_ref[:, at]
        target = targets_ref[:, at]
        top = pos
        for m in chunks:
            logc, ids = logc_ref[m, :], ids_ref[m, :]
            value = dot_nt(own_ref[m, :], h_own) + dot_nt(other_ref[m, :], h_other)
            value = value - jnp.concatenate([logc, logc], axis=1)
            value = jnp.where(jnp.concatenate([ids, ids], axis=1) != target, value, NEG_INF)
            l_ref[m, :] = value
            top = jnp.maximum(top, jnp.max(value, axis=0, keepdims=True))
        total = jnp.exp(pos - top)
        for m in chunks:
            total = total + jnp.sum(jnp.exp(l_ref[m, :] - top), axis=0, keepdims=True)
        log_total = top + jnp.log(total)
        in_range = iota((1, B), 1) + t * B < length - 1
        loss_ref[:, at] = jnp.where(in_range, log_total - pos, 0.0)
        coef_ref[:, at] = jnp.where(in_range, jnp.exp(pos - log_total) - 1.0, 0.0)
        shift = jnp.where(in_range, log_total, POS_INF)
        for m in chunks:
            probs_ref[m, at] = jnp.exp(l_ref[m, :] - shift).astype(BF)

    coef = coef_ref[...]
    high = coef.astype(BF).astype(F32)
    middle = (coef - high).astype(BF).astype(F32)
    low = coef - high - middle
    pieces = by_place(slot_ref[1:2, :], slot_ref[2:3, :], [high, middle, low], NCHIPS)
    for k, piece in enumerate(pieces):
        meta_ref[k] = piece
    for m in chunks:
        term_other_ref[m, :] = dot(probs_ref[m, :], hidden_ref[:, other_cols]).astype(BF)
        term_own_ref[m, :] = dot(probs_ref[m, :], hidden_ref[:, own_cols])


def rank_kernel(info_ref, row_ref, neg_ref, at_ref, sorted_key_ref, start_ref, neg_at_ref):
    core = info_ref[0]
    row = row_ref[...] - 1 - core * ITEMS_DEV
    row = jnp.where((row >= 0) & (row < ITEMS_DEV), row, 2 * ITEMS_DEV - 1)
    n = row.shape[1]
    key = row * 4096 + iota((1, n), 1)
    eye = iota((128, 128), 1) == iota((128, 128), 0)
    at = jnp.zeros((1, n), F32)
    for m in range(n // 128):
        col = jnp.sum(jnp.where(eye, key[:, m * 128 : (m + 1) * 128], 0), axis=1, keepdims=True)
        at = at + jnp.sum((col < key).astype(F32), axis=0, keepdims=True)
    at = at.astype(I32)
    at_ref[...] = at
    for i in range(ITEMS_DEV // TILE + 1):
        start_ref[i] = jnp.sum((row < i * TILE).astype(I32))
    start_ref[31] = core
    neg = neg_ref[:, :1]
    neg = jnp.where(neg < 0, 2 * ITEMS_DEV, neg) * 64 + iota((32, 1), 0)
    small_eye = iota((32, 32), 1) == iota((32, 32), 0)
    neg_row = jnp.sum(jnp.where(small_eye, neg, 0), axis=0, keepdims=True)
    neg_rank = jnp.sum((neg < neg_row).astype(I32), axis=0, keepdims=True)
    for p in range(16):
        found = jnp.sum(jnp.where(neg_rank == p, neg_row, 0))
        neg_at_ref[p] = found & 63
        neg_at_ref[16 + p] = found >> 6
    for i in range(ITEMS_DEV // TILE + 1):
        neg_at_ref[32 + i] = jnp.sum(((neg_row >> 6) < i * TILE).astype(I32))
    key_high, key_low = by_place(at >> 7, at & 127, [row >> 6, row & 63], PLACES // 128)
    sorted_key_ref[...] = (key_high * 64.0 + key_low).astype(I32)


def sort_kernel(at_ref, own_ref, other_ref, sorted_ref):
    for m in range(PLACES // B):
        block = slice(m * B, (m + 1) * B)
        sorted_ref[block, :] = (
            dot(onehot(m * B, B, at_ref[:, :SLOTS]), own_ref[...])
            + dot(onehot(m * B, B, at_ref[:, SLOTS:]), other_ref[...])
        ).astype(BF)


def collect_kernel(got_ref, small_ref):
    total = jnp.zeros((2 * CSLOTS, 128), F32)
    parts = [[], [], []]
    for g in range(NCHIPS // GROUP):
        block = got_ref[g * GROUP : (g + 1) * GROUP].astype(F32)
        total = total + jnp.sum(block[:, : 2 * CSLOTS], axis=0)
        for p in range(3):
            parts[p].append(block[:, 2 * CSLOTS + p])
    small_ref[:CSLOTS, :] = jnp.concatenate([total[:CSLOTS], total[CSLOTS:]], axis=1)
    k = iota((1, SLOTS), 1)
    chip = ((k.astype(F32) + 0.5) * (1.0 / CSLOTS)).astype(I32)
    spread = (iota((128, SLOTS), 0) == k - chip * CSLOTS).astype(F32).astype(BF)
    mine = iota((NCHIPS, SLOTS), 0) == chip
    row = jnp.zeros((1, SLOTS), F32)
    for p in range(3):
        piece = jnp.concatenate(parts[p], axis=0).astype(BF)
        row = row + jnp.sum(jnp.where(mine, dot(piece, spread), 0.0), axis=0, keepdims=True)
    for r in range(SLOTS // B):
        small_ref[CSLOTS + r : CSLOTS + r + 1, :] = row[:, r * B : (r + 1) * B]
    small_ref[CSLOTS + SLOTS // B :, :] = jnp.zeros((8 - SLOTS // B, B), F32)


def place_kernel(
    start_ref, neg_at_ref, small_ref, small_other_ref, at_ref, key_ref, rows_ref, out_hbm,
    scaled_ref, neg_ref, total_ref, out_ref, sems,
):
    coef = jnp.concatenate(
        [ref[CSLOTS + r : CSLOTS + r + 1, :] for ref in (small_ref, small_other_ref) for r in range(SLOTS // B)],
        axis=1,
    )
    top = coef.astype(BF).astype(F32)
    middle = (coef - top).astype(BF).astype(F32)
    at = at_ref[...]
    top, middle, low = by_place(at >> 7, at & 127, [top, middle, coef - top - middle], PLACES // 128)
    coef = top + middle + low
    cols = jnp.transpose(jnp.concatenate([coef, jnp.zeros((128 - coef.shape[0], 128), F32)], axis=0))
    for m in range(PLACES // 128):
        block = slice(m * 128, (m + 1) * 128)
        scaled_ref[block, :] = (rows_ref[block, :].astype(F32) * cols[:, m : m + 1]).astype(BF)
    own, other = small_ref[:CSLOTS, :], small_other_ref[:CSLOTS, :]
    first = start_ref[31] == 0
    neg_ref[...] = jnp.concatenate([jnp.where(first, own, other), jnp.where(first, other, own)], axis=1)

    def part(base, j):
        block = pl.ds(pl.multiple_of(j * B, B), B)
        key = jnp.concatenate([key_ref[pl.ds(2 * j, 1), :], key_ref[pl.ds(2 * j + 1, 1), :]], axis=1)
        return dot(onehot(base, TILE, key), scaled_ref[block, :])

    copies = []
    for i in range(ITEMS_DEV // TILE):
        base = i * TILE
        tile = slice(base, base + TILE)
        first = jnp.minimum(start_ref[i] // B, PLACES // B - 1)
        total_ref[...] = part(base, first)

        @pl.loop(first + 1, (start_ref[i + 1] + B - 1) // B)
        def _(j):
            total_ref[...] += part(base, j)

        @pl.loop(neg_at_ref[32 + i], neg_at_ref[33 + i])
        def _(p):
            total_ref[pl.ds(neg_at_ref[16 + p] - base, 1), :] += neg_ref[pl.ds(neg_at_ref[p], 1), :]

        out_ref[tile, :] = total_ref[...].astype(BF)
        copies.append(pltpu.make_async_copy(out_ref.at[tile, :], out_hbm.at[tile, :], sems.at[i]))
        copies[-1].start()
    for copy in copies:
        copy.wait()


def swap(v):
    return lax.ppermute(v, "c", SWAP)


def chips_a2a(v):
    return lax.all_to_all(v, CHIPS, split_axis=0, concat_axis=0, tiled=True)


def per_device(events, lengths, target_ids, neg_ids, neg_counts, item_table, w_uvqk, w_out):
    width = 512
    core = lax.axis_index("c")
    chip = lax.axis_index(CHIPS)
    info = jnp.stack([core, lengths[0], chip]).astype(I32)
    ev = events[0]

    w_mine = jnp.concatenate([w_uvqk, w_out], axis=1)
    w_own = lax.all_to_all(
        jnp.broadcast_to(w_mine[None], (16,) + w_mine.shape), ("x", "z"), split_axis=0, concat_axis=0, tiled=True
    ).reshape(256, 2560)

    normed, ids, logc, target_slot, send_row, neg_table = call(
        prep_kernel,
        (
            jax.ShapeDtypeStruct((1024, width), BF),
            jax.ShapeDtypeStruct((SLOTS, 128), I32),
            jax.ShapeDtypeStruct((SLOTS, 128), F32),
            jax.ShapeDtypeStruct((3, 1024), I32),
            jax.ShapeDtypeStruct((2, NCHIPS, 128), F32),
            jax.ShapeDtypeStruct((32, 128), I32),
        ),
        [SMEM] + [VMEM] * 4,
        scratch=[pltpu.VMEM((1024, 1024), BF), pltpu.VMEM((2 * DEVS, 1024), BF), pltpu.VMEM((512, 512), BF)],
        vmem=16,
    )(info, ev, target_ids, neg_ids[None], neg_counts[None])

    neg_local = neg_table[:, 0]
    packed = jnp.where((neg_local >= 0)[:, None], item_table[jnp.maximum(neg_local, 0)], 0)
    packed_own = lax.dynamic_slice(packed, (0, core * B), (32, B))
    packed_other = lax.dynamic_slice(packed, (0, (1 - core) * B), (32, B))
    neg_block = call(
        neg_block_kernel, jax.ShapeDtypeStruct((NCHIPS, BLOCK, 128), BF), [VMEM] * 3, vmem=8
    )(packed_own, swap(packed_other), send_row)

    follow = jnp.concatenate([ev[1:], jnp.zeros((1, width), BF)], axis=0)
    w_own, normed, follow, neg_block = lax.optimization_barrier((w_own, normed, follow, neg_block))
    got_neg = chips_a2a(neg_block)
    w_other = swap(w_own)
    any_space = pl.BlockSpec(memory_space=pl.ANY)
    positive, hidden, send_rows = pl.pallas_call(
        layer_kernel,
        out_shape=(
            jax.ShapeDtypeStruct((1, 1024), F32),
            jax.ShapeDtypeStruct((1024, width), BF),
            jax.ShapeDtypeStruct((SLOTS, width), BF),
        ),
        in_specs=[SMEM, VMEM] + [any_space] * 5,
        out_specs=(VMEM, any_space, any_space),
        scratch_shapes=[
            pltpu.VMEM((512, 512), BF),
            pltpu.VMEM((512, 2560), BF),
            pltpu.VMEM((1024, width), BF),
            pltpu.VMEM((1024, width), BF),
            pltpu.VMEM((1024, width), BF),
            pltpu.VMEM((1024, 2048), BF),
            pltpu.VMEM((B, width), F32),
            pltpu.VMEM((1024, width), BF),
            pltpu.VMEM((SLOTS, width), BF),
            pltpu.SemaphoreType.DMA((4, 4)),
            pltpu.SemaphoreType.DMA((10,)),
        ],
        cost_estimate=pl.CostEstimate(flops=0, bytes_accessed=0, transcendentals=0),
        compiler_params=pltpu.CompilerParams(vmem_limit_bytes=48 << 20),
    )(info, target_slot, w_own, normed, w_other, ev, follow)
    got_neg, send_rows = lax.optimization_barrier((got_neg, send_rows))
    other_neg = swap(got_neg)

    neg_own, neg_other, row_table = call(
        unpack_kernel,
        (
            jax.ShapeDtypeStruct((SLOTS, B), BF),
            jax.ShapeDtypeStruct((SLOTS, B), BF),
            jax.ShapeDtypeStruct((2, NCHIPS, 128), I32),
        ),
        [VMEM] * 2,
        vmem=16,
    )(got_neg, other_neg)

    recv_rows = chips_a2a(send_rows.reshape(NCHIPS, CSLOTS, width)).reshape(SLOTS, width)

    loss, term_own, term_other, meta = call(
        loss_kernel,
        (
            jax.ShapeDtypeStruct((1, 1024), F32),
            jax.ShapeDtypeStruct((SLOTS, B), F32),
            jax.ShapeDtypeStruct((SLOTS, B), BF),
            jax.ShapeDtypeStruct((3, NCHIPS, 128), F32),
        ),
        [SMEM] + [VMEM] * 8,
        scratch=[
            pltpu.VMEM((SLOTS, B), F32),
            pltpu.VMEM((SLOTS, 1024), BF),
            pltpu.VMEM((1, 1024), F32),
        ],
        flops=0,
        nbytes=0,
        vmem=28,
    )(
        info, hidden, neg_own, neg_other, ids, logc, positive, target_ids, target_slot,
    )
    block = call(
        term_block_kernel, jax.ShapeDtypeStruct((NCHIPS, BLOCK, 128), BF), [VMEM] * 3, vmem=16
    )(term_own, swap(term_other), meta)

    at, sorted_key, starts, neg_at = pl.pallas_call(
        rank_kernel,
        out_shape=(
            jax.ShapeDtypeStruct((1, 2 * SLOTS), I32),
            jax.ShapeDtypeStruct((PLACES // 128, 128), I32),
            jax.ShapeDtypeStruct((32,), I32),
            jax.ShapeDtypeStruct((64,), I32),
        ),
        in_specs=[SMEM, VMEM, VMEM],
        out_specs=(VMEM, VMEM, SMEM, SMEM),
        cost_estimate=pl.CostEstimate(flops=0, bytes_accessed=0, transcendentals=0),
        compiler_params=pltpu.CompilerParams(vmem_limit_bytes=16 << 20),
    )(info, row_table[:, :, :CSLOTS].reshape(1, 2 * SLOTS), neg_table)
    recv_rows, block, at = lax.optimization_barrier((recv_rows, block, at))
    got = chips_a2a(block)
    recv_other = swap(recv_rows)
    rows = call(sort_kernel, jax.ShapeDtypeStruct((PLACES, width), BF), [VMEM] * 3, vmem=24)(
        at, recv_rows, recv_other
    )

    got, rows = lax.optimization_barrier((got, rows))
    small = call(collect_kernel, jax.ShapeDtypeStruct((32, B), F32), [VMEM], vmem=8)(got)
    small_other = swap(small)
    tiles = ITEMS_DEV // TILE
    grad = pl.pallas_call(
        place_kernel,
        out_shape=jax.ShapeDtypeStruct((ITEMS_DEV, width), BF),
        in_specs=[SMEM] * 2 + [VMEM] * 5,
        out_specs=pl.BlockSpec(memory_space=pl.ANY),
        scratch_shapes=[
            pltpu.VMEM((PLACES, width), BF),
            pltpu.VMEM((CSLOTS, width), F32),
            pltpu.VMEM((TILE, width), F32),
            pltpu.VMEM((ITEMS_DEV, width), BF),
            pltpu.SemaphoreType.DMA((tiles,)),
        ],
        cost_estimate=pl.CostEstimate(flops=0, bytes_accessed=0, transcendentals=0),
        compiler_params=pltpu.CompilerParams(vmem_limit_bytes=24 << 20),
    )(starts, neg_at, small, small_other, at, sorted_key, rows)
    return loss, grad


def solution(mesh):
    fine = Mesh(mesh.devices.reshape(4, 4, 4, 2), ALL)
    in_specs = (P(ALL), P(ALL), P(ALL), P(), P(), P(ALL), P(MP), P(MP))
    return jax.shard_map(
        per_device, mesh=fine, in_specs=in_specs, out_specs=(P(ALL), P(ALL)), check_vma=False
    )
```
